32 devices in a mesh: section: 2 (over core), dp: 4 (over z), replica: 4 (over y, x).
Axes of the slice: x: 2, y: 2, z: 4, core: 2. Of those that a mesh axis runs over, the one named last changes fastest.
Arguments:
- tokens: bfloat16 [16384, 768], P(('dp', 'replica')), may hold values from -6 to 6
- cotangent: bfloat16 [16384, 768], P(('dp', 'replica')), may hold values from -6 to 6
- lengths: int32 [32], P(('dp', 'replica')), may hold values from 100 to 512, as said below
- attn_gain: bfloat16 [2, 768], P('section'), may hold values from 0.25 to 1.75
- attn_shift: bfloat16 [2, 768], P('section'), may hold values from -1.5 to 1.5
- qkv_weight: bfloat16 [2, 768, 2304], P('section'), may hold values from -0.3125 to 0.3125
- qkv_bias: bfloat16 [2, 2304], P('section'), may hold values from -1.5 to 1.5
- out_weight: bfloat16 [2, 768, 768], P('section'), may hold values from -0.625 to 0.625
- out_bias: bfloat16 [2, 768], P('section'), may hold values from -1.5 to 1.5
- mlp_gain: bfloat16 [2, 768], P('section'), may hold values from 0.25 to 1.75
- mlp_shift: bfloat16 [2, 768], P('section'), may hold values from -1.5 to 1.5
- up_weight: bfloat16 [2, 768, 3072], P('section'), may hold values from -0.21875 to 0.21875
- up_bias: bfloat16 [2, 3072], P('section'), may hold values from -2.5 to 2.5
- down_weight: bfloat16 [2, 3072, 768], P('section'), may hold values from -0.109375 to 0.109375
- down_bias: bfloat16 [2, 768], P('section'), may hold values from -1.5 to 1.5
Outputs:
- block_outputs: bfloat16 [2, 16384, 768], P('section', ('dp', 'replica'))
- input_grads: float32 [2, 16384, 768], P('section', ('dp', 'replica'))
- grad_attn_gain: float32 [2, 768], P('section', 'dp')
- grad_attn_shift: float32 [2, 768], P('section', 'dp')
- grad_qkv_weight: float32 [2, 768, 2304], P('section', 'dp')
- grad_qkv_bias: float32 [2, 2304], P('section', 'dp')
- grad_out_weight: float32 [2, 768, 768], P('section', 'dp')
- grad_out_bias: float32 [2, 768], P('section', 'dp')
- grad_mlp_gain: float32 [2, 768], P('section', 'dp')
- grad_mlp_shift: float32 [2, 768], P('section', 'dp')
- grad_up_weight: float32 [2, 768, 3072], P('section', 'dp')
- grad_up_bias: float32 [2, 3072], P('section', 'dp')
- grad_down_weight: float32 [2, 3072, 768], P('section', 'dp')
- grad_down_bias: float32 [2, 768], P('section', 'dp')
The draws below stay inside these ranges and needn't reach their ends.
Inputs may be any that keep to these rules, and one draw needn't show every extreme that they name: `lengths`: some sentence has exactly 512 genes and another exactly 100.
All inputs are finite; a program needn't handle non-finite values.
Results may differ from the reference program's by a relative error of at most 0.03.
The reference program's roundings to bfloat16 on the way count: a program that leaves them out, or rounds other values in their place, can miss the bound.
Values may be sent and summed in bfloat16 or wider, within the bound.
A program may use at most 256 MiB of HBM per device.

```python
import jax
import jax.numpy as jnp
from jax import lax

D = 768
HEADS = 12
HEAD_DIM = 64
ROTARY = 16
FF = 3072
SEQ = 512
LEN_MIN = 100
SEQS = 32
TOKENS = 16384
N_SECTION = 2


def draw_lengths(key, part):
    key = jax.random.fold_in(key, 7)
    base_key, long_key, short_key = jax.random.split(key, 3)
    drawn_len = jax.random.randint(base_key, (SEQS,), LEN_MIN, SEQ + 1)
    longest_at = jax.random.randint(long_key, (), 0, SEQS)
    shortest_at = (longest_at + 1 + jax.random.randint(short_key, (), 0, SEQS - 1)) % SEQS
    positions = jnp.arange(SEQS)
    drawn_len = jnp.where(positions == longest_at, SEQ, drawn_len)
    drawn_len = jnp.where(positions == shortest_at, LEN_MIN, drawn_len)
    return drawn_len.astype(jnp.int32)


def block_scale(key, dims, cuts, low, largest):
    gain = 1.0
    for dim, shards_of in cuts:
        draws = jax.random.uniform(jax.random.fold_in(jax.random.fold_in(key, 6), dim), (shards_of,), jnp.float32, low / len(cuts), largest / len(cuts))
        gain = gain * jnp.repeat(jnp.exp(draws), dims[dim] // shards_of).reshape((-1,) + (1,) * (len(dims) - 1 - dim))
    return gain


def scatter_about(own_key, extent, scale, limit, cuts=(), kind=jnp.bfloat16):
    values = jax.random.normal(own_key, extent, jnp.float32) * scale
    if len(cuts) > 0:
        values = block_scale(own_key, extent, cuts, -0.22, 0.18) * values
    return jnp.clip(values, min=-limit, max=limit).astype(kind)


def setup_inputs(seed: int = 0) -> dict:
    keys = jax.random.split(jax.random.key(seed), 16)
    return {
        "tokens": scatter_about(keys[0], (TOKENS, D), 1.0, 6.0, ((0, 16),)),
        "cotangent": scatter_about(keys[1], (TOKENS, D), 1.0, 6.0, ((0, 16),)),
        "lengths": draw_lengths(jax.random.fold_in(keys[15], 71), 0),
        "attn_gain": jnp.clip(1.0 + 0.15 * jax.random.normal(keys[3], (N_SECTION, D), jnp.float32), 0.25, 1.75).astype(jnp.bfloat16),
        "attn_shift": scatter_about(keys[4], (N_SECTION, D), 0.3, 1.5, ((0, 2),)),
        "qkv_weight": scatter_about(keys[5], (N_SECTION, D, 3 * D), (D // 2) ** -0.5, 0.3125, ((0, 2),)),
        "qkv_bias": scatter_about(keys[6], (N_SECTION, 3 * D), 0.3, 1.5, ((0, 2),)),
        "out_weight": scatter_about(keys[7], (N_SECTION, D, D), (D // 8) ** -0.5, 0.625, ((0, 2),)),
        "out_bias": scatter_about(keys[8], (N_SECTION, D), 0.3, 1.5, ((0, 2),)),
        "mlp_gain": jnp.clip(1.0 + 0.15 * jax.random.normal(keys[9], (N_SECTION, D), jnp.float32), 0.25, 1.75).astype(jnp.bfloat16),
        "mlp_shift": scatter_about(keys[10], (N_SECTION, D), 0.3, 1.5, ((0, 2),)),
        "up_weight": scatter_about(keys[11], (N_SECTION, D, FF), D ** -0.5, 0.21875, ((0, 2),)),
        "up_bias": scatter_about(keys[12], (N_SECTION, FF), 0.5, 2.5, ((0, 2),)),
        "down_weight": scatter_about(keys[13], (N_SECTION, FF, D), FF ** -0.5, 0.109375, ((0, 2),)),
        "down_bias": scatter_about(keys[14], (N_SECTION, D), 0.3, 1.5, ((0, 2),)),
    }


EPSILON = 1e-05
ROTARY_BASE = 10000.0
MASKED = -1e+30
HIGHEST = lax.Precision.HIGHEST

@jax.custom_vjp
def low(v):
    return lax.optimization_barrier(v.astype(jnp.bfloat16)).astype(jnp.float32)

@jax.custom_vjp
def low_back(v):
    return v

def low_keep(v):
    return (low(v), None)

def low_pass(kept, grad):
    return (grad,)

def back_keep(v):
    return (v, None)

def back_low(kept, grad):
    return (low(grad),)
low.defvjp(low_keep, low_pass)
low_back.defvjp(back_keep, back_low)

def product(left, right):
    return jnp.dot(left, right, precision=HIGHEST, preferred_element_type=jnp.float32)

def layer_norm(values, norm_gain, norm_shift):
    centre = lax.optimization_barrier(jnp.mean(values, axis=-1, keepdims=True))
    centred = values - centre
    spread = lax.optimization_barrier(jnp.mean(centred * centred, axis=-1, keepdims=True))
    return centred * lax.rsqrt(spread + EPSILON) * norm_gain + norm_shift

def rotary_tables(seq_len):
    positions = jnp.arange(seq_len, dtype=jnp.float32)
    inverse = 1.0 / ROTARY_BASE ** (jnp.arange(0, ROTARY, 2, dtype=jnp.float32) / ROTARY)
    angles = positions[:, None] * inverse[None, :]
    angles = jnp.concatenate([angles, angles], axis=-1)
    return (jnp.cos(angles), jnp.sin(angles))

def rotate(per_head, cosine_tab, sine_tab):
    half_rot = ROTARY // 2
    turning = per_head[..., :ROTARY]
    swapped = jnp.concatenate([-turning[..., half_rot:], turning[..., :half_rot]], axis=-1)
    turned = turning * cosine_tab[:, None, :] + swapped * sine_tab[:, None, :]
    return jnp.concatenate([turned, per_head[..., ROTARY:]], axis=-1)

def layer_forward(block_in, length, weights):
    attn_gain, attn_shift, qkv_weight, qkv_bias, out_weight, out_bias, mlp_gain, mlp_shift, up_weight, up_bias, down_weight, down_bias = weights
    seq_len = block_in.shape[0]
    attn_in = low(layer_norm(block_in, attn_gain, attn_shift))
    projected = low_back(product(attn_in, qkv_weight) + qkv_bias)
    projected = projected.reshape(seq_len, 3, HEADS, HEAD_DIM)
    cosine_tab, sine_tab = rotary_tables(seq_len)
    queries = low(rotate(projected[:, 0], cosine_tab, sine_tab))
    keys_rot = low(rotate(projected[:, 1], cosine_tab, sine_tab))
    values_in = low(projected[:, 2])
    raw_scores = jnp.einsum('qhd,khd->hqk', queries, keys_rot, precision=HIGHEST) * HEAD_DIM ** (-0.5)
    row_ids = jnp.arange(seq_len)[:, None]
    col_ids = jnp.arange(seq_len)[None, :]
    allowed = (col_ids <= row_ids) & (col_ids < length)
    scores = low_back(jnp.where(allowed[None], raw_scores, MASKED))
    probs_low = low(jax.nn.softmax(scores, axis=-1))
    context = jnp.einsum('hqk,khd->qhd', probs_low, values_in, precision=HIGHEST)
    context = low(low_back(context.reshape(seq_len, D)))
    attn_out = low_back(product(context, out_weight) + out_bias)
    mlp_in = low(layer_norm(block_in, mlp_gain, mlp_shift))
    up_pre = low_back(product(mlp_in, up_weight) + up_bias)
    hidden = low(jax.nn.gelu(up_pre, approximate=False))
    mlp_out = low_back(product(hidden, down_weight) + down_bias)
    return block_in + attn_out + mlp_out

def reference(tokens, cotangent, lengths, attn_gain, attn_shift, qkv_weight, qkv_bias, out_weight, out_bias, mlp_gain, mlp_shift, up_weight, up_bias, down_weight, down_bias):
    params = tuple((weight_arr.astype(jnp.float32) for weight_arr in (attn_gain, attn_shift, qkv_weight, qkv_bias, out_weight, out_bias, mlp_gain, mlp_shift, up_weight, up_bias, down_weight, down_bias)))
    first_layer = tuple((weight_arr[0] for weight_arr in params))
    second_layer = tuple((weight_arr[1] for weight_arr in params))
    inputs = tokens.astype(jnp.float32).reshape(SEQS, SEQ, D)
    cotans = cotangent.astype(jnp.float32).reshape(SEQS, SEQ, D)

    def one_sequence(carried, entry_data):
        block_in, cot_rows, length = entry_data
        first_out, first_back = jax.vjp(lambda rows_in, layer_w: layer_forward(rows_in, length, layer_w), block_in, first_layer)
        middle = low(first_out)
        second_out, second_back = jax.vjp(lambda rows_in, layer_w: layer_forward(rows_in, length, layer_w), middle, second_layer)
        valid_rows = (jnp.arange(SEQ) < length)[:, None]
        out_grad = jnp.where(valid_rows, cot_rows, 0.0)
        middle_grad, second_grads = second_back(out_grad)
        middle_grad = low(middle_grad)
        input_grad, first_grads = first_back(middle_grad)
        carried = (jax.tree.map(jnp.add, carried[0], first_grads), jax.tree.map(jnp.add, carried[1], second_grads))
        return (carried, (middle.astype(jnp.bfloat16), second_out.astype(jnp.bfloat16), input_grad, middle_grad))
    zeros_init = (jax.tree.map(jnp.zeros_like, first_layer), jax.tree.map(jnp.zeros_like, second_layer))
    carried, stacked = lax.scan(one_sequence, zeros_init, (inputs, cotans, lengths))
    firsts, seconds, input_grad, middle_grad = stacked
    block_outputs = jnp.stack([firsts.reshape(TOKENS, D), seconds.reshape(TOKENS, D)])
    input_grads = jnp.stack([input_grad.reshape(TOKENS, D), middle_grad.reshape(TOKENS, D)])
    grad_scale = TOKENS ** (-0.5)
    summed = tuple((jnp.stack([first_sum, second_sum]) * grad_scale for first_sum, second_sum in zip(carried[0], carried[1])))
    return (block_outputs, input_grads, summed[0], summed[1], summed[2], summed[3], summed[4], summed[5], summed[6], summed[7], summed[8], summed[9], summed[10], summed[11])
```

```python
import functools

import jax
import jax.numpy as jnp
from jax import lax
from jax.experimental import pallas as pl
from jax.experimental.pallas import tpu as pltpu
from jax.sharding import PartitionSpec as P

HEADS = 12
HEAD_DIM = 64
ROTARY = 16
HALF = ROTARY // 2
EPSILON = 1e-05
ROTARY_BASE = 10000.0
MASKED = -1e30
SCALE = HEAD_DIM**-0.5
F32 = jnp.float32
BF16 = jnp.bfloat16
ANY = pl.BlockSpec(memory_space=pl.ANY)
VMEM = pl.BlockSpec(memory_space=pltpu.VMEM)
SMEM = pl.BlockSpec(memory_space=pltpu.SMEM)
ROW_CHUNK = 128
QKV_TILE = 256
FF_TILE = 512


def dims_dot(left, right, left_dim, right_dim):
    return lax.dot_general(
        left, right, (((left_dim,), (right_dim,)), ((), ())), preferred_element_type=F32
    )


def normal_parts(v):
    t = 1.0 / (1.0 + (0.3275911 * 0.7071067811865476) * jnp.abs(v))
    bell = jnp.exp(-0.5 * v * v)
    series = 0.7107068705 + t * (-0.7265760135 + t * 0.5307027145)
    tail = t * (0.127414796 + t * (-0.142248368 + t * series)) * bell
    return jnp.where(v >= 0, 1.0 - tail, tail), bell * 0.3989422804014327


class Copies:
    def __init__(self, sems):
        self.sems, self.copies = sems, []

    def start(self, src, dst):
        copy = pltpu.make_async_copy(src, dst, self.sems.at[len(self.copies)])
        copy.start()
        self.copies.append(copy)
        return copy

    def wait(self):
        for copy in self.copies:
            copy.wait()


def forward_kernel(moment, micros, n_alias, *refs):
    (
        lengths, tokens_h, received_h, attn_gain, attn_shift, qkv_bias, out_bias, mlp_gain, mlp_shift,
        up_bias, down_bias, cosine, sine, qkv_h, out_h, up_h, down_h,
    ) = refs[:17]
    (
        y_send_h, y_h, attn_in_h, mlp_in_h, queries_h, keys_h, values_h, probs_h, context_h, hidden_h, slope_h,
        qkv_w, out_w, up_w, down_w, x, attn_in, mlp_in, attn_in_t, mlp_in_t, heads_t, context_t, hidden_t, slope,
        bias, total, probs, y, in_sems, out_sems, probs_sems,
    ) = refs[17 + n_alias :]
    section = lax.axis_index("section")
    micro = moment - section
    rows, width = x.shape
    hidden_width = up_w.shape[1]
    half = rows // 2

    @pl.when((micro >= 0) & (micro < micros))
    def _():
        loads = [
            pltpu.make_async_copy(src, dst, in_sems.at[i])
            for i, (src, dst) in enumerate(((qkv_h, qkv_w), (out_h, out_w), (up_h, up_w), (down_h, down_w)))
        ]
        own = pltpu.make_async_copy(tokens_h.at[micro], x, in_sems.at[4])
        passed = pltpu.make_async_copy(received_h, x, in_sems.at[4])

        @pl.when(section == 0)
        def _():
            own.start()

        @pl.when(section != 0)
        def _():
            passed.start()

        loads[0].start()
        stores = Copies(out_sems)
        length = lengths[micro]
        key_ids = lax.broadcasted_iota(jnp.int32, (rows, rows), 0)
        query_ids = lax.broadcasted_iota(jnp.int32, (rows, rows), 1)
        bias[...] = jnp.where((key_ids <= query_ids) & (key_ids < length), 0.0, MASKED)
        probs[:, half:, :half] = jnp.zeros((probs.shape[0], half, half), BF16)
        own.wait()

        for start in range(0, rows, ROW_CHUNK):
            part = slice(start, start + ROW_CHUNK)
            block = x[part, :].astype(F32)
            centred = block - jnp.mean(block, axis=-1, keepdims=True)
            unit = centred * lax.rsqrt(jnp.mean(centred * centred, axis=-1, keepdims=True) + EPSILON)
            attn = (unit * attn_gain[...].astype(F32) + attn_shift[...].astype(F32)).astype(BF16)
            mlp = (unit * mlp_gain[...].astype(F32) + mlp_shift[...].astype(F32)).astype(BF16)
            attn_in[part, :] = attn
            mlp_in[part, :] = mlp
            attn_in_t[:, part] = attn.T
            mlp_in_t[:, part] = mlp.T
        loads[0].wait()
        for load in loads[1:]:
            load.start()
        stores.start(attn_in_t, attn_in_h.at[micro])
        stores.start(mlp_in_t, mlp_in_h.at[micro])

        cos_rows, sin_rows = cosine[...], sine[...]
        for start in range(0, 3 * width, QKV_TILE):
            part = slice(start, start + QKV_TILE)
            projected = jnp.dot(attn_in[...], qkv_w[:, part], preferred_element_type=F32)
            turned = (projected + qkv_bias[:, part].astype(F32)).T
            if start >= 2 * width:
                heads_t[part, :] = turned.astype(BF16)
                continue
            for at in range(0, QKV_TILE, HEAD_DIM):
                low, high = turned[at : at + HALF], turned[at + HALF : at + ROTARY]
                heads_t[start + at : start + at + HEAD_DIM, :] = jnp.concatenate(
                    [
                        low * cos_rows - high * sin_rows,
                        high * cos_rows + low * sin_rows,
                        turned[at + ROTARY : at + HEAD_DIM],
                    ],
                    axis=0,
                ).astype(BF16)
        stores.start(heads_t.at[0:width], queries_h.at[micro])
        stores.start(heads_t.at[width : 2 * width], keys_h.at[micro])
        stores.start(heads_t.at[2 * width :], values_h.at[micro])

        def softmax(scores):
            raised = jnp.exp(scores - jnp.max(scores, axis=0, keepdims=True))
            return (raised * (1.0 / jnp.sum(raised, axis=0, keepdims=True))).astype(BF16)

        def attend(head, slot):
            at = pl.multiple_of(head * HEAD_DIM, HEAD_DIM)
            query = heads_t[pl.ds(at, HEAD_DIM), :] * jnp.bfloat16(SCALE)
            key = heads_t[pl.ds(width + at, HEAD_DIM), :]
            value = heads_t[pl.ds(2 * width + at, HEAD_DIM), :]
            early = softmax(dims_dot(key[:, :half], query[:, :half], 0, 0) + bias[:half, :half])
            late = softmax(dims_dot(key, query[:, half:], 0, 0) + bias[:, half:])
            probs[slot, :half, :half] = early
            probs[slot, :, half:] = late
            place = pl.ds(at, HEAD_DIM)
            context_t[place, :half] = jnp.dot(value[:, :half], early, preferred_element_type=F32).astype(BF16)
            context_t[place, half:] = jnp.dot(value, late, preferred_element_type=F32).astype(BF16)

        def probs_copy(head, slot):
            return pltpu.make_async_copy(probs.at[slot], probs_h.at[micro, head], probs_sems.at[slot])

        def attend_pair(pair, carry):
            first_slot = 2 * lax.rem(pair, 2)

            @pl.when(pair >= 2)
            def _():
                for own_head in range(2):
                    probs_copy(2 * pair + own_head - 4, first_slot + own_head).wait()

            for own_head in range(2):
                attend(2 * pair + own_head, first_slot + own_head)
            for own_head in range(2):
                probs_copy(2 * pair + own_head, first_slot + own_head).start()
            return carry

        lax.fori_loop(0, HEADS // 2, attend_pair, 0)
        for head in range(HEADS - 4, HEADS):
            probs_copy(head, head % 4).wait()
        stores.start(context_t, context_h.at[micro])

        for load in loads[1:]:
            load.wait()
        total[...] = (
            dims_dot(context_t[...], out_w[...], 0, 0)
            + x[...].astype(F32)
            + (out_bias[...].astype(F32) + down_bias[...].astype(F32))
        )
        for start in range(0, hidden_width, FF_TILE):
            part = slice(start, start + FF_TILE)
            up = jnp.dot(mlp_in[...], up_w[:, part], preferred_element_type=F32)
            up = up + up_bias[:, part].astype(F32)
            share, density = normal_parts(up)
            hidden = (up * share).astype(BF16)
            slope[:, part] = (share + up * density).astype(BF16)
            hidden_t[part, :] = hidden.T
            stores.start(hidden_t.at[part], hidden_h.at[micro, part])
            stores.start(slope.at[:, part], slope_h.at[micro, :, part])
            total[...] += jnp.dot(hidden, down_w[part, :], preferred_element_type=F32)
        y[...] = total[...].astype(BF16)
        stores.start(y, y_send_h)
        stores.start(y, y_h.at[micro])
        stores.wait()


def forward_call(moment, lengths, tokens, received, weights, tables, stash):
    (
        attn_gain, attn_shift, qkv_weight, qkv_bias, out_weight, out_bias, mlp_gain, mlp_shift, up_weight, up_bias,
        down_weight, down_bias,
    ) = weights
    micros, rows, width = tokens.shape
    hidden_width = up_weight.shape[1]
    wide, tall = (micros, rows, width), (micros, width, rows)
    shapes = [
        (rows, width), wide, tall, tall, tall, tall, tall, (micros, HEADS, rows, rows), tall,
        (micros, hidden_width, rows), (micros, rows, hidden_width),
    ]
    kept = () if stash is None else tuple(stash)
    buffers = [
        qkv_weight.shape, out_weight.shape, up_weight.shape, down_weight.shape, (rows, width), (rows, width),
        (rows, width), (width, rows), (width, rows), (3 * width, rows), (width, rows), (hidden_width, rows),
        (rows, hidden_width),
    ]
    outs = pl.pallas_call(
        functools.partial(forward_kernel, moment, micros, len(kept)),
        out_shape=[jax.ShapeDtypeStruct(shape, BF16) for shape in shapes],
        in_specs=[SMEM, ANY, ANY] + [VMEM] * 10 + [ANY] * (4 + len(kept)),
        out_specs=[ANY] * len(shapes),
        scratch_shapes=[pltpu.VMEM(shape, BF16) for shape in buffers]
        + [
            pltpu.VMEM((rows, rows), F32),
            pltpu.VMEM((rows, width), F32),
            pltpu.VMEM((4, rows, rows), BF16),
            pltpu.VMEM((rows, width), BF16),
            pltpu.SemaphoreType.DMA((5,)),
            pltpu.SemaphoreType.DMA((8 + 2 * (hidden_width // FF_TILE),)),
            pltpu.SemaphoreType.DMA((4,)),
        ],
        input_output_aliases={17 + i: 1 + i for i in range(len(kept))},
        compiler_params=pltpu.CompilerParams(vmem_limit_bytes=56 << 20),
        cost_estimate=pl.CostEstimate(
            flops=2 * rows * width * (4 * width + 2 * hidden_width) + 4 * rows * rows * width,
            bytes_accessed=40 << 20,
            transcendentals=rows * hidden_width,
        ),
        name="layer_forward",
    )(
        lengths, tokens, received, attn_gain, attn_shift, qkv_bias, out_bias, mlp_gain, mlp_shift, up_bias,
        down_bias, *tables, qkv_weight, out_weight, up_weight, down_weight, *kept,
    )
    return outs[0], outs[1:]


def backward_kernel(moment, micros, n_alias, *refs):
    n_in = 17 + micros
    lengths, cotangent_h, received_h, tokens_h = refs[:4]
    passed_h = refs[4 : 4 + micros]
    (
        attn_gain, mlp_gain, cosine, sine, qkv_h, out_h, up_h, down_h, queries_h, keys_h, values_h, probs_h,
        context_h, slope_h,
    ) = refs[4 + micros : 18 + micros]
    (
        send_h, grad_in_h, grad_heads_h, grad_up_h, grad_out_h, vectors_h,
        qkv_w, out_w, up_w, down_w, queries, keys, values, context, slope, probs, grad_out, x, grad_context,
        grad_up, grad_heads, grad_low, grad_mlp, grad_in, column_sums, vectors, in_sems, out_sems, probs_sems,
    ) = refs[18 + micros + n_alias :]
    section = lax.axis_index("section")
    last = lax.axis_size("section") - 1
    micro = moment - (last - section)
    rows, width = x.shape
    hidden_width = up_w.shape[1]
    half = rows // 2

    @pl.when((micro >= 0) & (micro < micros))
    def _():
        loads = [
            pltpu.make_async_copy(src, dst, in_sems.at[i])
            for i, (src, dst) in enumerate(
                (
                    (out_h, out_w), (down_h, down_w), (slope_h.at[micro], slope), (up_h, up_w),
                    (values_h.at[micro], values), (context_h.at[micro], context), (queries_h.at[micro], queries),
                    (keys_h.at[micro], keys), (qkv_h, qkv_w),
                )
            )
        ]
        own = pltpu.make_async_copy(cotangent_h.at[micro], grad_out, in_sems.at[9])
        passed = pltpu.make_async_copy(received_h, grad_out, in_sems.at[9])
        block = pltpu.make_async_copy(tokens_h.at[micro], x, in_sems.at[10])

        @pl.when(section == last)
        def _():
            own.start()

        @pl.when(section != last)
        def _():
            passed.start()

        for load in loads[:4]:
            load.start()

        @pl.when(section == 0)
        def _():
            block.start()

        for one, source in enumerate(passed_h):

            @pl.when((section != 0) & (micro == one))
            def _():
                pltpu.make_async_copy(source, x, in_sems.at[10]).start()

        stores = Copies(out_sems)
        length = lengths[micro]
        row_ids = lax.broadcasted_iota(jnp.int32, (rows, 1), 0)
        own.wait()
        grad_wide = jnp.where(row_ids < length, grad_out[...].astype(F32), 0.0)
        grad_out[...] = grad_wide.astype(BF16)
        vectors[...] = jnp.zeros_like(vectors)
        vectors[7:8, :] = jnp.sum(grad_wide, axis=0, keepdims=True)
        stores.start(grad_out, grad_out_h.at[micro])
        loads[0].wait()
        for load in loads[4:]:
            load.start()
        grad_context[...] = dims_dot(out_w[...], grad_out[...], 1, 1).astype(BF16)

        for load in loads[1:4]:
            load.wait()
        for start in range(0, hidden_width, FF_TILE):
            part = slice(start, start + FF_TILE)
            grad_hidden = dims_dot(grad_out[...], down_w[part, :], 1, 1)
            grad_pre = (grad_hidden * slope[:, part].astype(F32)).astype(BF16)
            grad_up[:, part] = grad_pre
            stores.start(grad_up.at[:, part], grad_up_h.at[micro, :, part])
            sums = jnp.sum(grad_pre.astype(F32), axis=0, keepdims=True)
            for at in range(0, FF_TILE, 128):
                row, column = divmod(start + at, width)
                vectors[8 + row : 9 + row, column : column + 128] = sums[:, at : at + 128]
            back = dims_dot(up_w[:, part], grad_pre, 1, 1)
            if start == 0:
                grad_mlp[...] = back
            else:
                grad_mlp[...] += back

        for load in loads[4:8]:
            load.wait()
        cos_rows, sin_rows = cosine[...], sine[...]

        def turn_back(grad):
            low, high = grad[:HALF], grad[HALF:ROTARY]
            return jnp.concatenate(
                [low * cos_rows + high * sin_rows, high * cos_rows - low * sin_rows, grad[ROTARY:]], axis=0
            )

        def over_queries(left, early, late):
            both = dims_dot(left[:, half:], late, 1, 1)
            return jnp.concatenate([both[:, :half] + dims_dot(left[:, :half], early, 1, 1), both[:, half:]], axis=1)

        def attend(head, slot):
            at = pl.multiple_of(head * HEAD_DIM, HEAD_DIM)
            place = pl.ds(at, HEAD_DIM)
            query, key, value, grad = queries[place, :], keys[place, :], values[place, :], grad_context[place, :]
            inner = jnp.sum(grad.astype(F32) * context[place, :].astype(F32), axis=0, keepdims=True)
            early, late = probs[slot, :half, :half], probs[slot, :, half:]
            grad_early = dims_dot(value[:, :half], grad[:, :half], 0, 0) - inner[:, :half]
            grad_late = dims_dot(value, grad[:, half:], 0, 0) - inner[:, half:]
            grad_early = (early.astype(F32) * grad_early).astype(BF16)
            grad_late = (late.astype(F32) * grad_late).astype(BF16)
            grad_value = over_queries(grad, early, late)
            grad_key = over_queries(query, grad_early, grad_late)
            grad_query = jnp.concatenate(
                [
                    jnp.dot(key[:, :half], grad_early, preferred_element_type=F32),
                    jnp.dot(key, grad_late, preferred_element_type=F32),
                ],
                axis=1,
            )
            grad_heads[place, :] = turn_back(grad_query * SCALE).astype(BF16)
            grad_heads[pl.ds(width + at, HEAD_DIM), :] = turn_back(grad_key * SCALE).astype(BF16)
            grad_heads[pl.ds(2 * width + at, HEAD_DIM), :] = grad_value.astype(BF16)

        def probs_copy(head, slot):
            return pltpu.make_async_copy(probs_h.at[micro, head], probs.at[slot], probs_sems.at[slot])

        for head in range(2):
            probs_copy(head, head).start()

        def attend_pair(pair, carry):
            first_slot = 2 * lax.rem(pair, 2)

            @pl.when(pair < HEADS // 2 - 1)
            def _():
                for own_head in range(2):
                    probs_copy(2 * pair + 2 + own_head, 2 - first_slot + own_head).start()

            for own_head in range(2):
                probs_copy(2 * pair + own_head, first_slot + own_head).wait()
            for own_head in range(2):
                attend(2 * pair + own_head, first_slot + own_head)
            return carry

        lax.fori_loop(0, HEADS // 2, attend_pair, 0)
        stores.start(grad_heads, grad_heads_h.at[micro])

        loads[8].wait()
        block.wait()
        attn_column = jnp.broadcast_to(attn_gain[...].astype(F32), (8, width)).T[:, 0:1]
        mlp_column = jnp.broadcast_to(mlp_gain[...].astype(F32), (8, width)).T[:, 0:1]
        column_sums[...] = jnp.zeros_like(column_sums)

        def norm_chunk(index, carry):
            part = pl.ds(pl.multiple_of(index * ROW_CHUNK, ROW_CHUNK), ROW_CHUNK)
            grad_attn_in = jnp.dot(qkv_w[...], grad_heads[:, part], preferred_element_type=F32)
            grad_mlp_in = grad_mlp[:, part]
            turned = x[part, :].astype(F32).T
            centred = turned - jnp.mean(turned, axis=0, keepdims=True)
            inv_spread = lax.rsqrt(jnp.mean(centred * centred, axis=0, keepdims=True) + EPSILON)
            unit = centred * inv_spread
            grad_unit = grad_attn_in * attn_column + grad_mlp_in * mlp_column
            through = inv_spread * (
                grad_unit
                - jnp.mean(grad_unit, axis=0, keepdims=True)
                - unit * jnp.mean(grad_unit * unit, axis=0, keepdims=True)
            )
            exact = through.T + grad_out[part, :].astype(F32)
            low = exact.astype(BF16)
            grad_low[part, :] = low
            grad_in[part, :] = jnp.where(section == 0, exact, low.astype(F32))
            column_sums[0] += grad_attn_in * unit
            column_sums[1] += grad_attn_in
            column_sums[2] += grad_mlp_in * unit
            column_sums[3] += grad_mlp_in
            return carry

        lax.fori_loop(0, rows // ROW_CHUNK, norm_chunk, 0)
        stores.start(grad_low, send_h)
        stores.start(grad_in, grad_in_h.at[micro])
        columns = [jnp.sum(column_sums[i], axis=1, keepdims=True) for i in range(4)]
        for start in range(0, 3 * width, width):
            columns.append(jnp.sum(grad_heads[start : start + width, :].astype(F32), axis=1, keepdims=True))
        lanes = lax.broadcasted_iota(jnp.int32, (width, 128), 1)
        gathered = jnp.zeros((width, 128), F32)
        for lane, column in enumerate(columns):
            gathered = jnp.where(lanes == lane, column, gathered)
        vectors[0:7, :] = gathered.T[0:7, :]
        stores.start(vectors, vectors_h.at[micro])
        stores.wait()


def backward_call(moment, lengths, cotangent, received, tokens, passed, weights, tables, stash, kept):
    attn_gain, _, qkv_weight, _, out_weight, _, mlp_gain, _, up_weight, _, down_weight, _ = weights
    _, _, _, queries, keys, values, probs, context, _, slope = stash
    micros, rows, width = tokens.shape
    hidden_width = up_weight.shape[1]
    vector_rows = 16
    kept = () if kept is None else tuple(kept)
    outs = [
        jax.ShapeDtypeStruct((rows, width), BF16),
        jax.ShapeDtypeStruct((micros, rows, width), F32),
        jax.ShapeDtypeStruct((micros, 3 * width, rows), BF16),
        jax.ShapeDtypeStruct((micros, rows, hidden_width), BF16),
        jax.ShapeDtypeStruct((micros, rows, width), BF16),
        jax.ShapeDtypeStruct((micros, vector_rows, width), F32),
    ]
    tall = (width, rows)
    n_in = 18 + micros
    results = pl.pallas_call(
        functools.partial(backward_kernel, moment, micros, len(kept)),
        out_shape=outs,
        in_specs=[SMEM] + [ANY] * (3 + micros) + [VMEM] * 4 + [ANY] * (10 + len(kept)),
        out_specs=[ANY] * len(outs),
        scratch_shapes=[
            pltpu.VMEM(qkv_weight.shape, BF16),
            pltpu.VMEM(out_weight.shape, BF16),
            pltpu.VMEM(up_weight.shape, BF16),
            pltpu.VMEM(down_weight.shape, BF16),
            pltpu.VMEM(tall, BF16),
            pltpu.VMEM(tall, BF16),
            pltpu.VMEM(tall, BF16),
            pltpu.VMEM(tall, BF16),
            pltpu.VMEM((rows, hidden_width), BF16),
            pltpu.VMEM((4, rows, rows), BF16),
            pltpu.VMEM((rows, width), BF16),
            pltpu.VMEM((rows, width), BF16),
            pltpu.VMEM(tall, BF16),
            pltpu.VMEM((rows, hidden_width), BF16),
            pltpu.VMEM((3 * width, rows), BF16),
            pltpu.VMEM((rows, width), BF16),
            pltpu.VMEM(tall, F32),
            pltpu.VMEM((rows, width), F32),
            pltpu.VMEM((4, width, 128), F32),
            pltpu.VMEM((vector_rows, width), F32),
            pltpu.SemaphoreType.DMA((11,)),
            pltpu.SemaphoreType.DMA((5 + hidden_width // FF_TILE,)),
            pltpu.SemaphoreType.DMA((4,)),
        ],
        input_output_aliases={n_in + i: 1 + i for i in range(len(kept))},
        compiler_params=pltpu.CompilerParams(vmem_limit_bytes=58 << 20),
        cost_estimate=pl.CostEstimate(
            flops=2 * rows * width * (4 * width + 2 * hidden_width) + 8 * rows * rows * width,
            bytes_accessed=40 << 20,
            transcendentals=0,
        ),
        name="layer_backward",
    )(
        lengths, cotangent, received, tokens, *passed, attn_gain, mlp_gain, *tables, qkv_weight, out_weight,
        up_weight, down_weight, queries, keys, values, probs, context, slope, *kept,
    )
    return results[0], results[1:]


def shifted(value, axis, by):
    size = lax.axis_size(axis)
    pairs = [(i, i + by) for i in range(size) if 0 <= i + by < size]
    return lax.ppermute(value, axis, pairs)


def rotary_tables(seq_len):
    positions = jnp.arange(seq_len, dtype=F32)
    inverse = 1.0 / ROTARY_BASE ** (jnp.arange(0, ROTARY, 2, dtype=F32) / ROTARY)
    angles = inverse[:, None] * positions[None, :]
    return jnp.cos(angles), jnp.sin(angles)


def summed(share):
    part = lax.psum_scatter(share.astype(BF16), "dp", scatter_dimension=0, tiled=True)
    return lax.psum(part, "replica").astype(F32)


def body(tokens, cotangent, lengths, *weights):
    weights = tuple(array if array.ndim == 2 else array[0] for array in weights)
    micros = lengths.shape[0]
    width = tokens.shape[1]
    rows = tokens.shape[0] // micros
    sections = lax.axis_size("section")
    inputs = tokens.reshape(micros, rows, width)
    cotans = cotangent.reshape(micros, rows, width)
    tables = rotary_tables(rows)

    stash, received, passed = None, inputs[0], []
    for moment in range(micros + sections - 1):
        sent, stash = forward_call(moment, lengths, inputs, received, weights, tables, stash)
        if moment < micros:
            received = shifted(sent, "section", 1)
            passed.append(received)

    kept, received = None, cotans[0]
    for moment in range(micros + sections - 1):
        sent, kept = backward_call(
            moment, lengths, cotans, received, inputs, passed, weights, tables, stash, kept
        )
        if moment < micros:
            received = shifted(sent, "section", -1)

    outputs, attn_in, mlp_in, _, _, _, _, context, hidden, _ = stash
    grad_in, grad_heads, grad_up, grad_out, vectors = kept
    vector_sums = jnp.sum(vectors, axis=0)
    totals = (
        vector_sums[0],
        vector_sums[1],
        jnp.einsum("mdr,mer->de", attn_in, grad_heads, preferred_element_type=F32),
        vector_sums[4:7].reshape(-1),
        jnp.einsum("mer,mrd->ed", context, grad_out, preferred_element_type=F32),
        vector_sums[7],
        vector_sums[2],
        vector_sums[3],
        jnp.einsum("mdr,mrf->df", mlp_in, grad_up, preferred_element_type=F32),
        vector_sums[8:12].reshape(-1),
        jnp.einsum("mfr,mrd->fd", hidden, grad_out, preferred_element_type=F32),
        vector_sums[7],
    )
    grad_scale = float(tokens.shape[0] * lax.axis_size("dp") * lax.axis_size("replica")) ** (-0.5)
    scaled = tuple(summed(total)[None] * grad_scale for total in totals)
    return (outputs.reshape(1, micros * rows, width), grad_in.reshape(1, micros * rows, width), *scaled)


def solution(mesh):
    rows = P(("dp", "replica"), None)
    vector, matrix = P("section", None), P("section", None, None)
    out_rows = P("section", ("dp", "replica"), None)
    vector_out, matrix_out = P("section", "dp"), P("section", "dp", None)
    return jax.shard_map(
        body,
        mesh=mesh,
        in_specs=(
            rows, rows, P(("dp", "replica")), vector, vector, matrix, vector, matrix, vector, vector, vector, matrix,
            vector, matrix, vector,
        ),
        out_specs=(
            out_rows, out_rows, vector_out, vector_out, matrix_out, vector_out, matrix_out, vector_out, vector_out,
            vector_out, matrix_out, vector_out, matrix_out, vector_out,
        ),
        check_vma=False,
    )
```

```python
import functools

import jax
import jax.numpy as jnp
from jax import lax
from jax.experimental import pallas as pl
from jax.experimental.pallas import tpu as pltpu
from jax.sharding import PartitionSpec as P

HEADS = 12
HEAD_DIM = 64
ROTARY = 16
HALF = ROTARY // 2
EPSILON = 1e-05
ROTARY_BASE = 10000.0
MASKED = -1e30
SCALE = HEAD_DIM**-0.5
F32 = jnp.float32
BF16 = jnp.bfloat16
ANY = pl.BlockSpec(memory_space=pl.ANY)
VMEM = pl.BlockSpec(memory_space=pltpu.VMEM)
SMEM = pl.BlockSpec(memory_space=pltpu.SMEM)
ROW_CHUNK = 128
QKV_TILE = 256
FF_TILE = 512
PIECE = 384


def dims_dot(left, right, left_dim, right_dim):
    return lax.dot_general(
        left, right, (((left_dim,), (right_dim,)), ((), ())), preferred_element_type=F32
    )


def normal_parts(v):
    t = 1.0 / (1.0 + (0.3275911 * 0.7071067811865476) * jnp.abs(v))
    bell = jnp.exp(-0.5 * v * v)
    series = 0.7107068705 + t * (-0.7265760135 + t * 0.5307027145)
    tail = t * (0.127414796 + t * (-0.142248368 + t * series)) * bell
    return jnp.where(v >= 0, 1.0 - tail, tail), bell * 0.3989422804014327


class Copies:
    def __init__(self, sems):
        self.sems, self.copies = sems, []

    def start(self, src, dst):
        copy = pltpu.make_async_copy(src, dst, self.sems.at[len(self.copies)])
        copy.start()
        self.copies.append(copy)
        return copy

    def wait(self):
        for copy in self.copies:
            copy.wait()


def forward_kernel(moment, micros, n_alias, *refs):
    (
        lengths, tokens_h, received_h, attn_gain, attn_shift, qkv_bias, out_bias, mlp_gain, mlp_shift,
        up_bias, down_bias, cosine, sine, qkv_h, out_h, up_h, down_h,
    ) = refs[:17]
    (
        y_send_h, y_h, attn_in_h, mlp_in_h, queries_h, keys_h, values_h, probs_h, context_h, hidden_h, slope_h,
        qkv_w, out_w, up_w, down_w, x, attn_in, mlp_in, attn_in_t, mlp_in_t, heads_t, context_t, hidden_t, slope,
        bias, total, probs, y, in_sems, out_sems, probs_sems,
    ) = refs[17 + n_alias :]
    section = lax.axis_index("section")
    micro = moment - section
    rows, width = x.shape
    hidden_width = up_w.shape[1]
    half = rows // 2

    @pl.when((micro >= 0) & (micro < micros))
    def _():
        loads = [
            pltpu.make_async_copy(src, dst, in_sems.at[i])
            for i, (src, dst) in enumerate(((qkv_h, qkv_w), (out_h, out_w), (up_h, up_w), (down_h, down_w)))
        ]
        own = pltpu.make_async_copy(tokens_h.at[micro], x, in_sems.at[4])
        passed = pltpu.make_async_copy(received_h, x, in_sems.at[4])

        @pl.when(section == 0)
        def _():
            own.start()

        @pl.when(section != 0)
        def _():
            passed.start()

        loads[0].start()
        stores = Copies(out_sems)
        length = lengths[micro]
        key_ids = lax.broadcasted_iota(jnp.int32, (rows, rows), 0)
        query_ids = lax.broadcasted_iota(jnp.int32, (rows, rows), 1)
        bias[...] = jnp.where((key_ids <= query_ids) & (key_ids < length), 0.0, MASKED)
        probs[:, half:, :half] = jnp.zeros((probs.shape[0], half, half), BF16)
        own.wait()

        for start in range(0, rows, ROW_CHUNK):
            part = slice(start, start + ROW_CHUNK)
            block = x[part, :].astype(F32)
            centred = block - jnp.mean(block, axis=-1, keepdims=True)
            unit = centred * lax.rsqrt(jnp.mean(centred * centred, axis=-1, keepdims=True) + EPSILON)
            attn = (unit * attn_gain[...].astype(F32) + attn_shift[...].astype(F32)).astype(BF16)
            mlp = (unit * mlp_gain[...].astype(F32) + mlp_shift[...].astype(F32)).astype(BF16)
            attn_in[part, :] = attn
            mlp_in[part, :] = mlp
            attn_in_t[:, part] = attn.T
            mlp_in_t[:, part] = mlp.T
        loads[0].wait()
        for load in loads[1:]:
            load.start()
        stores.start(attn_in_t, attn_in_h.at[micro])
        stores.start(mlp_in_t, mlp_in_h.at[micro])

        cos_rows, sin_rows = cosine[...], sine[...]
        for start in range(0, 3 * width, QKV_TILE):
            part = slice(start, start + QKV_TILE)
            projected = jnp.dot(attn_in[...], qkv_w[:, part], preferred_element_type=F32)
            turned = (projected + qkv_bias[:, part].astype(F32)).T
            if start >= 2 * width:
                heads_t[part, :] = turned.astype(BF16)
                continue
            for at in range(0, QKV_TILE, HEAD_DIM):
                low, high = turned[at : at + HALF], turned[at + HALF : at + ROTARY]
                heads_t[start + at : start + at + HEAD_DIM, :] = jnp.concatenate(
                    [
                        low * cos_rows - high * sin_rows,
                        high * cos_rows + low * sin_rows,
                        turned[at + ROTARY : at + HEAD_DIM],
                    ],
                    axis=0,
                ).astype(BF16)
        stores.start(heads_t.at[0:width], queries_h.at[micro])
        stores.start(heads_t.at[width : 2 * width], keys_h.at[micro])
        stores.start(heads_t.at[2 * width :], values_h.at[micro])

        def softmax(scores):
            raised = jnp.exp(scores - jnp.max(scores, axis=0, keepdims=True))
            return (raised * (1.0 / jnp.sum(raised, axis=0, keepdims=True))).astype(BF16)

        def attend(head, slot):
            at = pl.multiple_of(head * HEAD_DIM, HEAD_DIM)
            query = heads_t[pl.ds(at, HEAD_DIM), :] * jnp.bfloat16(SCALE)
            key = heads_t[pl.ds(width + at, HEAD_DIM), :]
            value = heads_t[pl.ds(2 * width + at, HEAD_DIM), :]
            early = softmax(dims_dot(key[:, :half], query[:, :half], 0, 0) + bias[:half, :half])
            late = softmax(dims_dot(key, query[:, half:], 0, 0) + bias[:, half:])
            probs[slot, :half, :half] = early
            probs[slot, :, half:] = late
            place = pl.ds(at, HEAD_DIM)
            context_t[place, :half] = jnp.dot(value[:, :half], early, preferred_element_type=F32).astype(BF16)
            context_t[place, half:] = jnp.dot(value, late, preferred_element_type=F32).astype(BF16)

        def probs_copy(head, slot):
            return pltpu.make_async_copy(probs.at[slot], probs_h.at[micro, head], probs_sems.at[slot])

        def attend_pair(pair, carry):
            first_slot = 2 * lax.rem(pair, 2)

            @pl.when(pair >= 2)
            def _():
                for own_head in range(2):
                    probs_copy(2 * pair + own_head - 4, first_slot + own_head).wait()

            for own_head in range(2):
                attend(2 * pair + own_head, first_slot + own_head)
            for own_head in range(2):
                probs_copy(2 * pair + own_head, first_slot + own_head).start()
            return carry

        lax.fori_loop(0, HEADS // 2, attend_pair, 0)
        for head in range(HEADS - 4, HEADS):
            probs_copy(head, head % 4).wait()
        stores.start(context_t, context_h.at[micro])

        for load in loads[1:]:
            load.wait()
        total[...] = (
            dims_dot(context_t[...], out_w[...], 0, 0)
            + x[...].astype(F32)
            + (out_bias[...].astype(F32) + down_bias[...].astype(F32))
        )
        for start in range(0, hidden_width, FF_TILE):
            part = slice(start, start + FF_TILE)
            up = jnp.dot(mlp_in[...], up_w[:, part], preferred_element_type=F32)
            up = up + up_bias[:, part].astype(F32)
            share, density = normal_parts(up)
            hidden = (up * share).astype(BF16)
            slope[:, part] = (share + up * density).astype(BF16)
            hidden_t[part, :] = hidden.T
            stores.start(hidden_t.at[part], hidden_h.at[micro, part])
            stores.start(slope.at[:, part], slope_h.at[micro, :, part])
            total[...] += jnp.dot(hidden, down_w[part, :], preferred_element_type=F32)
        y[...] = total[...].astype(BF16)
        stores.start(y, y_send_h)
        stores.start(y, y_h.at[micro])
        stores.wait()


def forward_call(moment, lengths, tokens, received, weights, tables, stash):
    (
        attn_gain, attn_shift, qkv_weight, qkv_bias, out_weight, out_bias, mlp_gain, mlp_shift, up_weight, up_bias,
        down_weight, down_bias,
    ) = weights
    micros, rows, width = tokens.shape
    hidden_width = up_weight.shape[1]
    wide, tall = (micros, rows, width), (micros, width, rows)
    shapes = [
        (rows, width), wide, tall, tall, tall, tall, tall, (micros, HEADS, rows, rows), tall,
        (micros, hidden_width, rows), (micros, rows, hidden_width),
    ]
    kept = () if stash is None else tuple(stash)
    buffers = [
        qkv_weight.shape, out_weight.shape, up_weight.shape, down_weight.shape, (rows, width), (rows, width),
        (rows, width), (width, rows), (width, rows), (3 * width, rows), (width, rows), (hidden_width, rows),
        (rows, hidden_width),
    ]
    outs = pl.pallas_call(
        functools.partial(forward_kernel, moment, micros, len(kept)),
        out_shape=[jax.ShapeDtypeStruct(shape, BF16) for shape in shapes],
        in_specs=[SMEM, ANY, ANY] + [VMEM] * 10 + [ANY] * (4 + len(kept)),
        out_specs=[ANY] * len(shapes),
        scratch_shapes=[pltpu.VMEM(shape, BF16) for shape in buffers]
        + [
            pltpu.VMEM((rows, rows), F32),
            pltpu.VMEM((rows, width), F32),
            pltpu.VMEM((4, rows, rows), BF16),
            pltpu.VMEM((rows, width), BF16),
            pltpu.SemaphoreType.DMA((5,)),
            pltpu.SemaphoreType.DMA((8 + 2 * (hidden_width // FF_TILE),)),
            pltpu.SemaphoreType.DMA((4,)),
        ],
        input_output_aliases={17 + i: 1 + i for i in range(len(kept))},
        compiler_params=pltpu.CompilerParams(vmem_limit_bytes=56 << 20),
        cost_estimate=pl.CostEstimate(
            flops=2 * rows * width * (4 * width + 2 * hidden_width) + 4 * rows * rows * width,
            bytes_accessed=40 << 20,
            transcendentals=rows * hidden_width,
        ),
        name="layer_forward",
    )(
        lengths, tokens, received, attn_gain, attn_shift, qkv_bias, out_bias, mlp_gain, mlp_shift, up_bias,
        down_bias, *tables, qkv_weight, out_weight, up_weight, down_weight, *kept,
    )
    return outs[0], outs[1:]


def backward_kernel(moment, micros, n_alias, *refs):
    n_in = 17 + micros
    lengths, cotangent_h, received_h, tokens_h = refs[:4]
    passed_h = refs[4 : 4 + micros]
    (
        attn_gain, mlp_gain, cosine, sine, qkv_h, out_h, up_h, down_h, queries_h, keys_h, values_h, probs_h,
        context_h, slope_h,
    ) = refs[4 + micros : 18 + micros]
    (
        send_h, grad_in_h, grad_heads_h, grad_up_h, grad_out_h, vectors_h,
        qkv_w, out_w, up_w, down_w, queries, keys, values, context, slope, probs, grad_out, x, grad_context,
        grad_up, grad_heads, grad_low, grad_mlp, grad_in, column_sums, vectors, in_sems, out_sems, probs_sems,
    ) = refs[18 + micros + n_alias :]
    section = lax.axis_index("section")
    last = lax.axis_size("section") - 1
    micro = moment - (last - section)
    rows, width = x.shape
    hidden_width = up_w.shape[1]
    half = rows // 2

    @pl.when((micro >= 0) & (micro < micros))
    def _():
        loads = [
            pltpu.make_async_copy(src, dst, in_sems.at[i])
            for i, (src, dst) in enumerate(
                (
                    (out_h, out_w), (down_h, down_w), (slope_h.at[micro], slope), (up_h, up_w),
                    (values_h.at[micro], values), (context_h.at[micro], context), (queries_h.at[micro], queries),
                    (keys_h.at[micro], keys), (qkv_h, qkv_w),
                )
            )
        ]
        own = pltpu.make_async_copy(cotangent_h.at[micro], grad_out, in_sems.at[9])
        passed = pltpu.make_async_copy(received_h, grad_out, in_sems.at[9])
        block = pltpu.make_async_copy(tokens_h.at[micro], x, in_sems.at[10])

        @pl.when(section == last)
        def _():
            own.start()

        @pl.when(section != last)
        def _():
            passed.start()

        for load in loads[:4]:
            load.start()

        @pl.when(section == 0)
        def _():
            block.start()

        for one, source in enumerate(passed_h):

            @pl.when((section != 0) & (micro == one))
            def _():
                pltpu.make_async_copy(source, x, in_sems.at[10]).start()

        stores = Copies(out_sems)
        length = lengths[micro]
        row_ids = lax.broadcasted_iota(jnp.int32, (rows, 1), 0)
        own.wait()
        grad_wide = jnp.where(row_ids < length, grad_out[...].astype(F32), 0.0)
        grad_out[...] = grad_wide.astype(BF16)
        vectors[...] = jnp.zeros_like(vectors)
        vectors[7:8, :] = jnp.sum(grad_wide, axis=0, keepdims=True)
        stores.start(grad_out, grad_out_h.at[micro])
        loads[0].wait()
        for load in loads[4:]:
            load.start()
        grad_context[...] = dims_dot(out_w[...], grad_out[...], 1, 1).astype(BF16)

        for load in loads[1:4]:
            load.wait()
        for start in range(0, hidden_width, FF_TILE):
            part = slice(start, start + FF_TILE)
            grad_hidden = dims_dot(grad_out[...], down_w[part, :], 1, 1)
            grad_pre = (grad_hidden * slope[:, part].astype(F32)).astype(BF16)
            grad_up[:, part] = grad_pre
            stores.start(grad_up.at[:, part], grad_up_h.at[micro, :, part])
            sums = jnp.sum(grad_pre.astype(F32), axis=0, keepdims=True)
            for at in range(0, FF_TILE, 128):
                row, column = divmod(start + at, width)
                vectors[8 + row : 9 + row, column : column + 128] = sums[:, at : at + 128]
            back = dims_dot(up_w[:, part], grad_pre, 1, 1)
            if start == 0:
                grad_mlp[...] = back
            else:
                grad_mlp[...] += back

        for load in loads[4:8]:
            load.wait()
        cos_rows, sin_rows = cosine[...], sine[...]

        def turn_back(grad):
            low, high = grad[:HALF], grad[HALF:ROTARY]
            return jnp.concatenate(
                [low * cos_rows + high * sin_rows, high * cos_rows - low * sin_rows, grad[ROTARY:]], axis=0
            )

        def over_queries(left, early, late):
            both = dims_dot(left[:, half:], late, 1, 1)
            return jnp.concatenate([both[:, :half] + dims_dot(left[:, :half], early, 1, 1), both[:, half:]], axis=1)

        def attend(head, slot):
            at = pl.multiple_of(head * HEAD_DIM, HEAD_DIM)
            place = pl.ds(at, HEAD_DIM)
            query, key, value, grad = queries[place, :], keys[place, :], values[place, :], grad_context[place, :]
            inner = jnp.sum(grad.astype(F32) * context[place, :].astype(F32), axis=0, keepdims=True)
            early, late = probs[slot, :half, :half], probs[slot, :, half:]
            grad_early = dims_dot(value[:, :half], grad[:, :half], 0, 0) - inner[:, :half]
            grad_late = dims_dot(value, grad[:, half:], 0, 0) - inner[:, half:]
            grad_early = (early.astype(F32) * grad_early).astype(BF16)
            grad_late = (late.astype(F32) * grad_late).astype(BF16)
            grad_value = over_queries(grad, early, late)
            grad_key = over_queries(query, grad_early, grad_late)
            grad_query = jnp.concatenate(
                [
                    jnp.dot(key[:, :half], grad_early, preferred_element_type=F32),
                    jnp.dot(key, grad_late, preferred_element_type=F32),
                ],
                axis=1,
            )
            grad_heads[place, :] = turn_back(grad_query * SCALE).astype(BF16)
            grad_heads[pl.ds(width + at, HEAD_DIM), :] = turn_back(grad_key * SCALE).astype(BF16)
            grad_heads[pl.ds(2 * width + at, HEAD_DIM), :] = grad_value.astype(BF16)

        def probs_copy(head, slot):
            return pltpu.make_async_copy(probs_h.at[micro, head], probs.at[slot], probs_sems.at[slot])

        for head in range(2):
            probs_copy(head, head).start()

        def attend_pair(pair, carry):
            first_slot = 2 * lax.rem(pair, 2)

            @pl.when(pair < HEADS // 2 - 1)
            def _():
                for own_head in range(2):
                    probs_copy(2 * pair + 2 + own_head, 2 - first_slot + own_head).start()

            for own_head in range(2):
                probs_copy(2 * pair + own_head, first_slot + own_head).wait()
            for own_head in range(2):
                attend(2 * pair + own_head, first_slot + own_head)
            return carry

        lax.fori_loop(0, HEADS // 2, attend_pair, 0)
        stores.start(grad_heads, grad_heads_h.at[micro])

        loads[8].wait()
        block.wait()
        attn_column = jnp.broadcast_to(attn_gain[...].astype(F32), (8, width)).T[:, 0:1]
        mlp_column = jnp.broadcast_to(mlp_gain[...].astype(F32), (8, width)).T[:, 0:1]
        column_sums[...] = jnp.zeros_like(column_sums)

        def norm_chunk(index, carry):
            part = pl.ds(pl.multiple_of(index * ROW_CHUNK, ROW_CHUNK), ROW_CHUNK)
            grad_attn_in = jnp.dot(qkv_w[...], grad_heads[:, part], preferred_element_type=F32)
            grad_mlp_in = grad_mlp[:, part]
            turned = x[part, :].astype(F32).T
            centred = turned - jnp.mean(turned, axis=0, keepdims=True)
            inv_spread = lax.rsqrt(jnp.mean(centred * centred, axis=0, keepdims=True) + EPSILON)
            unit = centred * inv_spread
            grad_unit = grad_attn_in * attn_column + grad_mlp_in * mlp_column
            through = inv_spread * (
                grad_unit
                - jnp.mean(grad_unit, axis=0, keepdims=True)
                - unit * jnp.mean(grad_unit * unit, axis=0, keepdims=True)
            )
            exact = through.T + grad_out[part, :].astype(F32)
            low = exact.astype(BF16)
            grad_low[part, :] = low
            grad_in[part, :] = jnp.where(section == 0, exact, low.astype(F32))
            column_sums[0] += grad_attn_in * unit
            column_sums[1] += grad_attn_in
            column_sums[2] += grad_mlp_in * unit
            column_sums[3] += grad_mlp_in
            return carry

        lax.fori_loop(0, rows // ROW_CHUNK, norm_chunk, 0)
        stores.start(grad_low, send_h)
        stores.start(grad_in, grad_in_h.at[micro])
        columns = [jnp.sum(column_sums[i], axis=1, keepdims=True) for i in range(4)]
        for start in range(0, 3 * width, width):
            columns.append(jnp.sum(grad_heads[start : start + width, :].astype(F32), axis=1, keepdims=True))
        lanes = lax.broadcasted_iota(jnp.int32, (width, 128), 1)
        gathered = jnp.zeros((width, 128), F32)
        for lane, column in enumerate(columns):
            gathered = jnp.where(lanes == lane, column, gathered)
        vectors[0:7, :] = gathered.T[0:7, :]
        stores.start(vectors, vectors_h.at[micro])
        stores.wait()


def backward_call(moment, lengths, cotangent, received, tokens, passed, weights, tables, stash, kept):
    attn_gain, _, qkv_weight, _, out_weight, _, mlp_gain, _, up_weight, _, down_weight, _ = weights
    _, _, _, queries, keys, values, probs, context, _, slope = stash
    micros, rows, width = tokens.shape
    hidden_width = up_weight.shape[1]
    vector_rows = 16
    kept = () if kept is None else tuple(kept)
    outs = [
        jax.ShapeDtypeStruct((rows, width), BF16),
        jax.ShapeDtypeStruct((micros, rows, width), F32),
        jax.ShapeDtypeStruct((micros, 3 * width, rows), BF16),
        jax.ShapeDtypeStruct((micros, rows, hidden_width), BF16),
        jax.ShapeDtypeStruct((micros, rows, width), BF16),
        jax.ShapeDtypeStruct((micros, vector_rows, width), F32),
    ]
    tall = (width, rows)
    n_in = 18 + micros
    results = pl.pallas_call(
        functools.partial(backward_kernel, moment, micros, len(kept)),
        out_shape=outs,
        in_specs=[SMEM] + [ANY] * (3 + micros) + [VMEM] * 4 + [ANY] * (10 + len(kept)),
        out_specs=[ANY] * len(outs),
        scratch_shapes=[
            pltpu.VMEM(qkv_weight.shape, BF16),
            pltpu.VMEM(out_weight.shape, BF16),
            pltpu.VMEM(up_weight.shape, BF16),
            pltpu.VMEM(down_weight.shape, BF16),
            pltpu.VMEM(tall, BF16),
            pltpu.VMEM(tall, BF16),
            pltpu.VMEM(tall, BF16),
            pltpu.VMEM(tall, BF16),
            pltpu.VMEM((rows, hidden_width), BF16),
            pltpu.VMEM((4, rows, rows), BF16),
            pltpu.VMEM((rows, width), BF16),
            pltpu.VMEM((rows, width), BF16),
            pltpu.VMEM(tall, BF16),
            pltpu.VMEM((rows, hidden_width), BF16),
            pltpu.VMEM((3 * width, rows), BF16),
            pltpu.VMEM((rows, width), BF16),
            pltpu.VMEM(tall, F32),
            pltpu.VMEM((rows, width), F32),
            pltpu.VMEM((4, width, 128), F32),
            pltpu.VMEM((vector_rows, width), F32),
            pltpu.SemaphoreType.DMA((11,)),
            pltpu.SemaphoreType.DMA((5 + hidden_width // FF_TILE,)),
            pltpu.SemaphoreType.DMA((4,)),
        ],
        input_output_aliases={n_in + i: 1 + i for i in range(len(kept))},
        compiler_params=pltpu.CompilerParams(vmem_limit_bytes=58 << 20),
        cost_estimate=pl.CostEstimate(
            flops=2 * rows * width * (4 * width + 2 * hidden_width) + 8 * rows * rows * width,
            bytes_accessed=40 << 20,
            transcendentals=0,
        ),
        name="layer_backward",
    )(
        lengths, cotangent, received, tokens, *passed, attn_gain, mlp_gain, *tables, qkv_weight, out_weight,
        up_weight, down_weight, queries, keys, values, probs, context, slope, *kept,
    )
    return results[0], results[1:]


def partner(axis, bit):
    index = lax.axis_index(axis)
    own_bit = (index // bit) % 2
    return {axis: index + bit - 2 * bit * own_bit}, own_bit


def piece_plan(width, hidden_width, piece):
    counts = [width // piece, hidden_width // piece, hidden_width // piece, 3 * width // piece]
    starts = [0]
    for count in counts:
        starts.append(starts[-1] + count)
    return starts


def reduce_kernel(bits, piece, *refs):
    (
        context_h, hidden_h, mlp_in_h, attn_in_h, grad_out_h, grad_up_h, grad_heads_h, vectors_h,
        qkv_o, out_o, up_o, down_o, vectors_o,
        left, right, heads, vectors, own, final, from_first, *rest,
    ) = refs
    from_dp, rest = rest[:bits], rest[bits:]
    (
        from_second, vector_sum, from_vector,
        in_sems, send_sems, recv_sems, vector_send, vector_recv, out_sems,
    ) = rest
    micros, devices, share, rows = attn_in_h.shape
    width = devices * share
    hidden_width = grad_up_h.shape[2]
    groups = hidden_width // width
    out_at, down_at, up_at, qkv_at, pieces = piece_plan(width, hidden_width, piece)
    across = width // piece

    barrier = pltpu.get_barrier_semaphore()
    dp_peers = [partner("dp", 1 << bit) for bit in range(bits)]
    replica_peers = [partner("replica", 1), partner("replica", 2)]
    for device, _ in dp_peers + replica_peers:
        pl.semaphore_signal(barrier, inc=1, device_id=device, device_id_type=pl.DeviceIdType.MESH)

    wide = hidden_width + width
    loads = [
        [(context_h, left.at[0]), (grad_out_h, right.at[:, :, 0:width]), (vectors_h, vectors)],
        [(hidden_h.at[:, :, group], left.at[3 + group]) for group in range(groups)],
        [(mlp_in_h, left.at[1]), (grad_up_h, right.at[:, :, width:wide])],
        [(attn_in_h, left.at[2]), (grad_heads_h, heads)],
    ]
    copies, count = [], 0
    for group in loads:
        copies.append([])
        for src, dst in group:
            copies[-1].append(pltpu.make_async_copy(src, dst, in_sems.at[count]))
            count += 1
    for copy in copies[0]:
        copy.start()
    for copy in copies[0]:
        copy.wait()
    for group in copies[1:]:
        for copy in group:
            copy.start()
    vector_sum[0] = jnp.sum(vectors[...], axis=0)
    pl.semaphore_wait(barrier, len(dp_peers) + len(replica_peers))

    dp_bits = [own_bit for _, own_bit in dp_peers]

    def keep(k, depth, first_bit=None, second_bit=None, flip=None):
        index = [k] + [slice(None)] * (bits - depth)
        for bit in reversed(range(depth)):
            index.append(1 - dp_bits[bit] if flip == bit else dp_bits[bit])
        if first_bit is not None:
            index.append(first_bit)
        if second_bit is not None:
            index.append(second_bit)
        return tuple(index)

    def transfers(k, turned):
        (first, first_bit), (second, second_bit) = replica_peers[::-1] if turned else replica_peers
        steps = [
            (own.at[keep(k, 0, 1 - first_bit)], from_first.at[k], first, own.at[keep(k, 0, first_bit)]),
        ]
        for bit in range(bits):
            steps.append(
                (
                    own.at[keep(k, bit + 1, first_bit, flip=bit)],
                    from_dp[bit].at[k],
                    dp_peers[bit][0],
                    own.at[keep(k, bit + 1, first_bit)],
                )
            )
        mine = final.at[k, first_bit, second_bit]
        steps.append(
            (
                own.at[keep(k, bits, first_bit, 1 - second_bit)],
                from_second.at[k],
                second,
                own.at[keep(k, bits, first_bit, second_bit)],
            )
        )
        steps.append((mine, mine, second, None))
        steps.append((final.at[k, first_bit], final.at[k, first_bit], first, None))
        return steps, mine

    def copy_of(k, stage, step):
        src, dst, device, _ = step
        return pltpu.make_async_remote_copy(
            src_ref=src,
            dst_ref=dst,
            send_sem=send_sems.at[k, stage],
            recv_sem=recv_sems.at[k, stage],
            device_id=device,
            device_id_type=pl.DeviceIdType.MESH,
        )

    n_steps = bits + 4

    def advance(k, stage, turned):
        steps, mine = transfers(k, turned)
        if stage > 0:
            step = steps[stage - 1]
            copy_of(k, stage - 1, step).wait()
            if step[3] is not None:
                total = step[3][...].astype(F32) + step[1][...].astype(F32)
                if stage == bits + 2:
                    mine[...] = total.astype(BF16)
                else:
                    step[3][...] = total.astype(BF16)
        if stage < n_steps:
            copy_of(k, stage, steps[stage]).start()

    def advance_either(k, stage):
        for turned in (False, True):

            @pl.when(k % 2 == int(turned))
            def _():
                advance(k, stage, turned)

    shape = own.shape[1:]

    def panel(index, micro):
        return left[index, micro].reshape(width, rows)

    def set_own(k, index, columns):
        value = columns(0, panel(index, 0))
        for micro in range(1, micros):
            value = value + columns(micro, panel(index, micro))
        own[k] = value.astype(BF16).reshape(shape)

    def lanes(index):
        return pl.ds(pl.multiple_of(index * piece, 128), piece)

    def compute(k):
        @pl.when(k < down_at)
        def _():
            part = lanes(k)
            set_own(k, 0, lambda micro, block: dims_dot(block, right[micro, :, part], 1, 0))

        @pl.when((k >= down_at) & (k < up_at))
        def _():
            part = lanes((k - down_at) % across)
            set_own(
                k, 3 + (k - down_at) // across, lambda micro, block: dims_dot(block, right[micro, :, part], 1, 0)
            )

        @pl.when((k >= up_at) & (k < qkv_at))
        def _():
            part = lanes(across + k - up_at)
            set_own(k, 1, lambda micro, block: dims_dot(block, right[micro, :, part], 1, 0))

        @pl.when(k >= qkv_at)
        def _():
            part = lanes(k - qkv_at)
            set_own(k, 2, lambda micro, block: dims_dot(block, heads[micro, part, :], 1, 1))

    def out_copy(k, kind):
        if kind == "down":
            target = down_o.at[(k - down_at) // across, :, :, :, lanes((k - down_at) % across)]
        else:
            ref, start = {"out": (out_o, out_at), "up": (up_o, up_at), "qkv": (qkv_o, qkv_at)}[kind]
            target = ref.at[:, :, :, lanes(k - start)]
        return pltpu.make_async_copy(final.at[k], target, out_sems.at[k])

    ranges = {"out": (out_at, down_at), "down": (down_at, up_at), "up": (up_at, qkv_at), "qkv": (qkv_at, pieces)}

    def stored(k, do):
        for kind, (first, end) in ranges.items():

            @pl.when((k >= first) & (k < end))
            def _():
                do(out_copy(k, kind))

    vector_peers = dp_peers + replica_peers

    def vector_copy(i):
        return pltpu.make_async_remote_copy(
            src_ref=vector_sum.at[i],
            dst_ref=from_vector.at[i],
            send_sem=vector_send.at[i],
            recv_sem=vector_recv.at[i],
            device_id=vector_peers[i][0],
            device_id_type=pl.DeviceIdType.MESH,
        )

    lags = [0]
    for stage in range(n_steps):
        lags.append(lags[-1] + (4 if stage == 0 else 2))

    def turn(t, carry):
        for at, group in zip((down_at, up_at, qkv_at), copies[1:]):

            @pl.when(t == at)
            def _():
                for copy in group:
                    copy.wait()

        @pl.when(t < pieces)
        def _():
            compute(t)

        for stage in range(n_steps + 1):
            k = t - lags[stage]

            @pl.when((k >= 0) & (k < pieces))
            def _():
                advance_either(k, stage)
                if stage == n_steps:
                    stored(k, lambda copy: copy.start())

        for i in range(len(vector_peers) + 1):

            @pl.when(t == 4 * i)
            def _():
                if i > 0:
                    vector_copy(i - 1).wait()
                    vector_sum[i] = vector_sum[i - 1] + from_vector[i - 1]
                if i < len(vector_peers):
                    vector_copy(i).start()
                else:
                    pltpu.make_async_copy(vector_sum.at[i], vectors_o, out_sems.at[pieces]).start()

        return carry

    lax.fori_loop(0, pieces + lags[-1], turn, 0)

    def finish(k, carry):
        stored(k, lambda copy: copy.wait())
        return carry

    lax.fori_loop(0, pieces, finish, 0)
    pltpu.make_async_copy(vector_sum.at[len(vector_peers)], vectors_o, out_sems.at[pieces]).wait()


def reduce_call(stash, kept):
    _, attn_in, mlp_in, _, _, _, _, context, hidden, _ = stash
    _, grad_heads, grad_up, grad_out, vectors = kept
    micros, width, rows = attn_in.shape
    hidden_width = hidden.shape[1]
    groups = hidden_width // width
    devices = lax.axis_size("dp")
    bits = devices.bit_length() - 1
    share, quarter = width // devices, width // devices // 4
    piece = PIECE
    pieces = piece_plan(width, hidden_width, piece)[-1]
    loads = 6 + groups + 1
    tall = (micros, devices, share, rows)
    halves = [2] * bits
    steps = bits + 4
    peers = bits + 2
    shape = lambda columns: jax.ShapeDtypeStruct((2, 2, quarter, columns), BF16)
    outs = pl.pallas_call(
        functools.partial(reduce_kernel, bits, piece),
        out_shape=[
            shape(3 * width),
            shape(width),
            shape(hidden_width),
            jax.ShapeDtypeStruct((groups, 2, 2, quarter, width), BF16),
            jax.ShapeDtypeStruct(vectors.shape[1:], F32),
        ],
        in_specs=[ANY] * 8,
        out_specs=[ANY] * 5,
        scratch_shapes=[
            pltpu.VMEM((3 + groups, *tall), BF16),
            pltpu.VMEM((micros, rows, width + hidden_width), BF16),
            pltpu.VMEM(grad_heads.shape, BF16),
            pltpu.VMEM(vectors.shape, F32),
            pltpu.VMEM((pieces, *halves, 2, 2, quarter, piece), BF16),
            pltpu.VMEM((pieces, 2, 2, quarter, piece), BF16),
            pltpu.VMEM((pieces, *halves, 2, quarter, piece), BF16),
            *[pltpu.VMEM((pieces, *halves[bit + 1 :], 2, quarter, piece), BF16) for bit in range(bits)],
            pltpu.VMEM((pieces, quarter, piece), BF16),
            pltpu.VMEM((peers + 1, *vectors.shape[1:]), F32),
            pltpu.VMEM((peers, *vectors.shape[1:]), F32),
            pltpu.SemaphoreType.DMA((loads,)),
            pltpu.SemaphoreType.DMA((pieces, steps)),
            pltpu.SemaphoreType.DMA((pieces, steps)),
            pltpu.SemaphoreType.DMA((peers,)),
            pltpu.SemaphoreType.DMA((peers,)),
            pltpu.SemaphoreType.DMA((pieces + 1,)),
        ],
        compiler_params=pltpu.CompilerParams(
            collective_id=0, has_side_effects=True, vmem_limit_bytes=60 << 20
        ),
        cost_estimate=pl.CostEstimate(
            flops=2 * micros * rows * width * (4 * width + 2 * hidden_width),
            bytes_accessed=30 << 20,
            transcendentals=0,
        ),
        name="weight_gradients",
    )(
        context.reshape(tall),
        hidden.reshape(micros, devices, groups, share, rows),
        mlp_in.reshape(tall),
        attn_in.reshape(tall),
        grad_out,
        grad_up,
        grad_heads,
        vectors,
    )
    qkv, out, up, down, sums = outs
    scattered = [array.reshape(-1, array.shape[-1]) for array in (qkv, out, up, down)]
    return scattered, sums


def shifted(value, axis, by):
    size = lax.axis_size(axis)
    pairs = [(i, i + by) for i in range(size) if 0 <= i + by < size]
    return lax.ppermute(value, axis, pairs)


def rotary_tables(seq_len):
    positions = jnp.arange(seq_len, dtype=F32)
    inverse = 1.0 / ROTARY_BASE ** (jnp.arange(0, ROTARY, 2, dtype=F32) / ROTARY)
    angles = inverse[:, None] * positions[None, :]
    return jnp.cos(angles), jnp.sin(angles)


def summed(share):
    part = lax.psum_scatter(share.astype(BF16), "dp", scatter_dimension=0, tiled=True)
    return lax.psum(part, "replica").astype(F32)


def in_pieces(width):
    devices = lax.axis_size("dp")
    return devices & (devices - 1) == 0 and lax.axis_size("replica") == 4 and width % (64 * devices) == 0


def local_totals(stash, kept):
    _, attn_in, mlp_in, _, _, _, _, context, hidden, _ = stash
    _, grad_heads, grad_up, grad_out, vectors = kept
    vector_sums = jnp.sum(vectors, axis=0)
    groups = hidden.shape[1] // attn_in.shape[1]
    return (
        vector_sums[0],
        vector_sums[1],
        jnp.einsum("mdr,mer->de", attn_in, grad_heads, preferred_element_type=F32),
        vector_sums[4:7].reshape(-1),
        jnp.einsum("mer,mrd->ed", context, grad_out, preferred_element_type=F32),
        vector_sums[7],
        vector_sums[2],
        vector_sums[3],
        jnp.einsum("mdr,mrf->df", mlp_in, grad_up, preferred_element_type=F32),
        vector_sums[8 : 8 + groups].reshape(-1),
        jnp.einsum("mfr,mrd->fd", hidden, grad_out, preferred_element_type=F32),
        vector_sums[7],
    )


def body(tokens, cotangent, lengths, *weights):
    weights = tuple(array if array.ndim == 2 else array[0] for array in weights)
    micros = lengths.shape[0]
    width = tokens.shape[1]
    rows = tokens.shape[0] // micros
    sections = lax.axis_size("section")
    inputs = tokens.reshape(micros, rows, width)
    cotans = cotangent.reshape(micros, rows, width)
    tables = rotary_tables(rows)

    stash, received, passed = None, inputs[0], []
    for moment in range(micros + sections - 1):
        sent, stash = forward_call(moment, lengths, inputs, received, weights, tables, stash)
        if moment < micros:
            received = shifted(sent, "section", 1)
            passed.append(received)

    kept, received = None, cotans[0]
    for moment in range(micros + sections - 1):
        sent, kept = backward_call(
            moment, lengths, cotans, received, inputs, passed, weights, tables, stash, kept
        )
        if moment < micros:
            received = shifted(sent, "section", -1)

    grad_scale = float(tokens.shape[0] * lax.axis_size("dp") * lax.axis_size("replica")) ** (-0.5)
    if in_pieces(width):
        matrices, vectors = reduce_call(stash, kept)
        mine = lax.axis_index("dp")
        devices = lax.axis_size("dp")

        def slice_of(first, count):
            size = count * width // devices
            return lax.dynamic_slice_in_dim(vectors[first : first + count].reshape(-1), mine * size, size)

        down_bias = slice_of(7, 1)
        shares = (
            slice_of(0, 1), slice_of(1, 1), matrices[0], slice_of(4, 3), matrices[1], down_bias, slice_of(2, 1),
            slice_of(3, 1), matrices[2], slice_of(8, weights[8].shape[1] // width), matrices[3], down_bias,
        )
    else:
        shares = tuple(summed(total) for total in local_totals(stash, kept))
    scaled = tuple(share.astype(F32)[None] * grad_scale for share in shares)
    return (stash[0].reshape(1, micros * rows, width), kept[0].reshape(1, micros * rows, width), *scaled)


def solution(mesh):
    rows = P(("dp", "replica"), None)
    vector, matrix = P("section", None), P("section", None, None)
    out_rows = P("section", ("dp", "replica"), None)
    vector_out, matrix_out = P("section", "dp"), P("section", "dp", None)
    return jax.shard_map(
        body,
        mesh=mesh,
        in_specs=(
            rows, rows, P(("dp", "replica")), vector, vector, matrix, vector, matrix, vector, vector, vector, matrix,
            vector, matrix, vector,
        ),
        out_specs=(
            out_rows, out_rows, vector_out, vector_out, matrix_out, vector_out, matrix_out, vector_out, vector_out,
            vector_out, matrix_out, vector_out, matrix_out, vector_out,
        ),
        check_vma=False,
    )
```

```python
import functools

import jax
import jax.numpy as jnp
from jax import lax
from jax.experimental import pallas as pl
from jax.experimental.pallas import tpu as pltpu
from jax.sharding import PartitionSpec as P

HEADS = 12
HEAD_DIM = 64
ROTARY = 16
HALF = ROTARY // 2
EPSILON = 1e-05
ROTARY_BASE = 10000.0
MASKED = -1e30
SCALE = HEAD_DIM**-0.5
F32 = jnp.float32
BF16 = jnp.bfloat16
ANY = pl.BlockSpec(memory_space=pl.ANY)
VMEM = pl.BlockSpec(memory_space=pltpu.VMEM)
SMEM = pl.BlockSpec(memory_space=pltpu.SMEM)
ROW_CHUNK = 128
QKV_TILE = 256
FF_TILE = 512
PIECE = 384


def dims_dot(left, right, left_dim, right_dim):
    return lax.dot_general(
        left, right, (((left_dim,), (right_dim,)), ((), ())), preferred_element_type=F32
    )


def normal_parts(v):
    t = 1.0 / (1.0 + (0.3275911 * 0.7071067811865476) * jnp.abs(v))
    bell = jnp.exp(-0.5 * v * v)
    series = 0.7107068705 + t * (-0.7265760135 + t * 0.5307027145)
    tail = t * (0.127414796 + t * (-0.142248368 + t * series)) * bell
    return jnp.where(v >= 0, 1.0 - tail, tail), bell * 0.3989422804014327


def forward_kernel(micros, *refs):
    (
        lengths, tokens_h, attn_gain, attn_shift, qkv_bias, out_bias, mlp_gain, mlp_shift, up_bias, down_bias,
        cosine, sine, qkv_h, out_h, up_h, down_h,
        y_h, inputs_h, attn_in_h, mlp_in_h, queries_h, keys_h, values_h, probs_h, context_h, hidden_h, slope_h,
        qkv_w, out_w, up_w, down_w, x, attn_in, mlp_in, attn_in_t, mlp_in_t, heads_t, context_t, hidden_t, slope,
        bias, total, probs, y, in_sems, out_sems, probs_sems, send_sems, recv_sems,
    ) = refs
    section = lax.axis_index("section")
    rows, width = attn_in.shape
    hidden_width = up_w.shape[1]
    half = rows // 2
    other = {"section": 1 - section}

    barrier = pltpu.get_barrier_semaphore()
    pl.semaphore_signal(barrier, inc=1, device_id=other, device_id_type=pl.DeviceIdType.MESH)
    loads = [
        pltpu.make_async_copy(src, dst, in_sems.at[i])
        for i, (src, dst) in enumerate(
            ((tokens_h, x), (qkv_h, qkv_w), (out_h, out_w), (up_h, up_w), (down_h, down_w))
        )
    ]

    @pl.when(section == 0)
    def _():
        loads[0].start()

    loads[1].start()
    probs[:, half:, :half] = jnp.zeros((probs.shape[0], half, half), BF16)
    cos_rows, sin_rows = cosine[...], sine[...]

    def hand_over(micro):
        return pltpu.make_async_remote_copy(
            src_ref=y.at[micro],
            dst_ref=x.at[micro],
            send_sem=send_sems.at[micro],
            recv_sem=recv_sems.at[micro],
            device_id=other,
            device_id_type=pl.DeviceIdType.MESH,
        )

    def stores(micro):
        pairs = [
            (x.at[micro], inputs_h.at[micro]),
            (attn_in_t, attn_in_h.at[micro]),
            (mlp_in_t, mlp_in_h.at[micro]),
            (heads_t.at[0:width], queries_h.at[micro]),
            (heads_t.at[width : 2 * width], keys_h.at[micro]),
            (heads_t.at[2 * width :], values_h.at[micro]),
            (context_t, context_h.at[micro]),
            (y.at[micro], y_h.at[micro]),
        ]
        for start in range(0, hidden_width, FF_TILE):
            part = slice(start, start + FF_TILE)
            pairs.append((hidden_t.at[part], hidden_h.at[micro, part]))
            pairs.append((slope.at[:, part], slope_h.at[micro, :, part]))
        return [pltpu.make_async_copy(src, dst, out_sems.at[i]) for i, (src, dst) in enumerate(pairs)]

    pl.semaphore_wait(barrier, 1)

    def sentence(micro, carry):
        store = stores(micro)

        @pl.when((section == 0) & (micro == 0))
        def _():
            loads[0].wait()

        @pl.when(section == 1)
        def _():
            hand_over(micro).wait_recv()

        store[0].start()
        length = lengths[micro]
        key_ids = lax.broadcasted_iota(jnp.int32, (rows, rows), 0)
        query_ids = lax.broadcasted_iota(jnp.int32, (rows, rows), 1)
        bias[...] = jnp.where((key_ids <= query_ids) & (key_ids < length), 0.0, MASKED)

        @pl.when(micro > 0)
        def _():
            for copy in stores(micro - 1):
                copy.wait()

        for start in range(0, rows, ROW_CHUNK):
            part = slice(start, start + ROW_CHUNK)
            block = x[micro, part, :].astype(F32)
            centred = block - jnp.mean(block, axis=-1, keepdims=True)
            unit = centred * lax.rsqrt(jnp.mean(centred * centred, axis=-1, keepdims=True) + EPSILON)
            attn = (unit * attn_gain[...].astype(F32) + attn_shift[...].astype(F32)).astype(BF16)
            mlp = (unit * mlp_gain[...].astype(F32) + mlp_shift[...].astype(F32)).astype(BF16)
            attn_in[part, :] = attn
            mlp_in[part, :] = mlp
            attn_in_t[:, part] = attn.T
            mlp_in_t[:, part] = mlp.T
        store[1].start()
        store[2].start()

        @pl.when(micro == 0)
        def _():
            loads[1].wait()
            for load in loads[2:]:
                load.start()

        for start in range(0, 3 * width, QKV_TILE):
            part = slice(start, start + QKV_TILE)
            projected = jnp.dot(attn_in[...], qkv_w[:, part], preferred_element_type=F32)
            turned = (projected + qkv_bias[:, part].astype(F32)).T
            if start >= 2 * width:
                heads_t[part, :] = turned.astype(BF16)
                continue
            for at in range(0, QKV_TILE, HEAD_DIM):
                low, high = turned[at : at + HALF], turned[at + HALF : at + ROTARY]
                heads_t[start + at : start + at + HEAD_DIM, :] = jnp.concatenate(
                    [
                        low * cos_rows - high * sin_rows,
                        high * cos_rows + low * sin_rows,
                        turned[at + ROTARY : at + HEAD_DIM],
                    ],
                    axis=0,
                ).astype(BF16)
        for copy in store[3:6]:
            copy.start()

        def softmax(scores):
            raised = jnp.exp(scores - jnp.max(scores, axis=0, keepdims=True))
            return (raised * (1.0 / jnp.sum(raised, axis=0, keepdims=True))).astype(BF16)

        def attend(head, slot):
            at = pl.multiple_of(head * HEAD_DIM, HEAD_DIM)
            query = heads_t[pl.ds(at, HEAD_DIM), :] * jnp.bfloat16(SCALE)
            key = heads_t[pl.ds(width + at, HEAD_DIM), :]
            value = heads_t[pl.ds(2 * width + at, HEAD_DIM), :]
            early = softmax(dims_dot(key[:, :half], query[:, :half], 0, 0) + bias[:half, :half])
            late = softmax(dims_dot(key, query[:, half:], 0, 0) + bias[:, half:])
            probs[slot, :half, :half] = early
            probs[slot, :, half:] = late
            place = pl.ds(at, HEAD_DIM)
            context_t[place, :half] = jnp.dot(value[:, :half], early, preferred_element_type=F32).astype(BF16)
            context_t[place, half:] = jnp.dot(value, late, preferred_element_type=F32).astype(BF16)

        def probs_copy(head, slot):
            return pltpu.make_async_copy(probs.at[slot], probs_h.at[micro, head], probs_sems.at[slot])

        def attend_pair(pair, carry):
            first_slot = 2 * lax.rem(pair, 2)

            @pl.when(pair >= 2)
            def _():
                for own_head in range(2):
                    probs_copy(2 * pair + own_head - 4, first_slot + own_head).wait()

            for own_head in range(2):
                attend(2 * pair + own_head, first_slot + own_head)
            for own_head in range(2):
                probs_copy(2 * pair + own_head, first_slot + own_head).start()
            return carry

        lax.fori_loop(0, HEADS // 2, attend_pair, 0)
        store[6].start()

        @pl.when(micro == 0)
        def _():
            for load in loads[2:]:
                load.wait()

        total[...] = (
            dims_dot(context_t[...], out_w[...], 0, 0)
            + x[micro].astype(F32)
            + (out_bias[...].astype(F32) + down_bias[...].astype(F32))
        )
        for start in range(0, hidden_width, FF_TILE):
            part = slice(start, start + FF_TILE)
            up = jnp.dot(mlp_in[...], up_w[:, part], preferred_element_type=F32)
            up = up + up_bias[:, part].astype(F32)
            share, density = normal_parts(up)
            hidden = (up * share).astype(BF16)
            slope[:, part] = (share + up * density).astype(BF16)
            hidden_t[part, :] = hidden.T
            tile = start // FF_TILE
            store[8 + 2 * tile].start()
            store[9 + 2 * tile].start()
            total[...] += jnp.dot(hidden, down_w[part, :], preferred_element_type=F32)
        y[micro] = total[...].astype(BF16)

        @pl.when(section == 0)
        def _():
            hand_over(micro).start()

        store[7].start()
        for head in range(HEADS - 4, HEADS):
            probs_copy(head, head % 4).wait()
        return carry

    lax.fori_loop(0, micros, sentence, 0)
    for copy in stores(micros - 1):
        copy.wait()

    @pl.when(section == 0)
    def _():
        for micro in range(micros):
            hand_over(micro).wait_send()


def forward_call(lengths, tokens, weights, tables):
    (
        attn_gain, attn_shift, qkv_weight, qkv_bias, out_weight, out_bias, mlp_gain, mlp_shift, up_weight, up_bias,
        down_weight, down_bias,
    ) = weights
    micros, rows, width = tokens.shape
    hidden_width = up_weight.shape[1]
    wide, tall = (micros, rows, width), (micros, width, rows)
    shapes = [
        wide, wide, tall, tall, tall, tall, tall, (micros, HEADS, rows, rows), tall, (micros, hidden_width, rows),
        (micros, rows, hidden_width),
    ]
    buffers = [
        qkv_weight.shape, out_weight.shape, up_weight.shape, down_weight.shape, wide, (rows, width), (rows, width),
        (width, rows), (width, rows), (3 * width, rows), (width, rows), (hidden_width, rows), (rows, hidden_width),
    ]
    return pl.pallas_call(
        functools.partial(forward_kernel, micros),
        out_shape=[jax.ShapeDtypeStruct(shape, BF16) for shape in shapes],
        in_specs=[SMEM, ANY] + [VMEM] * 10 + [ANY] * 4,
        out_specs=[ANY] * len(shapes),
        scratch_shapes=[pltpu.VMEM(shape, BF16) for shape in buffers]
        + [
            pltpu.VMEM((rows, rows), F32),
            pltpu.VMEM((rows, width), F32),
            pltpu.VMEM((4, rows, rows), BF16),
            pltpu.VMEM(wide, BF16),
            pltpu.SemaphoreType.DMA((5,)),
            pltpu.SemaphoreType.DMA((8 + 2 * (hidden_width // FF_TILE),)),
            pltpu.SemaphoreType.DMA((4,)),
            pltpu.SemaphoreType.DMA((micros,)),
            pltpu.SemaphoreType.DMA((micros,)),
        ],
        compiler_params=pltpu.CompilerParams(collective_id=1, has_side_effects=True, vmem_limit_bytes=58 << 20),
        cost_estimate=pl.CostEstimate(
            flops=micros * (2 * rows * width * (4 * width + 2 * hidden_width) + 4 * rows * rows * width),
            bytes_accessed=80 << 20,
            transcendentals=micros * rows * hidden_width,
        ),
        name="layer_forward",
    )(
        lengths, tokens, attn_gain, attn_shift, qkv_bias, out_bias, mlp_gain, mlp_shift, up_bias, down_bias,
        *tables, qkv_weight, out_weight, up_weight, down_weight,
    )


def backward_kernel(micros, *refs):
    (
        lengths, cotangent_h, inputs_h, attn_gain, mlp_gain, cosine, sine, qkv_h, out_h, up_h, down_h,
        queries_h, keys_h, values_h, probs_h, context_h, slope_h,
        grad_in_h, grad_heads_h, grad_up_h, grad_out_h, vectors_h,
        qkv_w, out_w, up_w, down_w, queries, keys, values, context, slope, probs, grad_out, x, grad_context,
        grad_up, grad_heads, grad_low, grad_mlp, grad_in, column_sums, vectors,
        in_sems, stash_sems, out_sems, probs_sems, send_sems, recv_sems,
    ) = refs
    section = lax.axis_index("section")
    rows, width = x.shape
    hidden_width = up_w.shape[1]
    half = rows // 2
    other = {"section": 1 - section}

    barrier = pltpu.get_barrier_semaphore()
    pl.semaphore_signal(barrier, inc=1, device_id=other, device_id_type=pl.DeviceIdType.MESH)
    loads = [
        pltpu.make_async_copy(src, dst, in_sems.at[i])
        for i, (src, dst) in enumerate(
            ((cotangent_h, grad_out), (out_h, out_w), (down_h, down_w), (up_h, up_w), (qkv_h, qkv_w))
        )
    ]

    def stash_loads(micro):
        pairs = (
            (slope_h, slope), (values_h, values), (context_h, context), (queries_h, queries), (keys_h, keys),
            (inputs_h, x),
        )
        return [
            pltpu.make_async_copy(src.at[micro], dst, stash_sems.at[i]) for i, (src, dst) in enumerate(pairs)
        ]

    @pl.when(section == 1)
    def _():
        loads[0].start()

    for load in loads[1:3]:
        load.start()
    stash_loads(0)[0].start()
    loads[3].start()
    for load in stash_loads(0)[1:]:
        load.start()
    loads[4].start()
    cos_rows, sin_rows = cosine[...], sine[...]
    attn_column = jnp.broadcast_to(attn_gain[...].astype(F32), (8, width)).T[:, 0:1]
    mlp_column = jnp.broadcast_to(mlp_gain[...].astype(F32), (8, width)).T[:, 0:1]

    def hand_over(micro):
        return pltpu.make_async_remote_copy(
            src_ref=grad_low.at[micro],
            dst_ref=grad_out.at[micro],
            send_sem=send_sems.at[micro],
            recv_sem=recv_sems.at[micro],
            device_id=other,
            device_id_type=pl.DeviceIdType.MESH,
        )

    def stores(micro):
        pairs = [
            (grad_out.at[micro], grad_out_h.at[micro]),
            (grad_heads, grad_heads_h.at[micro]),
            (grad_in, grad_in_h.at[micro]),
            (vectors, vectors_h.at[micro]),
        ]
        for start in range(0, hidden_width, FF_TILE):
            part = slice(start, start + FF_TILE)
            pairs.append((grad_up.at[:, part], grad_up_h.at[micro, :, part]))
        return [pltpu.make_async_copy(src, dst, out_sems.at[i]) for i, (src, dst) in enumerate(pairs)]

    pl.semaphore_wait(barrier, 1)

    def sentence(micro, carry):
        store = stores(micro)
        stash = stash_loads(micro)
        upcoming = stash_loads(micro + 1)

        def probs_copy(head, slot):
            return pltpu.make_async_copy(probs_h.at[micro, head], probs.at[slot], probs_sems.at[slot])

        for head in range(2):
            probs_copy(head, head).start()

        @pl.when((section == 1) & (micro == 0))
        def _():
            loads[0].wait()

        @pl.when(section == 0)
        def _():
            hand_over(micro).wait_recv()

        row_ids = lax.broadcasted_iota(jnp.int32, (rows, 1), 0)
        grad_wide = jnp.where(row_ids < lengths[micro], grad_out[micro].astype(F32), 0.0)
        grad_out[micro] = grad_wide.astype(BF16)

        @pl.when(micro > 0)
        def _():
            for copy in stores(micro - 1):
                copy.wait()

        vectors[...] = jnp.zeros_like(vectors)
        vectors[7:8, :] = jnp.sum(grad_wide, axis=0, keepdims=True)
        store[0].start()

        @pl.when(micro == 0)
        def _():
            loads[1].wait()

        grad_context[...] = dims_dot(out_w[...], grad_out[micro], 1, 1).astype(BF16)

        @pl.when(micro == 0)
        def _():
            loads[2].wait()
            loads[3].wait()

        stash[0].wait()
        for start in range(0, hidden_width, FF_TILE):
            part = slice(start, start + FF_TILE)
            grad_hidden = dims_dot(grad_out[micro], down_w[part, :], 1, 1)
            grad_pre = (grad_hidden * slope[:, part].astype(F32)).astype(BF16)
            grad_up[:, part] = grad_pre
            store[4 + start // FF_TILE].start()
            sums = jnp.sum(grad_pre.astype(F32), axis=0, keepdims=True)
            for at in range(0, FF_TILE, 128):
                row, column = divmod(start + at, width)
                vectors[8 + row : 9 + row, column : column + 128] = sums[:, at : at + 128]
            back = dims_dot(up_w[:, part], grad_pre, 1, 1)
            if start == 0:
                grad_mlp[...] = back
            else:
                grad_mlp[...] += back

        @pl.when(micro < micros - 1)
        def _():
            upcoming[0].start()

        for load in stash[1:5]:
            load.wait()

        def turn_back(grad):
            low, high = grad[:HALF], grad[HALF:ROTARY]
            return jnp.concatenate(
                [low * cos_rows + high * sin_rows, high * cos_rows - low * sin_rows, grad[ROTARY:]], axis=0
            )

        def over_queries(left, early, late):
            both = dims_dot(left[:, half:], late, 1, 1)
            return jnp.concatenate([both[:, :half] + dims_dot(left[:, :half], early, 1, 1), both[:, half:]], axis=1)

        def attend(head, slot):
            at = pl.multiple_of(head * HEAD_DIM, HEAD_DIM)
            place = pl.ds(at, HEAD_DIM)
            query, key, value, grad = queries[place, :], keys[place, :], values[place, :], grad_context[place, :]
            inner = jnp.sum(grad.astype(F32) * context[place, :].astype(F32), axis=0, keepdims=True)
            early, late = probs[slot, :half, :half], probs[slot, :, half:]
            grad_early = dims_dot(value[:, :half], grad[:, :half], 0, 0) - inner[:, :half]
            grad_late = dims_dot(value, grad[:, half:], 0, 0) - inner[:, half:]
            grad_early = (early.astype(F32) * grad_early).astype(BF16)
            grad_late = (late.astype(F32) * grad_late).astype(BF16)
            grad_value = over_queries(grad, early, late)
            grad_key = over_queries(query, grad_early, grad_late)
            grad_query = jnp.concatenate(
                [
                    jnp.dot(key[:, :half], grad_early, preferred_element_type=F32),
                    jnp.dot(key, grad_late, preferred_element_type=F32),
                ],
                axis=1,
            )
            grad_heads[place, :] = turn_back(grad_query * SCALE).astype(BF16)
            grad_heads[pl.ds(width + at, HEAD_DIM), :] = turn_back(grad_key * SCALE).astype(BF16)
            grad_heads[pl.ds(2 * width + at, HEAD_DIM), :] = grad_value.astype(BF16)

        def attend_pair(pair, carry):
            first_slot = 2 * lax.rem(pair, 2)

            @pl.when(pair < HEADS // 2 - 1)
            def _():
                for own_head in range(2):
                    probs_copy(2 * pair + 2 + own_head, 2 - first_slot + own_head).start()

            for own_head in range(2):
                probs_copy(2 * pair + own_head, first_slot + own_head).wait()
            for own_head in range(2):
                attend(2 * pair + own_head, first_slot + own_head)
            return carry

        lax.fori_loop(0, HEADS // 2, attend_pair, 0)
        store[1].start()

        @pl.when(micro < micros - 1)
        def _():
            for load in upcoming[1:5]:
                load.start()

        @pl.when(micro == 0)
        def _():
            loads[4].wait()

        stash[5].wait()
        column_sums[...] = jnp.zeros_like(column_sums)

        def norm_chunk(index, carry):
            part = pl.ds(pl.multiple_of(index * ROW_CHUNK, ROW_CHUNK), ROW_CHUNK)
            grad_attn_in = jnp.dot(qkv_w[...], grad_heads[:, part], preferred_element_type=F32)
            grad_mlp_in = grad_mlp[:, part]
            turned = x[part, :].astype(F32).T
            centred = turned - jnp.mean(turned, axis=0, keepdims=True)
            inv_spread = lax.rsqrt(jnp.mean(centred * centred, axis=0, keepdims=True) + EPSILON)
            unit = centred * inv_spread
            grad_unit = grad_attn_in * attn_column + grad_mlp_in * mlp_column
            through = inv_spread * (
                grad_unit
                - jnp.mean(grad_unit, axis=0, keepdims=True)
                - unit * jnp.mean(grad_unit * unit, axis=0, keepdims=True)
            )
            exact = through.T + grad_out[micro, part, :].astype(F32)
            low = exact.astype(BF16)
            grad_low[micro, part, :] = low
            grad_in[part, :] = jnp.where(section == 0, exact, low.astype(F32))
            column_sums[0] += grad_attn_in * unit
            column_sums[1] += grad_attn_in
            column_sums[2] += grad_mlp_in * unit
            column_sums[3] += grad_mlp_in
            return carry

        lax.fori_loop(0, rows // ROW_CHUNK, norm_chunk, 0)

        @pl.when(section == 1)
        def _():
            hand_over(micro).start()

        @pl.when(micro < micros - 1)
        def _():
            upcoming[5].start()

        store[2].start()
        columns = [jnp.sum(column_sums[i], axis=1, keepdims=True) for i in range(4)]
        for start in range(0, 3 * width, width):
            columns.append(jnp.sum(grad_heads[start : start + width, :].astype(F32), axis=1, keepdims=True))
        lanes = lax.broadcasted_iota(jnp.int32, (width, 128), 1)
        gathered = jnp.zeros((width, 128), F32)
        for lane, column in enumerate(columns):
            gathered = jnp.where(lanes == lane, column, gathered)
        vectors[0:7, :] = gathered.T[0:7, :]
        store[3].start()
        return carry

    lax.fori_loop(0, micros, sentence, 0)
    for copy in stores(micros - 1):
        copy.wait()

    @pl.when(section == 1)
    def _():
        for micro in range(micros):
            hand_over(micro).wait_send()


def backward_call(lengths, cotangent, weights, tables, stash):
    attn_gain, _, qkv_weight, _, out_weight, _, mlp_gain, _, up_weight, _, down_weight, _ = weights
    _, inputs, _, _, queries, keys, values, probs, context, _, slope = stash
    micros, rows, width = cotangent.shape
    hidden_width = up_weight.shape[1]
    vector_rows = 16
    wide, tall = (micros, rows, width), (width, rows)
    outs = [
        jax.ShapeDtypeStruct(wide, F32),
        jax.ShapeDtypeStruct((micros, 3 * width, rows), BF16),
        jax.ShapeDtypeStruct((micros, rows, hidden_width), BF16),
        jax.ShapeDtypeStruct(wide, BF16),
        jax.ShapeDtypeStruct((micros, vector_rows, width), F32),
    ]
    return pl.pallas_call(
        functools.partial(backward_kernel, micros),
        out_shape=outs,
        in_specs=[SMEM] + [ANY] * 2 + [VMEM] * 4 + [ANY] * 10,
        out_specs=[ANY] * len(outs),
        scratch_shapes=[
            pltpu.VMEM(qkv_weight.shape, BF16),
            pltpu.VMEM(out_weight.shape, BF16),
            pltpu.VMEM(up_weight.shape, BF16),
            pltpu.VMEM(down_weight.shape, BF16),
            pltpu.VMEM(tall, BF16),
            pltpu.VMEM(tall, BF16),
            pltpu.VMEM(tall, BF16),
            pltpu.VMEM(tall, BF16),
            pltpu.VMEM((rows, hidden_width), BF16),
            pltpu.VMEM((4, rows, rows), BF16),
            pltpu.VMEM(wide, BF16),
            pltpu.VMEM((rows, width), BF16),
            pltpu.VMEM(tall, BF16),
            pltpu.VMEM((rows, hidden_width), BF16),
            pltpu.VMEM((3 * width, rows), BF16),
            pltpu.VMEM(wide, BF16),
            pltpu.VMEM(tall, F32),
            pltpu.VMEM((rows, width), F32),
            pltpu.VMEM((4, width, 128), F32),
            pltpu.VMEM((vector_rows, width), F32),
            pltpu.SemaphoreType.DMA((5,)),
            pltpu.SemaphoreType.DMA((6,)),
            pltpu.SemaphoreType.DMA((4 + hidden_width // FF_TILE,)),
            pltpu.SemaphoreType.DMA((4,)),
            pltpu.SemaphoreType.DMA((micros,)),
            pltpu.SemaphoreType.DMA((micros,)),
        ],
        compiler_params=pltpu.CompilerParams(collective_id=2, has_side_effects=True, vmem_limit_bytes=58 << 20),
        cost_estimate=pl.CostEstimate(
            flops=micros * (2 * rows * width * (4 * width + 2 * hidden_width) + 8 * rows * rows * width),
            bytes_accessed=80 << 20,
            transcendentals=0,
        ),
        name="layer_backward",
    )(
        lengths, cotangent, inputs, attn_gain, mlp_gain, *tables, qkv_weight, out_weight, up_weight, down_weight,
        queries, keys, values, probs, context, slope,
    )


def partner(axis, bit):
    index = lax.axis_index(axis)
    own_bit = (index // bit) % 2
    return {axis: index + bit - 2 * bit * own_bit}, own_bit


def piece_plan(width, hidden_width, piece):
    counts = [width // piece, hidden_width // piece, hidden_width // piece, 3 * width // piece]
    starts = [0]
    for count in counts:
        starts.append(starts[-1] + count)
    return starts


def reduce_kernel(bits, piece, *refs):
    (
        context_h, hidden_h, mlp_in_h, attn_in_h, grad_out_h, grad_up_h, grad_heads_h, vectors_h,
        qkv_o, out_o, up_o, down_o, vectors_o,
        left, right, heads, vectors, own, final, from_first, *rest,
    ) = refs
    from_dp, rest = rest[:bits], rest[bits:]
    (
        from_second, vector_sum, from_vector,
        in_sems, send_sems, recv_sems, vector_send, vector_recv, out_sems,
    ) = rest
    micros, devices, share, rows = attn_in_h.shape
    width = devices * share
    hidden_width = grad_up_h.shape[2]
    groups = hidden_width // width
    out_at, down_at, up_at, qkv_at, pieces = piece_plan(width, hidden_width, piece)
    across = width // piece

    barrier = pltpu.get_barrier_semaphore()
    dp_peers = [partner("dp", 1 << bit) for bit in range(bits)]
    replica_peers = [partner("replica", 1), partner("replica", 2)]
    for device, _ in dp_peers + replica_peers:
        pl.semaphore_signal(barrier, inc=1, device_id=device, device_id_type=pl.DeviceIdType.MESH)

    wide = hidden_width + width
    loads = [
        [(context_h, left.at[0]), (grad_out_h, right.at[:, :, 0:width]), (vectors_h, vectors)],
        [(hidden_h.at[:, :, group], left.at[3 + group]) for group in range(groups)],
        [(mlp_in_h, left.at[1]), (grad_up_h, right.at[:, :, width:wide])],
        [(attn_in_h, left.at[2]), (grad_heads_h, heads)],
    ]
    copies, count = [], 0
    for group in loads:
        copies.append([])
        for src, dst in group:
            copies[-1].append(pltpu.make_async_copy(src, dst, in_sems.at[count]))
            count += 1
    for copy in copies[0]:
        copy.start()
    for copy in copies[0]:
        copy.wait()
    for group in copies[1:]:
        for copy in group:
            copy.start()
    vector_sum[0] = jnp.sum(vectors[...], axis=0)
    pl.semaphore_wait(barrier, len(dp_peers) + len(replica_peers))

    dp_bits = [own_bit for _, own_bit in dp_peers]

    def keep(k, depth, first_bit=None, second_bit=None, flip=None):
        index = [k] + [slice(None)] * (bits - depth)
        for bit in reversed(range(depth)):
            index.append(1 - dp_bits[bit] if flip == bit else dp_bits[bit])
        if first_bit is not None:
            index.append(first_bit)
        if second_bit is not None:
            index.append(second_bit)
        return tuple(index)

    def transfers(k, turned):
        (first, first_bit), (second, second_bit) = replica_peers[::-1] if turned else replica_peers
        steps = [
            (own.at[keep(k, 0, 1 - first_bit)], from_first.at[k], first, own.at[keep(k, 0, first_bit)]),
        ]
        for bit in range(bits):
            steps.append(
                (
                    own.at[keep(k, bit + 1, first_bit, flip=bit)],
                    from_dp[bit].at[k],
                    dp_peers[bit][0],
                    own.at[keep(k, bit + 1, first_bit)],
                )
            )
        mine = final.at[k, first_bit, second_bit]
        steps.append(
            (
                own.at[keep(k, bits, first_bit, 1 - second_bit)],
                from_second.at[k],
                second,
                own.at[keep(k, bits, first_bit, second_bit)],
            )
        )
        steps.append((mine, mine, second, None))
        steps.append((final.at[k, first_bit], final.at[k, first_bit], first, None))
        return steps, mine

    def copy_of(k, stage, step):
        src, dst, device, _ = step
        return pltpu.make_async_remote_copy(
            src_ref=src,
            dst_ref=dst,
            send_sem=send_sems.at[k, stage],
            recv_sem=recv_sems.at[k, stage],
            device_id=device,
            device_id_type=pl.DeviceIdType.MESH,
        )

    n_steps = bits + 4

    def advance(k, stage, turned):
        steps, mine = transfers(k, turned)
        if stage > 0:
            step = steps[stage - 1]
            copy_of(k, stage - 1, step).wait()
            if step[3] is not None:
                total = step[3][...].astype(F32) + step[1][...].astype(F32)
                if stage == bits + 2:
                    mine[...] = total.astype(BF16)
                else:
                    step[3][...] = total.astype(BF16)
        if stage < n_steps:
            copy_of(k, stage, steps[stage]).start()

    def advance_either(k, stage):
        for turned in (False, True):

            @pl.when(k % 2 == int(turned))
            def _():
                advance(k, stage, turned)

    shape = own.shape[1:]

    def panel(index, micro):
        return left[index, micro].reshape(width, rows)

    def set_own(k, index, columns):
        value = columns(0, panel(index, 0))
        for micro in range(1, micros):
            value = value + columns(micro, panel(index, micro))
        own[k] = value.astype(BF16).reshape(shape)

    def lanes(index):
        return pl.ds(pl.multiple_of(index * piece, 128), piece)

    def compute(k):
        @pl.when(k < down_at)
        def _():
            part = lanes(k)
            set_own(k, 0, lambda micro, block: dims_dot(block, right[micro, :, part], 1, 0))

        @pl.when((k >= down_at) & (k < up_at))
        def _():
            part = lanes((k - down_at) % across)
            set_own(
                k, 3 + (k - down_at) // across, lambda micro, block: dims_dot(block, right[micro, :, part], 1, 0)
            )

        @pl.when((k >= up_at) & (k < qkv_at))
        def _():
            part = lanes(across + k - up_at)
            set_own(k, 1, lambda micro, block: dims_dot(block, right[micro, :, part], 1, 0))

        @pl.when(k >= qkv_at)
        def _():
            part = lanes(k - qkv_at)
            set_own(k, 2, lambda micro, block: dims_dot(block, heads[micro, part, :], 1, 1))

    def out_copy(k, kind):
        if kind == "down":
            target = down_o.at[(k - down_at) // across, :, :, :, lanes((k - down_at) % across)]
        else:
            ref, start = {"out": (out_o, out_at), "up": (up_o, up_at), "qkv": (qkv_o, qkv_at)}[kind]
            target = ref.at[:, :, :, lanes(k - start)]
        return pltpu.make_async_copy(final.at[k], target, out_sems.at[k])

    ranges = {"out": (out_at, down_at), "down": (down_at, up_at), "up": (up_at, qkv_at), "qkv": (qkv_at, pieces)}

    def stored(k, do):
        for kind, (first, end) in ranges.items():

            @pl.when((k >= first) & (k < end))
            def _():
                do(out_copy(k, kind))

    vector_peers = dp_peers + replica_peers

    def vector_copy(i):
        return pltpu.make_async_remote_copy(
            src_ref=vector_sum.at[i],
            dst_ref=from_vector.at[i],
            send_sem=vector_send.at[i],
            recv_sem=vector_recv.at[i],
            device_id=vector_peers[i][0],
            device_id_type=pl.DeviceIdType.MESH,
        )

    lags = [0]
    for stage in range(n_steps):
        lags.append(lags[-1] + (4 if stage == 0 else 2))

    def turn(t, carry):
        for at, group in zip((down_at, up_at, qkv_at), copies[1:]):

            @pl.when(t == at)
            def _():
                for copy in group:
                    copy.wait()

        @pl.when(t < pieces)
        def _():
            compute(t)

        for stage in range(n_steps + 1):
            k = t - lags[stage]

            @pl.when((k >= 0) & (k < pieces))
            def _():
                advance_either(k, stage)
                if stage == n_steps:
                    stored(k, lambda copy: copy.start())

        for i in range(len(vector_peers) + 1):

            @pl.when(t == 4 * i)
            def _():
                if i > 0:
                    vector_copy(i - 1).wait()
                    vector_sum[i] = vector_sum[i - 1] + from_vector[i - 1]
                if i < len(vector_peers):
                    vector_copy(i).start()
                else:
                    pltpu.make_async_copy(vector_sum.at[i], vectors_o, out_sems.at[pieces]).start()

        return carry

    lax.fori_loop(0, pieces + lags[-1], turn, 0)

    def finish(k, carry):
        stored(k, lambda copy: copy.wait())
        return carry

    lax.fori_loop(0, pieces, finish, 0)
    pltpu.make_async_copy(vector_sum.at[len(vector_peers)], vectors_o, out_sems.at[pieces]).wait()


def reduce_call(stash, kept):
    _, _, attn_in, mlp_in, _, _, _, _, context, hidden, _ = stash
    _, grad_heads, grad_up, grad_out, vectors = kept
    micros, width, rows = attn_in.shape
    hidden_width = hidden.shape[1]
    groups = hidden_width // width
    devices = lax.axis_size("dp")
    bits = devices.bit_length() - 1
    share, quarter = width // devices, width // devices // 4
    piece = PIECE
    pieces = piece_plan(width, hidden_width, piece)[-1]
    loads = 6 + groups + 1
    tall = (micros, devices, share, rows)
    halves = [2] * bits
    steps = bits + 4
    peers = bits + 2
    shape = lambda columns: jax.ShapeDtypeStruct((2, 2, quarter, columns), BF16)
    outs = pl.pallas_call(
        functools.partial(reduce_kernel, bits, piece),
        out_shape=[
            shape(3 * width),
            shape(width),
            shape(hidden_width),
            jax.ShapeDtypeStruct((groups, 2, 2, quarter, width), BF16),
            jax.ShapeDtypeStruct(vectors.shape[1:], F32),
        ],
        in_specs=[ANY] * 8,
        out_specs=[ANY] * 5,
        scratch_shapes=[
            pltpu.VMEM((3 + groups, *tall), BF16),
            pltpu.VMEM((micros, rows, width + hidden_width), BF16),
            pltpu.VMEM(grad_heads.shape, BF16),
            pltpu.VMEM(vectors.shape, F32),
            pltpu.VMEM((pieces, *halves, 2, 2, quarter, piece), BF16),
            pltpu.VMEM((pieces, 2, 2, quarter, piece), BF16),
            pltpu.VMEM((pieces, *halves, 2, quarter, piece), BF16),
            *[pltpu.VMEM((pieces, *halves[bit + 1 :], 2, quarter, piece), BF16) for bit in range(bits)],
            pltpu.VMEM((pieces, quarter, piece), BF16),
            pltpu.VMEM((peers + 1, *vectors.shape[1:]), F32),
            pltpu.VMEM((peers, *vectors.shape[1:]), F32),
            pltpu.SemaphoreType.DMA((loads,)),
            pltpu.SemaphoreType.DMA((pieces, steps)),
            pltpu.SemaphoreType.DMA((pieces, steps)),
            pltpu.SemaphoreType.DMA((peers,)),
            pltpu.SemaphoreType.DMA((peers,)),
            pltpu.SemaphoreType.DMA((pieces + 1,)),
        ],
        compiler_params=pltpu.CompilerParams(
            collective_id=0, has_side_effects=True, vmem_limit_bytes=60 << 20
        ),
        cost_estimate=pl.CostEstimate(
            flops=2 * micros * rows * width * (4 * width + 2 * hidden_width),
            bytes_accessed=30 << 20,
            transcendentals=0,
        ),
        name="weight_gradients",
    )(
        context.reshape(tall),
        hidden.reshape(micros, devices, groups, share, rows),
        mlp_in.reshape(tall),
        attn_in.reshape(tall),
        grad_out,
        grad_up,
        grad_heads,
        vectors,
    )
    qkv, out, up, down, sums = outs
    scattered = [array.reshape(-1, array.shape[-1]) for array in (qkv, out, up, down)]
    return scattered, sums


def finish_kernel(grad_scale, *refs):
    vectors = refs[0]
    sources = refs[1:7]
    targets = refs[7:13]
    vector_outs = refs[13:21]
    held, wide = refs[21:27], refs[27:31]
    in_sems, out_sems = refs[31:]
    ready = (*held[:2], *wide)
    loads = [pltpu.make_async_copy(src, dst, in_sems.at[i]) for i, (src, dst) in enumerate(zip(sources, held))]
    stores = [pltpu.make_async_copy(src, dst, out_sems.at[i]) for i, (src, dst) in enumerate(zip(ready, targets))]
    for load in loads:
        load.start()
    devices = lax.axis_size("dp")
    mine = lax.axis_index("dp")
    width = vectors.shape[1]
    first_rows = (0, 1, 4, 7, 2, 3, 8, 7)
    for device in range(devices):

        @pl.when(mine == device)
        def _():
            for out, first in zip(vector_outs, first_rows):
                at, size, filled = device * out.shape[1], out.shape[1], 0
                while filled < size:
                    row, column = divmod(at + filled, width)
                    count = min(size - filled, width - column)
                    piece = vectors[first + row : first + row + 1, column : column + count]
                    out[:, filled : filled + count] = piece * grad_scale
                    filled += count

    for i, (load, store) in enumerate(zip(loads, stores)):
        load.wait()
        if i >= 2:
            wide[i - 2][...] = held[i][...].astype(F32) * grad_scale
        store.start()
    for store in stores:
        store.wait()


def finish_call(grad_scale, shares, vectors, outputs, grad_in, hidden_width):
    width = vectors.shape[1]
    devices = lax.axis_size("dp")
    sizes = [width, width, 3 * width, width, width, width, hidden_width, width]
    matrices = [jax.ShapeDtypeStruct(share.shape, F32) for share in shares]
    results = pl.pallas_call(
        functools.partial(finish_kernel, grad_scale),
        out_shape=[
            jax.ShapeDtypeStruct(outputs.shape, BF16),
            jax.ShapeDtypeStruct(grad_in.shape, F32),
            *matrices,
            *[jax.ShapeDtypeStruct((1, size // devices), F32) for size in sizes],
        ],
        in_specs=[VMEM] + [ANY] * 6,
        out_specs=[ANY] * 6 + [VMEM] * 8,
        scratch_shapes=[pltpu.VMEM(array.shape, array.dtype) for array in (outputs, grad_in, *shares)]
        + [pltpu.VMEM(share.shape, F32) for share in shares]
        + [pltpu.SemaphoreType.DMA((6,)), pltpu.SemaphoreType.DMA((6,))],
        compiler_params=pltpu.CompilerParams(vmem_limit_bytes=60 << 20),
        name="finish",
    )(vectors, outputs, grad_in, *shares)
    return results[:2], results[2:6], results[6:]


def rotary_tables(seq_len):
    positions = jnp.arange(seq_len, dtype=F32)
    inverse = 1.0 / ROTARY_BASE ** (jnp.arange(0, ROTARY, 2, dtype=F32) / ROTARY)
    angles = inverse[:, None] * positions[None, :]
    return jnp.cos(angles), jnp.sin(angles)


def summed(share):
    part = lax.psum_scatter(share.astype(BF16), "dp", scatter_dimension=0, tiled=True)
    return lax.psum(part, "replica").astype(F32)


def in_pieces(width):
    devices = lax.axis_size("dp")
    return devices & (devices - 1) == 0 and lax.axis_size("replica") == 4 and width % (64 * devices) == 0


def local_totals(stash, kept):
    _, _, attn_in, mlp_in, _, _, _, _, context, hidden, _ = stash
    _, grad_heads, grad_up, grad_out, vectors = kept
    vector_sums = jnp.sum(vectors, axis=0)
    groups = hidden.shape[1] // attn_in.shape[1]
    return (
        vector_sums[0],
        vector_sums[1],
        jnp.einsum("mdr,mer->de", attn_in, grad_heads, preferred_element_type=F32),
        vector_sums[4:7].reshape(-1),
        jnp.einsum("mer,mrd->ed", context, grad_out, preferred_element_type=F32),
        vector_sums[7],
        vector_sums[2],
        vector_sums[3],
        jnp.einsum("mdr,mrf->df", mlp_in, grad_up, preferred_element_type=F32),
        vector_sums[8 : 8 + groups].reshape(-1),
        jnp.einsum("mfr,mrd->fd", hidden, grad_out, preferred_element_type=F32),
        vector_sums[7],
    )


def body(tokens, cotangent, lengths, *weights):
    weights = tuple(array if array.ndim == 2 else array[0] for array in weights)
    micros = lengths.shape[0]
    width = tokens.shape[1]
    rows = tokens.shape[0] // micros
    tables = rotary_tables(rows)
    stash = forward_call(lengths, tokens.reshape(micros, rows, width), weights, tables)
    kept = backward_call(lengths, cotangent.reshape(micros, rows, width), weights, tables, stash)
    grad_scale = float(tokens.shape[0] * lax.axis_size("dp") * lax.axis_size("replica")) ** (-0.5)
    if in_pieces(width):
        shares, vectors = reduce_call(stash, kept)
        (outputs, grad_in), matrices, parts = finish_call(
            grad_scale, shares, vectors, stash[0], kept[0], weights[8].shape[1]
        )
        qkv, out, up, down = (matrix[None] for matrix in matrices)
        gain, shift, qkv_bias, out_bias, mlp_gain, mlp_shift, up_bias, down_bias = parts
        grads = (gain, shift, qkv, qkv_bias, out, out_bias, mlp_gain, mlp_shift, up, up_bias, down, down_bias)
    else:
        outputs, grad_in = stash[0], kept[0]
        grads = tuple(summed(total)[None] * grad_scale for total in local_totals(stash, kept))
    return (outputs.reshape(1, micros * rows, width), grad_in.reshape(1, micros * rows, width), *grads)


def solution(mesh):
    rows = P(("dp", "replica"), None)
    vector, matrix = P("section", None), P("section", None, None)
    out_rows = P("section", ("dp", "replica"), None)
    vector_out, matrix_out = P("section", "dp"), P("section", "dp", None)
    return jax.shard_map(
        body,
        mesh=mesh,
        in_specs=(
            rows, rows, P(("dp", "replica")), vector, vector, matrix, vector, matrix, vector, vector, vector, matrix,
            vector, matrix, vector,
        ),
        out_specs=(
            out_rows, out_rows, vector_out, vector_out, matrix_out, vector_out, matrix_out, vector_out, vector_out,
            vector_out, matrix_out, vector_out, matrix_out, vector_out,
        ),
        check_vma=False,
    )
```

```python
import functools

import jax
import jax.numpy as jnp
from jax import lax
from jax.experimental import pallas as pl
from jax.experimental.pallas import tpu as pltpu
from jax.sharding import PartitionSpec as P

HEADS = 12
HEAD_DIM = 64
ROTARY = 16
HALF = ROTARY // 2
EPSILON = 1e-05
ROTARY_BASE = 10000.0
MASKED = -1e30
LOG2_E = 1.4426950408889634
LOG2_DENSITY = -1.3257480647361593
SCALE = HEAD_DIM**-0.5
F32 = jnp.float32
BF16 = jnp.bfloat16
ANY = pl.BlockSpec(memory_space=pl.ANY)
VMEM = pl.BlockSpec(memory_space=pltpu.VMEM)
SMEM = pl.BlockSpec(memory_space=pltpu.SMEM)
ROW_CHUNK = 128
NORM_CHUNK = 256
QKV_TILE = 256
FF_TILE = 768
PIECE = 384


def dims_dot(left, right, left_dim, right_dim):
    return lax.dot_general(
        left, right, (((left_dim,), (right_dim,)), ((), ())), preferred_element_type=F32
    )


def normal_parts(v):
    scaled = v * 0.7071067811865476
    bell = jnp.exp2(LOG2_DENSITY - scaled * (scaled * LOG2_E))
    return 0.5 + 0.5 * lax.erf(scaled), bell


def forward_kernel(micros, *refs):
    (
        lengths, tokens_h, attn_gain, attn_shift, qkv_bias, out_bias, mlp_gain, mlp_shift, up_bias, down_bias,
        cosine, sine, qkv_h, out_h, up_h, down_h,
        y_h, inputs_h, attn_in_h, mlp_in_h, queries_h, keys_h, values_h, probs_h, context_h, hidden_h, slope_h,
        qkv_w, out_w, up_w, down_w, x, attn_in, mlp_in, attn_in_t, mlp_in_t, heads_t, context_t, hidden_t, slope,
        bias, total, probs, y, in_sems, out_sems, probs_sems, send_sems, recv_sems,
    ) = refs
    section = lax.axis_index("section")
    rows, width = attn_in.shape
    hidden_width = up_w.shape[1]
    half = rows // 2
    other = {"section": 1 - section}

    barrier = pltpu.get_barrier_semaphore()
    pl.semaphore_signal(barrier, inc=1, device_id=other, device_id_type=pl.DeviceIdType.MESH)
    loads = [
        pltpu.make_async_copy(src, dst, in_sems.at[i])
        for i, (src, dst) in enumerate(
            ((tokens_h, x), (qkv_h, qkv_w), (out_h, out_w), (up_h, up_w), (down_h, down_w))
        )
    ]

    @pl.when(section == 0)
    def _():
        loads[0].start()

    loads[1].start()
    probs[:, half:, :half] = jnp.zeros((probs.shape[0], half, half), BF16)
    cos_rows, sin_rows = cosine[...], sine[...]

    def hand_over(micro):
        return pltpu.make_async_remote_copy(
            src_ref=y.at[micro],
            dst_ref=x.at[micro],
            send_sem=send_sems.at[micro],
            recv_sem=recv_sems.at[micro],
            device_id=other,
            device_id_type=pl.DeviceIdType.MESH,
        )

    def stores(micro):
        pairs = [
            (x.at[micro], inputs_h.at[micro]),
            (attn_in_t, attn_in_h.at[micro]),
            (mlp_in_t, mlp_in_h.at[micro]),
            (heads_t.at[0:width], queries_h.at[micro]),
            (heads_t.at[width : 2 * width], keys_h.at[micro]),
            (heads_t.at[2 * width :], values_h.at[micro]),
            (context_t, context_h.at[micro]),
            (y.at[micro], y_h.at[micro]),
        ]
        for start in range(0, hidden_width, FF_TILE):
            part = slice(start, start + FF_TILE)
            pairs.append((hidden_t.at[part], hidden_h.at[micro, part]))
            pairs.append((slope.at[:, part], slope_h.at[micro, :, part]))
        return [pltpu.make_async_copy(src, dst, out_sems.at[i]) for i, (src, dst) in enumerate(pairs)]

    pl.semaphore_wait(barrier, 1)

    def sentence(micro, carry):
        store = stores(micro)

        def settle(first, end):
            @pl.when(micro > 0)
            def _():
                for copy in stores(micro - 1)[first:end]:
                    copy.wait()

        @pl.when((section == 0) & (micro == 0))
        def _():
            loads[0].wait()

        @pl.when(section == 1)
        def _():
            hand_over(micro).wait_recv()

        length = lengths[micro]
        key_ids = lax.broadcasted_iota(jnp.int32, (rows, rows), 0)
        query_ids = lax.broadcasted_iota(jnp.int32, (rows, rows), 1)
        bias[...] = jnp.where((key_ids <= query_ids) & (key_ids < length), 0.0, MASKED)

        settle(0, 3)
        store[0].start()
        for start in range(0, rows, ROW_CHUNK):
            part = slice(start, start + ROW_CHUNK)
            block = x[micro, part, :].astype(F32)
            centred = block - jnp.mean(block, axis=-1, keepdims=True)
            unit = centred * lax.rsqrt(jnp.mean(centred * centred, axis=-1, keepdims=True) + EPSILON)
            attn = (unit * attn_gain[...].astype(F32) + attn_shift[...].astype(F32)).astype(BF16)
            mlp = (unit * mlp_gain[...].astype(F32) + mlp_shift[...].astype(F32)).astype(BF16)
            attn_in[part, :] = attn
            mlp_in[part, :] = mlp
            attn_in_t[:, part] = attn.T
            mlp_in_t[:, part] = mlp.T
        store[1].start()
        store[2].start()

        @pl.when(micro == 0)
        def _():
            loads[1].wait()
            for load in loads[2:]:
                load.start()

        settle(3, 6)
        for start in range(0, 3 * width, QKV_TILE):
            part = slice(start, start + QKV_TILE)
            projected = jnp.dot(attn_in[...], qkv_w[:, part], preferred_element_type=F32)
            turned = (projected + qkv_bias[:, part].astype(F32)).T
            if start >= 2 * width:
                heads_t[part, :] = turned.astype(BF16)
                continue
            for at in range(0, QKV_TILE, HEAD_DIM):
                low, high = turned[at : at + HALF], turned[at + HALF : at + ROTARY]
                heads_t[start + at : start + at + HEAD_DIM, :] = jnp.concatenate(
                    [
                        low * cos_rows - high * sin_rows,
                        high * cos_rows + low * sin_rows,
                        turned[at + ROTARY : at + HEAD_DIM],
                    ],
                    axis=0,
                ).astype(BF16)
        for copy in store[3:6]:
            copy.start()

        def softmax(scores):
            raised = jnp.exp(scores - jnp.max(scores, axis=0, keepdims=True))
            return (raised * (1.0 / jnp.sum(raised, axis=0, keepdims=True))).astype(BF16)

        def attend(head, slot):
            at = pl.multiple_of(head * HEAD_DIM, HEAD_DIM)
            query = heads_t[pl.ds(at, HEAD_DIM), :] * jnp.bfloat16(SCALE)
            key = heads_t[pl.ds(width + at, HEAD_DIM), :]
            value = heads_t[pl.ds(2 * width + at, HEAD_DIM), :]
            early = softmax(dims_dot(key[:, :half], query[:, :half], 0, 0) + bias[:half, :half])
            late = softmax(dims_dot(key, query[:, half:], 0, 0) + bias[:, half:])
            probs[slot, :half, :half] = early
            probs[slot, :, half:] = late
            place = pl.ds(at, HEAD_DIM)
            context_t[place, :half] = jnp.dot(value[:, :half], early, preferred_element_type=F32).astype(BF16)
            context_t[place, half:] = jnp.dot(value, late, preferred_element_type=F32).astype(BF16)

        def probs_copy(head, slot):
            return pltpu.make_async_copy(probs.at[slot], probs_h.at[micro, head], probs_sems.at[slot])

        def attend_pair(pair, carry):
            first_slot = 2 * lax.rem(pair, 2)

            @pl.when(pair >= 2)
            def _():
                for own_head in range(2):
                    probs_copy(2 * pair + own_head - 4, first_slot + own_head).wait()

            for own_head in range(2):
                attend(2 * pair + own_head, first_slot + own_head)
            for own_head in range(2):
                probs_copy(2 * pair + own_head, first_slot + own_head).start()
            return carry

        settle(6, 7)
        lax.fori_loop(0, HEADS // 2, attend_pair, 0)
        store[6].start()

        @pl.when(micro == 0)
        def _():
            for load in loads[2:]:
                load.wait()

        total[...] = (
            dims_dot(context_t[...], out_w[...], 0, 0)
            + x[micro].astype(F32)
            + (out_bias[...].astype(F32) + down_bias[...].astype(F32))
        )
        settle(7, len(store))
        for start in range(0, hidden_width, FF_TILE):
            part = slice(start, start + FF_TILE)
            up = jnp.dot(mlp_in[...], up_w[:, part], preferred_element_type=F32)
            up = up + up_bias[:, part].astype(F32)
            share, density = normal_parts(up)
            hidden = (up * share).astype(BF16)
            slope[:, part] = (share + up * density).astype(BF16)
            hidden_t[part, :] = hidden.T
            tile = start // FF_TILE
            store[8 + 2 * tile].start()
            store[9 + 2 * tile].start()
            total[...] += jnp.dot(hidden, down_w[part, :], preferred_element_type=F32)
        y[micro] = total[...].astype(BF16)

        @pl.when(section == 0)
        def _():
            hand_over(micro).start()

        store[7].start()
        for head in range(HEADS - 4, HEADS):
            probs_copy(head, head % 4).wait()
        return carry

    lax.fori_loop(0, micros, sentence, 0)
    for copy in stores(micros - 1):
        copy.wait()

    @pl.when(section == 0)
    def _():
        for micro in range(micros):
            hand_over(micro).wait_send()


def forward_call(lengths, tokens, weights, tables):
    (
        attn_gain, attn_shift, qkv_weight, qkv_bias, out_weight, out_bias, mlp_gain, mlp_shift, up_weight, up_bias,
        down_weight, down_bias,
    ) = weights
    micros, rows, width = tokens.shape
    hidden_width = up_weight.shape[1]
    wide, tall = (micros, rows, width), (micros, width, rows)
    shapes = [
        wide, wide, tall, tall, tall, tall, tall, (micros, HEADS, rows, rows), tall, (micros, hidden_width, rows),
        (micros, rows, hidden_width),
    ]
    buffers = [
        qkv_weight.shape, out_weight.shape, up_weight.shape, down_weight.shape, wide, (rows, width), (rows, width),
        (width, rows), (width, rows), (3 * width, rows), (width, rows), (hidden_width, rows), (rows, hidden_width),
    ]
    return pl.pallas_call(
        functools.partial(forward_kernel, micros),
        out_shape=[jax.ShapeDtypeStruct(shape, BF16) for shape in shapes],
        in_specs=[SMEM, ANY] + [VMEM] * 10 + [ANY] * 4,
        out_specs=[ANY] * len(shapes),
        scratch_shapes=[pltpu.VMEM(shape, BF16) for shape in buffers]
        + [
            pltpu.VMEM((rows, rows), F32),
            pltpu.VMEM((rows, width), F32),
            pltpu.VMEM((4, rows, rows), BF16),
            pltpu.VMEM(wide, BF16),
            pltpu.SemaphoreType.DMA((5,)),
            pltpu.SemaphoreType.DMA((8 + 2 * (hidden_width // FF_TILE),)),
            pltpu.SemaphoreType.DMA((4,)),
            pltpu.SemaphoreType.DMA((micros,)),
            pltpu.SemaphoreType.DMA((micros,)),
        ],
        compiler_params=pltpu.CompilerParams(collective_id=1, has_side_effects=True, vmem_limit_bytes=58 << 20),
        cost_estimate=pl.CostEstimate(
            flops=micros * (2 * rows * width * (4 * width + 2 * hidden_width) + 4 * rows * rows * width),
            bytes_accessed=80 << 20,
            transcendentals=micros * rows * hidden_width,
        ),
        name="layer_forward",
    )(
        lengths, tokens, attn_gain, attn_shift, qkv_bias, out_bias, mlp_gain, mlp_shift, up_bias, down_bias,
        *tables, qkv_weight, out_weight, up_weight, down_weight,
    )


def backward_kernel(micros, *refs):
    (
        lengths, cotangent_h, inputs_h, attn_gain, mlp_gain, cosine, sine, qkv_h, out_h, up_h, down_h,
        queries_h, keys_h, values_h, probs_h, context_h, slope_h,
        grad_in_h, grad_heads_h, grad_up_h, grad_out_h, vectors_h,
        qkv_w, out_w, up_w, down_w, queries, keys, values, context, slope, probs, grad_out, x, grad_context,
        grad_up, grad_heads, grad_low, grad_mlp, grad_in, column_sums, vectors,
        in_sems, stash_sems, out_sems, probs_sems, send_sems, recv_sems,
    ) = refs
    section = lax.axis_index("section")
    rows, width = x.shape
    hidden_width = up_w.shape[1]
    half = rows // 2
    other = {"section": 1 - section}

    barrier = pltpu.get_barrier_semaphore()
    pl.semaphore_signal(barrier, inc=1, device_id=other, device_id_type=pl.DeviceIdType.MESH)
    loads = [
        pltpu.make_async_copy(src, dst, in_sems.at[i])
        for i, (src, dst) in enumerate(
            ((cotangent_h, grad_out), (out_h, out_w), (down_h, down_w), (up_h, up_w), (qkv_h, qkv_w))
        )
    ]

    def stash_loads(micro):
        pairs = (
            (slope_h, slope), (values_h, values), (context_h, context), (queries_h, queries), (keys_h, keys),
            (inputs_h, x),
        )
        return [
            pltpu.make_async_copy(src.at[micro], dst, stash_sems.at[i]) for i, (src, dst) in enumerate(pairs)
        ]

    @pl.when(section == 1)
    def _():
        loads[0].start()

    for load in loads[1:3]:
        load.start()
    stash_loads(0)[0].start()
    loads[3].start()
    for load in stash_loads(0)[1:]:
        load.start()
    loads[4].start()
    cos_rows, sin_rows = cosine[...], sine[...]
    attn_column = jnp.broadcast_to(attn_gain[...].astype(F32), (8, width)).T[:, 0:1]
    mlp_column = jnp.broadcast_to(mlp_gain[...].astype(F32), (8, width)).T[:, 0:1]

    def hand_over(micro):
        return pltpu.make_async_remote_copy(
            src_ref=grad_low.at[micro],
            dst_ref=grad_out.at[micro],
            send_sem=send_sems.at[micro],
            recv_sem=recv_sems.at[micro],
            device_id=other,
            device_id_type=pl.DeviceIdType.MESH,
        )

    def stores(micro):
        pairs = [
            (grad_out.at[micro], grad_out_h.at[micro]),
            (grad_heads, grad_heads_h.at[micro]),
            (grad_in, grad_in_h.at[micro]),
            (vectors, vectors_h.at[micro]),
        ]
        for start in range(0, hidden_width, FF_TILE):
            part = slice(start, start + FF_TILE)
            pairs.append((grad_up.at[:, part], grad_up_h.at[micro, :, part]))
        return [pltpu.make_async_copy(src, dst, out_sems.at[i]) for i, (src, dst) in enumerate(pairs)]

    pl.semaphore_wait(barrier, 1)

    def sentence(micro, carry):
        store = stores(micro)
        stash = stash_loads(micro)
        upcoming = stash_loads(micro + 1)

        def settle(first, end):
            @pl.when(micro > 0)
            def _():
                for copy in stores(micro - 1)[first:end]:
                    copy.wait()

        def probs_copy(head, slot):
            return pltpu.make_async_copy(probs_h.at[micro, head], probs.at[slot], probs_sems.at[slot])

        for head in range(2):
            probs_copy(head, head).start()

        @pl.when((section == 1) & (micro == 0))
        def _():
            loads[0].wait()

        @pl.when(section == 0)
        def _():
            hand_over(micro).wait_recv()

        row_ids = lax.broadcasted_iota(jnp.int32, (rows, 1), 0)
        grad_wide = jnp.where(row_ids < lengths[micro], grad_out[micro].astype(F32), 0.0)
        grad_out[micro] = grad_wide.astype(BF16)

        settle(0, 1)
        settle(3, len(store))
        vectors[...] = jnp.zeros_like(vectors)
        vectors[7:8, :] = jnp.sum(grad_wide, axis=0, keepdims=True)
        store[0].start()

        @pl.when(micro == 0)
        def _():
            loads[1].wait()

        grad_context[...] = dims_dot(out_w[...], grad_out[micro], 1, 1).astype(BF16)

        @pl.when(micro == 0)
        def _():
            loads[2].wait()
            loads[3].wait()

        stash[0].wait()
        for start in range(0, hidden_width, FF_TILE):
            part = slice(start, start + FF_TILE)
            grad_hidden = dims_dot(grad_out[micro], down_w[part, :], 1, 1)
            grad_pre = (grad_hidden * slope[:, part].astype(F32)).astype(BF16)
            grad_up[:, part] = grad_pre
            store[4 + start // FF_TILE].start()
            sums = jnp.sum(grad_pre.astype(F32), axis=0, keepdims=True)
            for at in range(0, FF_TILE, 128):
                row, column = divmod(start + at, width)
                vectors[8 + row : 9 + row, column : column + 128] = sums[:, at : at + 128]
            back = dims_dot(up_w[:, part], grad_pre, 1, 1)
            if start == 0:
                grad_mlp[...] = back
            else:
                grad_mlp[...] += back

        @pl.when(micro < micros - 1)
        def _():
            upcoming[0].start()

        for load in stash[1:5]:
            load.wait()

        def turn_back(grad):
            low, high = grad[:HALF], grad[HALF:ROTARY]
            return jnp.concatenate(
                [low * cos_rows + high * sin_rows, high * cos_rows - low * sin_rows, grad[ROTARY:]], axis=0
            )

        def over_queries(left, early, late):
            both = dims_dot(left[:, half:], late, 1, 1)
            return jnp.concatenate([both[:, :half] + dims_dot(left[:, :half], early, 1, 1), both[:, half:]], axis=1)

        def attend(head, slot):
            at = pl.multiple_of(head * HEAD_DIM, HEAD_DIM)
            place = pl.ds(at, HEAD_DIM)
            query, key, value, grad = queries[place, :], keys[place, :], values[place, :], grad_context[place, :]
            inner = jnp.sum(grad.astype(F32) * context[place, :].astype(F32), axis=0, keepdims=True)
            early, late = probs[slot, :half, :half], probs[slot, :, half:]
            grad_early = dims_dot(value[:, :half], grad[:, :half], 0, 0) - inner[:, :half]
            grad_late = dims_dot(value, grad[:, half:], 0, 0) - inner[:, half:]
            grad_early = (early.astype(F32) * grad_early).astype(BF16)
            grad_late = (late.astype(F32) * grad_late).astype(BF16)
            grad_value = over_queries(grad, early, late)
            grad_key = over_queries(query, grad_early, grad_late)
            grad_query = jnp.concatenate(
                [
                    jnp.dot(key[:, :half], grad_early, preferred_element_type=F32),
                    jnp.dot(key, grad_late, preferred_element_type=F32),
                ],
                axis=1,
            )
            grad_heads[place, :] = turn_back(grad_query * SCALE).astype(BF16)
            grad_heads[pl.ds(width + at, HEAD_DIM), :] = turn_back(grad_key * SCALE).astype(BF16)
            grad_heads[pl.ds(2 * width + at, HEAD_DIM), :] = grad_value.astype(BF16)

        def attend_pair(pair, carry):
            first_slot = 2 * lax.rem(pair, 2)

            @pl.when(pair < HEADS // 2 - 1)
            def _():
                for own_head in range(2):
                    probs_copy(2 * pair + 2 + own_head, 2 - first_slot + own_head).start()

            for own_head in range(2):
                probs_copy(2 * pair + own_head, first_slot + own_head).wait()
            for own_head in range(2):
                attend(2 * pair + own_head, first_slot + own_head)
            return carry

        settle(1, 2)
        lax.fori_loop(0, HEADS // 2, attend_pair, 0)
        store[1].start()

        @pl.when(micro < micros - 1)
        def _():
            for load in upcoming[1:5]:
                load.start()

        @pl.when(micro == 0)
        def _():
            loads[4].wait()

        stash[5].wait()
        column_sums[...] = jnp.zeros_like(column_sums)
        settle(2, 3)

        def norm_chunk(index, carry):
            part = pl.ds(pl.multiple_of(index * NORM_CHUNK, NORM_CHUNK), NORM_CHUNK)
            grad_attn_in = jnp.dot(qkv_w[...], grad_heads[:, part], preferred_element_type=F32)
            grad_mlp_in = grad_mlp[:, part]
            turned = x[part, :].astype(F32).T
            centred = turned - jnp.mean(turned, axis=0, keepdims=True)
            inv_spread = lax.rsqrt(jnp.mean(centred * centred, axis=0, keepdims=True) + EPSILON)
            unit = centred * inv_spread
            grad_unit = grad_attn_in * attn_column + grad_mlp_in * mlp_column
            through = inv_spread * (
                grad_unit
                - jnp.mean(grad_unit, axis=0, keepdims=True)
                - unit * jnp.mean(grad_unit * unit, axis=0, keepdims=True)
            )
            exact = through.T + grad_out[micro, part, :].astype(F32)
            low = exact.astype(BF16)
            grad_low[micro, part, :] = low
            grad_in[part, :] = jnp.where(section == 0, exact, low.astype(F32))
            terms = (grad_attn_in * unit, grad_attn_in, grad_mlp_in * unit, grad_mlp_in)
            for i, term in enumerate(terms):
                for at in range(0, NORM_CHUNK, 128):
                    column_sums[i] += term[:, at : at + 128]
            return carry

        lax.fori_loop(0, rows // NORM_CHUNK, norm_chunk, 0)

        @pl.when(section == 1)
        def _():
            hand_over(micro).start()

        @pl.when(micro < micros - 1)
        def _():
            upcoming[5].start()

        store[2].start()
        columns = [jnp.sum(column_sums[i], axis=1, keepdims=True) for i in range(4)]
        for start in range(0, 3 * width, width):
            columns.append(jnp.sum(grad_heads[start : start + width, :].astype(F32), axis=1, keepdims=True))
        lanes = lax.broadcasted_iota(jnp.int32, (width, 128), 1)
        gathered = jnp.zeros((width, 128), F32)
        for lane, column in enumerate(columns):
            gathered = jnp.where(lanes == lane, column, gathered)
        vectors[0:7, :] = gathered.T[0:7, :]
        store[3].start()
        return carry

    lax.fori_loop(0, micros, sentence, 0)
    for copy in stores(micros - 1):
        copy.wait()

    @pl.when(section == 1)
    def _():
        for micro in range(micros):
            hand_over(micro).wait_send()


def backward_call(lengths, cotangent, weights, tables, stash):
    attn_gain, _, qkv_weight, _, out_weight, _, mlp_gain, _, up_weight, _, down_weight, _ = weights
    _, inputs, _, _, queries, keys, values, probs, context, _, slope = stash
    micros, rows, width = cotangent.shape
    hidden_width = up_weight.shape[1]
    vector_rows = 16
    wide, tall = (micros, rows, width), (width, rows)
    outs = [
        jax.ShapeDtypeStruct(wide, F32),
        jax.ShapeDtypeStruct((micros, 3 * width, rows), BF16),
        jax.ShapeDtypeStruct((micros, rows, hidden_width), BF16),
        jax.ShapeDtypeStruct(wide, BF16),
        jax.ShapeDtypeStruct((micros, vector_rows, width), F32),
    ]
    return pl.pallas_call(
        functools.partial(backward_kernel, micros),
        out_shape=outs,
        in_specs=[SMEM] + [ANY] * 2 + [VMEM] * 4 + [ANY] * 10,
        out_specs=[ANY] * len(outs),
        scratch_shapes=[
            pltpu.VMEM(qkv_weight.shape, BF16),
            pltpu.VMEM(out_weight.shape, BF16),
            pltpu.VMEM(up_weight.shape, BF16),
            pltpu.VMEM(down_weight.shape, BF16),
            pltpu.VMEM(tall, BF16),
            pltpu.VMEM(tall, BF16),
            pltpu.VMEM(tall, BF16),
            pltpu.VMEM(tall, BF16),
            pltpu.VMEM((rows, hidden_width), BF16),
            pltpu.VMEM((4, rows, rows), BF16),
            pltpu.VMEM(wide, BF16),
            pltpu.VMEM((rows, width), BF16),
            pltpu.VMEM(tall, BF16),
            pltpu.VMEM((rows, hidden_width), BF16),
            pltpu.VMEM((3 * width, rows), BF16),
            pltpu.VMEM(wide, BF16),
            pltpu.VMEM(tall, F32),
            pltpu.VMEM((rows, width), F32),
            pltpu.VMEM((4, width, 128), F32),
            pltpu.VMEM((vector_rows, width), F32),
            pltpu.SemaphoreType.DMA((5,)),
            pltpu.SemaphoreType.DMA((6,)),
            pltpu.SemaphoreType.DMA((4 + hidden_width // FF_TILE,)),
            pltpu.SemaphoreType.DMA((4,)),
            pltpu.SemaphoreType.DMA((micros,)),
            pltpu.SemaphoreType.DMA((micros,)),
        ],
        compiler_params=pltpu.CompilerParams(collective_id=2, has_side_effects=True, vmem_limit_bytes=58 << 20),
        cost_estimate=pl.CostEstimate(
            flops=micros * (2 * rows * width * (4 * width + 2 * hidden_width) + 8 * rows * rows * width),
            bytes_accessed=80 << 20,
            transcendentals=0,
        ),
        name="layer_backward",
    )(
        lengths, cotangent, inputs, attn_gain, mlp_gain, *tables, qkv_weight, out_weight, up_weight, down_weight,
        queries, keys, values, probs, context, slope,
    )


def partner(axis, bit):
    index = lax.axis_index(axis)
    own_bit = (index // bit) % 2
    return {axis: index + bit - 2 * bit * own_bit}, own_bit


def piece_plan(width, hidden_width, piece):
    counts = [width // piece, hidden_width // piece, hidden_width // piece, 3 * width // piece]
    starts = [0]
    for count in counts:
        starts.append(starts[-1] + count)
    return starts


def reduce_kernel(bits, piece, *refs):
    (
        context_h, hidden_h, mlp_in_h, attn_in_h, grad_out_h, grad_up_h, grad_heads_h, vectors_h,
        qkv_o, out_o, up_o, down_o, vectors_o,
        left, right, heads, vectors, own, final, from_first, *rest,
    ) = refs
    from_dp, rest = rest[:bits], rest[bits:]
    (
        from_second, vector_sum, from_vector,
        in_sems, send_sems, recv_sems, vector_send, vector_recv, out_sems,
    ) = rest
    micros, devices, share, rows = attn_in_h.shape
    width = devices * share
    hidden_width = grad_up_h.shape[2]
    groups = hidden_width // width
    out_at, down_at, up_at, qkv_at, pieces = piece_plan(width, hidden_width, piece)
    across = width // piece

    barrier = pltpu.get_barrier_semaphore()
    dp_peers = [partner("dp", 1 << bit) for bit in range(bits)]
    replica_peers = [partner("replica", 1), partner("replica", 2)]
    for device, _ in dp_peers + replica_peers:
        pl.semaphore_signal(barrier, inc=1, device_id=device, device_id_type=pl.DeviceIdType.MESH)

    wide = hidden_width + width
    loads = [
        [(context_h, left.at[0]), (grad_out_h, right.at[:, :, 0:width]), (vectors_h, vectors)],
        [(hidden_h.at[:, :, group], left.at[3 + group]) for group in range(groups)],
        [(mlp_in_h, left.at[1]), (grad_up_h, right.at[:, :, width:wide])],
        [(attn_in_h, left.at[2]), (grad_heads_h, heads)],
    ]
    copies, count = [], 0
    for group in loads:
        copies.append([])
        for src, dst in group:
            copies[-1].append(pltpu.make_async_copy(src, dst, in_sems.at[count]))
            count += 1
    for copy in copies[0]:
        copy.start()
    for copy in copies[0]:
        copy.wait()
    for group in copies[1:]:
        for copy in group:
            copy.start()
    vector_sum[0] = jnp.sum(vectors[...], axis=0)
    pl.semaphore_wait(barrier, len(dp_peers) + len(replica_peers))

    dp_bits = [own_bit for _, own_bit in dp_peers]

    def keep(k, depth, first_bit=None, second_bit=None, flip=None):
        index = [k] + [slice(None)] * (bits - depth)
        for bit in reversed(range(depth)):
            index.append(1 - dp_bits[bit] if flip == bit else dp_bits[bit])
        if first_bit is not None:
            index.append(first_bit)
        if second_bit is not None:
            index.append(second_bit)
        return tuple(index)

    def transfers(k, turned):
        (first, first_bit), (second, second_bit) = replica_peers[::-1] if turned else replica_peers
        steps = [
            (own.at[keep(k, 0, 1 - first_bit)], from_first.at[k], first, own.at[keep(k, 0, first_bit)]),
        ]
        for bit in range(bits):
            steps.append(
                (
                    own.at[keep(k, bit + 1, first_bit, flip=bit)],
                    from_dp[bit].at[k],
                    dp_peers[bit][0],
                    own.at[keep(k, bit + 1, first_bit)],
                )
            )
        mine = final.at[k, first_bit, second_bit]
        steps.append(
            (
                own.at[keep(k, bits, first_bit, 1 - second_bit)],
                from_second.at[k],
                second,
                own.at[keep(k, bits, first_bit, second_bit)],
            )
        )
        steps.append((mine, mine, second, None))
        steps.append((final.at[k, first_bit], final.at[k, first_bit], first, None))
        return steps, mine

    def copy_of(k, stage, step):
        src, dst, device, _ = step
        return pltpu.make_async_remote_copy(
            src_ref=src,
            dst_ref=dst,
            send_sem=send_sems.at[k, stage],
            recv_sem=recv_sems.at[k, stage],
            device_id=device,
            device_id_type=pl.DeviceIdType.MESH,
        )

    n_steps = bits + 4

    def advance(k, stage, turned):
        steps, mine = transfers(k, turned)
        if stage > 0:
            step = steps[stage - 1]
            copy_of(k, stage - 1, step).wait()
            if step[3] is not None:
                total = step[3][...].astype(F32) + step[1][...].astype(F32)
                if stage == bits + 2:
                    mine[...] = total.astype(BF16)
                else:
                    step[3][...] = total.astype(BF16)
        if stage < n_steps:
            copy_of(k, stage, steps[stage]).start()

    def advance_either(k, stage):
        for turned in (False, True):

            @pl.when(k % 2 == int(turned))
            def _():
                advance(k, stage, turned)

    shape = own.shape[1:]

    def panel(index, micro):
        return left[index, micro].reshape(width, rows)

    def set_own(k, index, columns):
        value = columns(0, panel(index, 0))
        for micro in range(1, micros):
            value = value + columns(micro, panel(index, micro))
        own[k] = value.astype(BF16).reshape(shape)

    def lanes(index):
        return pl.ds(pl.multiple_of(index * piece, 128), piece)

    def compute(k):
        @pl.when(k < down_at)
        def _():
            part = lanes(k)
            set_own(k, 0, lambda micro, block: dims_dot(block, right[micro, :, part], 1, 0))

        @pl.when((k >= down_at) & (k < up_at))
        def _():
            part = lanes((k - down_at) % across)
            set_own(
                k, 3 + (k - down_at) // across, lambda micro, block: dims_dot(block, right[micro, :, part], 1, 0)
            )

        @pl.when((k >= up_at) & (k < qkv_at))
        def _():
            part = lanes(across + k - up_at)
            set_own(k, 1, lambda micro, block: dims_dot(block, right[micro, :, part], 1, 0))

        @pl.when(k >= qkv_at)
        def _():
            part = lanes(k - qkv_at)
            set_own(k, 2, lambda micro, block: dims_dot(block, heads[micro, part, :], 1, 1))

    def out_copy(k, kind):
        if kind == "down":
            target = down_o.at[(k - down_at) // across, :, :, :, lanes((k - down_at) % across)]
        else:
            ref, start = {"out": (out_o, out_at), "up": (up_o, up_at), "qkv": (qkv_o, qkv_at)}[kind]
            target = ref.at[:, :, :, lanes(k - start)]
        return pltpu.make_async_copy(final.at[k], target, out_sems.at[k])

    ranges = {"out": (out_at, down_at), "down": (down_at, up_at), "up": (up_at, qkv_at), "qkv": (qkv_at, pieces)}

    def stored(k, do):
        for kind, (first, end) in ranges.items():

            @pl.when((k >= first) & (k < end))
            def _():
                do(out_copy(k, kind))

    vector_peers = dp_peers + replica_peers

    def vector_copy(i):
        return pltpu.make_async_remote_copy(
            src_ref=vector_sum.at[i],
            dst_ref=from_vector.at[i],
            send_sem=vector_send.at[i],
            recv_sem=vector_recv.at[i],
            device_id=vector_peers[i][0],
            device_id_type=pl.DeviceIdType.MESH,
        )

    lags = [0]
    for stage in range(n_steps):
        lags.append(lags[-1] + (4 if stage == 0 else 2))

    def turn(t, carry):
        for at, group in zip((down_at, up_at, qkv_at), copies[1:]):

            @pl.when(t == at)
            def _():
                for copy in group:
                    copy.wait()

        @pl.when(t < pieces)
        def _():
            compute(t)

        for stage in range(n_steps + 1):
            k = t - lags[stage]

            @pl.when((k >= 0) & (k < pieces))
            def _():
                advance_either(k, stage)
                if stage == n_steps:
                    stored(k, lambda copy: copy.start())

        for i in range(len(vector_peers) + 1):

            @pl.when(t == 4 * i)
            def _():
                if i > 0:
                    vector_copy(i - 1).wait()
                    vector_sum[i] = vector_sum[i - 1] + from_vector[i - 1]
                if i < len(vector_peers):
                    vector_copy(i).start()
                else:
                    pltpu.make_async_copy(vector_sum.at[i], vectors_o, out_sems.at[pieces]).start()

        return carry

    lax.fori_loop(0, pieces + lags[-1], turn, 0)

    def finish(k, carry):
        stored(k, lambda copy: copy.wait())
        return carry

    lax.fori_loop(0, pieces, finish, 0)
    pltpu.make_async_copy(vector_sum.at[len(vector_peers)], vectors_o, out_sems.at[pieces]).wait()


def reduce_call(stash, kept):
    _, _, attn_in, mlp_in, _, _, _, _, context, hidden, _ = stash
    _, grad_heads, grad_up, grad_out, vectors = kept
    micros, width, rows = attn_in.shape
    hidden_width = hidden.shape[1]
    groups = hidden_width // width
    devices = lax.axis_size("dp")
    bits = devices.bit_length() - 1
    share, quarter = width // devices, width // devices // 4
    piece = PIECE
    pieces = piece_plan(width, hidden_width, piece)[-1]
    loads = 6 + groups + 1
    tall = (micros, devices, share, rows)
    halves = [2] * bits
    steps = bits + 4
    peers = bits + 2
    shape = lambda columns: jax.ShapeDtypeStruct((2, 2, quarter, columns), BF16)
    outs = pl.pallas_call(
        functools.partial(reduce_kernel, bits, piece),
        out_shape=[
            shape(3 * width),
            shape(width),
            shape(hidden_width),
            jax.ShapeDtypeStruct((groups, 2, 2, quarter, width), BF16),
            jax.ShapeDtypeStruct(vectors.shape[1:], F32),
        ],
        in_specs=[ANY] * 8,
        out_specs=[ANY] * 5,
        scratch_shapes=[
            pltpu.VMEM((3 + groups, *tall), BF16),
            pltpu.VMEM((micros, rows, width + hidden_width), BF16),
            pltpu.VMEM(grad_heads.shape, BF16),
            pltpu.VMEM(vectors.shape, F32),
            pltpu.VMEM((pieces, *halves, 2, 2, quarter, piece), BF16),
            pltpu.VMEM((pieces, 2, 2, quarter, piece), BF16),
            pltpu.VMEM((pieces, *halves, 2, quarter, piece), BF16),
            *[pltpu.VMEM((pieces, *halves[bit + 1 :], 2, quarter, piece), BF16) for bit in range(bits)],
            pltpu.VMEM((pieces, quarter, piece), BF16),
            pltpu.VMEM((peers + 1, *vectors.shape[1:]), F32),
            pltpu.VMEM((peers, *vectors.shape[1:]), F32),
            pltpu.SemaphoreType.DMA((loads,)),
            pltpu.SemaphoreType.DMA((pieces, steps)),
            pltpu.SemaphoreType.DMA((pieces, steps)),
            pltpu.SemaphoreType.DMA((peers,)),
            pltpu.SemaphoreType.DMA((peers,)),
            pltpu.SemaphoreType.DMA((pieces + 1,)),
        ],
        compiler_params=pltpu.CompilerParams(
            collective_id=0, has_side_effects=True, vmem_limit_bytes=60 << 20
        ),
        cost_estimate=pl.CostEstimate(
            flops=2 * micros * rows * width * (4 * width + 2 * hidden_width),
            bytes_accessed=30 << 20,
            transcendentals=0,
        ),
        name="weight_gradients",
    )(
        context.reshape(tall),
        hidden.reshape(micros, devices, groups, share, rows),
        mlp_in.reshape(tall),
        attn_in.reshape(tall),
        grad_out,
        grad_up,
        grad_heads,
        vectors,
    )
    qkv, out, up, down, sums = outs
    scattered = [array.reshape(-1, array.shape[-1]) for array in (qkv, out, up, down)]
    return scattered, sums


def finish_kernel(grad_scale, *refs):
    vectors = refs[0]
    sources = refs[1:7]
    targets = refs[7:13]
    vector_outs = refs[13:21]
    held, wide = refs[21:27], refs[27:31]
    in_sems, out_sems = refs[31:]
    ready = (*held[:2], *wide)
    loads = [pltpu.make_async_copy(src, dst, in_sems.at[i]) for i, (src, dst) in enumerate(zip(sources, held))]
    stores = [pltpu.make_async_copy(src, dst, out_sems.at[i]) for i, (src, dst) in enumerate(zip(ready, targets))]
    for load in loads:
        load.start()
    devices = lax.axis_size("dp")
    mine = lax.axis_index("dp")
    width = vectors.shape[1]
    first_rows = (0, 1, 4, 7, 2, 3, 8, 7)
    for device in range(devices):

        @pl.when(mine == device)
        def _():
            for out, first in zip(vector_outs, first_rows):
                at, size, filled = device * out.shape[1], out.shape[1], 0
                while filled < size:
                    row, column = divmod(at + filled, width)
                    count = min(size - filled, width - column)
                    piece = vectors[first + row : first + row + 1, column : column + count]
                    out[:, filled : filled + count] = piece * grad_scale
                    filled += count

    for i, (load, store) in enumerate(zip(loads, stores)):
        load.wait()
        if i >= 2:
            wide[i - 2][...] = held[i][...].astype(F32) * grad_scale
        store.start()
    for store in stores:
        store.wait()


def finish_call(grad_scale, shares, vectors, outputs, grad_in, hidden_width):
    width = vectors.shape[1]
    devices = lax.axis_size("dp")
    sizes = [width, width, 3 * width, width, width, width, hidden_width, width]
    matrices = [jax.ShapeDtypeStruct(share.shape, F32) for share in shares]
    results = pl.pallas_call(
        functools.partial(finish_kernel, grad_scale),
        out_shape=[
            jax.ShapeDtypeStruct(outputs.shape, BF16),
            jax.ShapeDtypeStruct(grad_in.shape, F32),
            *matrices,
            *[jax.ShapeDtypeStruct((1, size // devices), F32) for size in sizes],
        ],
        in_specs=[VMEM] + [ANY] * 6,
        out_specs=[ANY] * 6 + [VMEM] * 8,
        scratch_shapes=[pltpu.VMEM(array.shape, array.dtype) for array in (outputs, grad_in, *shares)]
        + [pltpu.VMEM(share.shape, F32) for share in shares]
        + [pltpu.SemaphoreType.DMA((6,)), pltpu.SemaphoreType.DMA((6,))],
        compiler_params=pltpu.CompilerParams(vmem_limit_bytes=60 << 20),
        name="finish",
    )(vectors, outputs, grad_in, *shares)
    return results[:2], results[2:6], results[6:]


def rotary_tables(seq_len):
    positions = jnp.arange(seq_len, dtype=F32)
    inverse = 1.0 / ROTARY_BASE ** (jnp.arange(0, ROTARY, 2, dtype=F32) / ROTARY)
    angles = inverse[:, None] * positions[None, :]
    return jnp.cos(angles), jnp.sin(angles)


def summed(share):
    part = lax.psum_scatter(share.astype(BF16), "dp", scatter_dimension=0, tiled=True)
    return lax.psum(part, "replica").astype(F32)


def in_pieces(width):
    devices = lax.axis_size("dp")
    return devices & (devices - 1) == 0 and lax.axis_size("replica") == 4 and width % (64 * devices) == 0


def local_totals(stash, kept):
    _, _, attn_in, mlp_in, _, _, _, _, context, hidden, _ = stash
    _, grad_heads, grad_up, grad_out, vectors = kept
    vector_sums = jnp.sum(vectors, axis=0)
    groups = hidden.shape[1] // attn_in.shape[1]
    return (
        vector_sums[0],
        vector_sums[1],
        jnp.einsum("mdr,mer->de", attn_in, grad_heads, preferred_element_type=F32),
        vector_sums[4:7].reshape(-1),
        jnp.einsum("mer,mrd->ed", context, grad_out, preferred_element_type=F32),
        vector_sums[7],
        vector_sums[2],
        vector_sums[3],
        jnp.einsum("mdr,mrf->df", mlp_in, grad_up, preferred_element_type=F32),
        vector_sums[8 : 8 + groups].reshape(-1),
        jnp.einsum("mfr,mrd->fd", hidden, grad_out, preferred_element_type=F32),
        vector_sums[7],
    )


def body(tokens, cotangent, lengths, *weights):
    weights = tuple(array if array.ndim == 2 else array[0] for array in weights)
    micros = lengths.shape[0]
    width = tokens.shape[1]
    rows = tokens.shape[0] // micros
    tables = rotary_tables(rows)
    stash = forward_call(lengths, tokens.reshape(micros, rows, width), weights, tables)
    kept = backward_call(lengths, cotangent.reshape(micros, rows, width), weights, tables, stash)
    grad_scale = float(tokens.shape[0] * lax.axis_size("dp") * lax.axis_size("replica")) ** (-0.5)
    if in_pieces(width):
        shares, vectors = reduce_call(stash, kept)
        (outputs, grad_in), matrices, parts = finish_call(
            grad_scale, shares, vectors, stash[0], kept[0], weights[8].shape[1]
        )
        qkv, out, up, down = (matrix[None] for matrix in matrices)
        gain, shift, qkv_bias, out_bias, mlp_gain, mlp_shift, up_bias, down_bias = parts
        grads = (gain, shift, qkv, qkv_bias, out, out_bias, mlp_gain, mlp_shift, up, up_bias, down, down_bias)
    else:
        outputs, grad_in = stash[0], kept[0]
        grads = tuple(summed(total)[None] * grad_scale for total in local_totals(stash, kept))
    return (outputs.reshape(1, micros * rows, width), grad_in.reshape(1, micros * rows, width), *grads)


def solution(mesh):
    rows = P(("dp", "replica"), None)
    vector, matrix = P("section", None), P("section", None, None)
    out_rows = P("section", ("dp", "replica"), None)
    vector_out, matrix_out = P("section", "dp"), P("section", "dp", None)
    return jax.shard_map(
        body,
        mesh=mesh,
        in_specs=(
            rows, rows, P(("dp", "replica")), vector, vector, matrix, vector, matrix, vector, vector, vector, matrix,
            vector, matrix, vector,
        ),
        out_specs=(
            out_rows, out_rows, vector_out, vector_out, matrix_out, vector_out, matrix_out, vector_out, vector_out,
            vector_out, matrix_out, vector_out, matrix_out, vector_out,
        ),
        check_vma=False,
    )
```

```python
import functools

import jax
import jax.numpy as jnp
from jax import lax
from jax.experimental import pallas as pl
from jax.experimental.pallas import tpu as pltpu
from jax.sharding import PartitionSpec as P

HEADS = 12
HEAD_DIM = 64
ROTARY = 16
HALF = ROTARY // 2
EPSILON = 1e-05
ROTARY_BASE = 10000.0
MASKED = -1e30
LOG2_E = 1.4426950408889634
LOG2_DENSITY = -1.3257480647361593
SCALE = HEAD_DIM**-0.5
F32 = jnp.float32
BF16 = jnp.bfloat16
ANY = pl.BlockSpec(memory_space=pl.ANY)
VMEM = pl.BlockSpec(memory_space=pltpu.VMEM)
SMEM = pl.BlockSpec(memory_space=pltpu.SMEM)
ROW_CHUNK = 128
NORM_CHUNK = 256
QKV_TILE = 256
FF_TILE = 768
PIECE = 384


def dims_dot(left, right, left_dim, right_dim):
    return lax.dot_general(
        left, right, (((left_dim,), (right_dim,)), ((), ())), preferred_element_type=F32
    )


def normal_parts(v):
    scaled = v * 0.7071067811865476
    bell = jnp.exp2(LOG2_DENSITY - scaled * (scaled * LOG2_E))
    return 0.5 + 0.5 * lax.erf(scaled), bell


def forward_kernel(micros, *refs):
    (
        lengths, tokens_h, attn_gain, attn_shift, qkv_bias, out_bias, mlp_gain, mlp_shift, up_bias, down_bias,
        cosine, sine, qkv_h, out_h, up_h, down_h,
        y_h, inputs_h, attn_in_h, mlp_in_h, queries_h, keys_h, values_h, probs_h, context_h, hidden_h, slope_h,
        qkv_w, out_w, up_w, down_w, x, attn_in, mlp_in, attn_in_t, mlp_in_t, heads_t, context_t, hidden_t, slope,
        bias, total, probs, y, in_sems, out_sems, send_sems, recv_sems,
    ) = refs
    section = lax.axis_index("section")
    rows, width = attn_in.shape
    hidden_width = up_w.shape[1]
    half = rows // 2
    other = {"section": 1 - section}

    barrier = pltpu.get_barrier_semaphore()
    pl.semaphore_signal(barrier, inc=1, device_id=other, device_id_type=pl.DeviceIdType.MESH)
    loads = [
        pltpu.make_async_copy(src, dst, in_sems.at[i])
        for i, (src, dst) in enumerate(
            ((tokens_h, x), (qkv_h, qkv_w), (out_h, out_w), (up_h, up_w), (down_h, down_w))
        )
    ]

    @pl.when(section == 0)
    def _():
        loads[0].start()

    loads[1].start()
    probs[:, half:, :half] = jnp.zeros((probs.shape[0], half, half), BF16)
    cos_rows, sin_rows = cosine[...], sine[...]

    def hand_over(micro):
        return pltpu.make_async_remote_copy(
            src_ref=y.at[micro],
            dst_ref=x.at[micro],
            send_sem=send_sems.at[micro],
            recv_sem=recv_sems.at[micro],
            device_id=other,
            device_id_type=pl.DeviceIdType.MESH,
        )

    def stores(micro):
        pairs = [
            (x.at[micro], inputs_h.at[micro]),
            (attn_in_t, attn_in_h.at[micro]),
            (mlp_in_t, mlp_in_h.at[micro]),
            (heads_t.at[0:width], queries_h.at[micro]),
            (heads_t.at[width : 2 * width], keys_h.at[micro]),
            (heads_t.at[2 * width :], values_h.at[micro]),
            (context_t, context_h.at[micro]),
            (y.at[micro], y_h.at[micro]),
            (probs, probs_h.at[micro]),
        ]
        for start in range(0, hidden_width, FF_TILE):
            part = slice(start, start + FF_TILE)
            pairs.append((hidden_t.at[part], hidden_h.at[micro, part]))
            pairs.append((slope.at[:, part], slope_h.at[micro, :, part]))
        return [pltpu.make_async_copy(src, dst, out_sems.at[i]) for i, (src, dst) in enumerate(pairs)]

    pl.semaphore_wait(barrier, 1)

    def sentence(micro, carry):
        store = stores(micro)

        def settle(first, end):
            @pl.when(micro > 0)
            def _():
                for copy in stores(micro - 1)[first:end]:
                    copy.wait()

        @pl.when((section == 0) & (micro == 0))
        def _():
            loads[0].wait()

        @pl.when(section == 1)
        def _():
            hand_over(micro).wait_recv()

        length = lengths[micro]
        key_ids = lax.broadcasted_iota(jnp.int32, (rows, rows), 0)
        query_ids = lax.broadcasted_iota(jnp.int32, (rows, rows), 1)
        bias[...] = jnp.where((key_ids <= query_ids) & (key_ids < length), 0.0, MASKED)

        settle(0, 3)
        store[0].start()
        for start in range(0, rows, ROW_CHUNK):
            part = slice(start, start + ROW_CHUNK)
            block = x[micro, part, :].astype(F32)
            centred = block - jnp.mean(block, axis=-1, keepdims=True)
            unit = centred * lax.rsqrt(jnp.mean(centred * centred, axis=-1, keepdims=True) + EPSILON)
            attn = (unit * attn_gain[...].astype(F32) + attn_shift[...].astype(F32)).astype(BF16)
            mlp = (unit * mlp_gain[...].astype(F32) + mlp_shift[...].astype(F32)).astype(BF16)
            attn_in[part, :] = attn
            mlp_in[part, :] = mlp
            attn_in_t[:, part] = attn.T
            mlp_in_t[:, part] = mlp.T
        store[1].start()
        store[2].start()

        @pl.when(micro == 0)
        def _():
            loads[1].wait()
            for load in loads[2:]:
                load.start()

        settle(3, 6)
        for start in range(0, 3 * width, QKV_TILE):
            part = slice(start, start + QKV_TILE)
            projected = jnp.dot(attn_in[...], qkv_w[:, part], preferred_element_type=F32)
            turned = (projected + qkv_bias[:, part].astype(F32)).T
            if start >= 2 * width:
                heads_t[part, :] = turned.astype(BF16)
                continue
            for at in range(0, QKV_TILE, HEAD_DIM):
                low, high = turned[at : at + HALF], turned[at + HALF : at + ROTARY]
                heads_t[start + at : start + at + HEAD_DIM, :] = jnp.concatenate(
                    [
                        low * cos_rows - high * sin_rows,
                        high * cos_rows + low * sin_rows,
                        turned[at + ROTARY : at + HEAD_DIM],
                    ],
                    axis=0,
                ).astype(BF16)
        for copy in store[3:6]:
            copy.start()

        def softmax(scores):
            raised = jnp.exp(scores - jnp.max(scores, axis=0, keepdims=True))
            return (raised * (1.0 / jnp.sum(raised, axis=0, keepdims=True))).astype(BF16)

        def scored(head):
            at = head * HEAD_DIM
            query = heads_t[at : at + HEAD_DIM, :] * jnp.bfloat16(SCALE)
            key = heads_t[width + at : width + at + HEAD_DIM, :]
            early = dims_dot(key[:, :half], query[:, :half], 0, 0) + bias[:half, :half]
            return early, dims_dot(key, query[:, half:], 0, 0) + bias[:, half:]

        settle(6, 7)
        settle(8, 9)
        upcoming = scored(0)
        for head in range(HEADS):
            early, late = upcoming
            if head + 1 < HEADS:
                upcoming = scored(head + 1)
            early, late = softmax(early), softmax(late)
            probs[head, :half, :half] = early
            probs[head, :, half:] = late
            place = slice(head * HEAD_DIM, (head + 1) * HEAD_DIM)
            value = heads_t[2 * width + head * HEAD_DIM : 2 * width + (head + 1) * HEAD_DIM, :]
            context_t[place, :half] = jnp.dot(value[:, :half], early, preferred_element_type=F32).astype(BF16)
            context_t[place, half:] = jnp.dot(value, late, preferred_element_type=F32).astype(BF16)
        store[8].start()
        store[6].start()

        @pl.when(micro == 0)
        def _():
            for load in loads[2:]:
                load.wait()

        total[...] = (
            dims_dot(context_t[...], out_w[...], 0, 0)
            + x[micro].astype(F32)
            + (out_bias[...].astype(F32) + down_bias[...].astype(F32))
        )
        settle(7, 8)
        settle(9, len(store))
        for start in range(0, hidden_width, FF_TILE):
            part = slice(start, start + FF_TILE)
            up = jnp.dot(mlp_in[...], up_w[:, part], preferred_element_type=F32)
            up = up + up_bias[:, part].astype(F32)
            share, density = normal_parts(up)
            hidden = (up * share).astype(BF16)
            slope[:, part] = (share + up * density).astype(BF16)
            hidden_t[part, :] = hidden.T
            tile = start // FF_TILE
            store[9 + 2 * tile].start()
            store[10 + 2 * tile].start()
            total[...] += jnp.dot(hidden, down_w[part, :], preferred_element_type=F32)
        y[micro] = total[...].astype(BF16)

        @pl.when(section == 0)
        def _():
            hand_over(micro).start()

        store[7].start()
        return carry

    lax.fori_loop(0, micros, sentence, 0)
    for copy in stores(micros - 1):
        copy.wait()

    @pl.when(section == 0)
    def _():
        for micro in range(micros):
            hand_over(micro).wait_send()


def forward_call(lengths, tokens, weights, tables):
    (
        attn_gain, attn_shift, qkv_weight, qkv_bias, out_weight, out_bias, mlp_gain, mlp_shift, up_weight, up_bias,
        down_weight, down_bias,
    ) = weights
    micros, rows, width = tokens.shape
    hidden_width = up_weight.shape[1]
    wide, tall = (micros, rows, width), (micros, width, rows)
    shapes = [
        wide, wide, tall, tall, tall, tall, tall, (micros, HEADS, rows, rows), tall, (micros, hidden_width, rows),
        (micros, rows, hidden_width),
    ]
    buffers = [
        qkv_weight.shape, out_weight.shape, up_weight.shape, down_weight.shape, wide, (rows, width), (rows, width),
        (width, rows), (width, rows), (3 * width, rows), (width, rows), (hidden_width, rows), (rows, hidden_width),
    ]
    return pl.pallas_call(
        functools.partial(forward_kernel, micros),
        out_shape=[jax.ShapeDtypeStruct(shape, BF16) for shape in shapes],
        in_specs=[SMEM, ANY] + [VMEM] * 10 + [ANY] * 4,
        out_specs=[ANY] * len(shapes),
        scratch_shapes=[pltpu.VMEM(shape, BF16) for shape in buffers]
        + [
            pltpu.VMEM((rows, rows), F32),
            pltpu.VMEM((rows, width), F32),
            pltpu.VMEM((HEADS, rows, rows), BF16),
            pltpu.VMEM(wide, BF16),
            pltpu.SemaphoreType.DMA((5,)),
            pltpu.SemaphoreType.DMA((9 + 2 * (hidden_width // FF_TILE),)),
            pltpu.SemaphoreType.DMA((micros,)),
            pltpu.SemaphoreType.DMA((micros,)),
        ],
        compiler_params=pltpu.CompilerParams(collective_id=1, has_side_effects=True, vmem_limit_bytes=58 << 20),
        cost_estimate=pl.CostEstimate(
            flops=micros * (2 * rows * width * (4 * width + 2 * hidden_width) + 4 * rows * rows * width),
            bytes_accessed=80 << 20,
            transcendentals=micros * rows * hidden_width,
        ),
        name="layer_forward",
    )(
        lengths, tokens, attn_gain, attn_shift, qkv_bias, out_bias, mlp_gain, mlp_shift, up_bias, down_bias,
        *tables, qkv_weight, out_weight, up_weight, down_weight,
    )


def backward_kernel(micros, *refs):
    (
        lengths, cotangent_h, inputs_h, attn_gain, mlp_gain, cosine, sine, qkv_h, out_h, up_h, down_h,
        queries_h, keys_h, values_h, probs_h, context_h, slope_h,
        grad_in_h, grad_heads_h, grad_up_h, grad_out_h, vectors_h,
        qkv_w, out_w, up_w, down_w, queries, keys, values, context, slope, probs, grad_out, x, grad_context,
        grad_up, grad_heads, grad_low, grad_mlp, grad_in, column_sums, vectors,
        in_sems, stash_sems, out_sems, send_sems, recv_sems,
    ) = refs
    section = lax.axis_index("section")
    rows, width = x.shape
    hidden_width = up_w.shape[1]
    half = rows // 2
    other = {"section": 1 - section}

    barrier = pltpu.get_barrier_semaphore()
    pl.semaphore_signal(barrier, inc=1, device_id=other, device_id_type=pl.DeviceIdType.MESH)
    loads = [
        pltpu.make_async_copy(src, dst, in_sems.at[i])
        for i, (src, dst) in enumerate(
            ((cotangent_h, grad_out), (out_h, out_w), (down_h, down_w), (up_h, up_w), (qkv_h, qkv_w))
        )
    ]

    def stash_loads(micro):
        pairs = (
            (slope_h, slope), (values_h, values), (context_h, context), (queries_h, queries), (keys_h, keys),
            (probs_h, probs), (inputs_h, x),
        )
        return [
            pltpu.make_async_copy(src.at[micro], dst, stash_sems.at[i]) for i, (src, dst) in enumerate(pairs)
        ]

    @pl.when(section == 1)
    def _():
        loads[0].start()

    for load in loads[1:3]:
        load.start()
    stash_loads(0)[0].start()
    loads[3].start()
    for load in stash_loads(0)[1:]:
        load.start()
    loads[4].start()
    cos_rows, sin_rows = cosine[...], sine[...]
    attn_column = jnp.broadcast_to(attn_gain[...].astype(F32), (8, width)).T[:, 0:1]
    mlp_column = jnp.broadcast_to(mlp_gain[...].astype(F32), (8, width)).T[:, 0:1]

    def hand_over(micro):
        return pltpu.make_async_remote_copy(
            src_ref=grad_low.at[micro],
            dst_ref=grad_out.at[micro],
            send_sem=send_sems.at[micro],
            recv_sem=recv_sems.at[micro],
            device_id=other,
            device_id_type=pl.DeviceIdType.MESH,
        )

    def stores(micro):
        pairs = [
            (grad_out.at[micro], grad_out_h.at[micro]),
            (grad_heads, grad_heads_h.at[micro]),
            (grad_in, grad_in_h.at[micro]),
            (vectors, vectors_h.at[micro]),
        ]
        for start in range(0, hidden_width, FF_TILE):
            part = slice(start, start + FF_TILE)
            pairs.append((grad_up.at[:, part], grad_up_h.at[micro, :, part]))
        return [pltpu.make_async_copy(src, dst, out_sems.at[i]) for i, (src, dst) in enumerate(pairs)]

    pl.semaphore_wait(barrier, 1)

    def sentence(micro, carry):
        store = stores(micro)
        stash = stash_loads(micro)
        upcoming = stash_loads(micro + 1)

        def settle(first, end):
            @pl.when(micro > 0)
            def _():
                for copy in stores(micro - 1)[first:end]:
                    copy.wait()

        @pl.when((section == 1) & (micro == 0))
        def _():
            loads[0].wait()

        @pl.when(section == 0)
        def _():
            hand_over(micro).wait_recv()

        row_ids = lax.broadcasted_iota(jnp.int32, (rows, 1), 0)
        grad_wide = jnp.where(row_ids < lengths[micro], grad_out[micro].astype(F32), 0.0)
        grad_out[micro] = grad_wide.astype(BF16)

        settle(0, 1)
        settle(3, len(store))
        vectors[...] = jnp.zeros_like(vectors)
        vectors[7:8, :] = jnp.sum(grad_wide, axis=0, keepdims=True)
        store[0].start()

        @pl.when(micro == 0)
        def _():
            loads[1].wait()

        grad_context[...] = dims_dot(out_w[...], grad_out[micro], 1, 1).astype(BF16)

        @pl.when(micro == 0)
        def _():
            loads[2].wait()
            loads[3].wait()

        stash[0].wait()
        for start in range(0, hidden_width, FF_TILE):
            part = slice(start, start + FF_TILE)
            grad_hidden = dims_dot(grad_out[micro], down_w[part, :], 1, 1)
            grad_pre = (grad_hidden * slope[:, part].astype(F32)).astype(BF16)
            grad_up[:, part] = grad_pre
            store[4 + start // FF_TILE].start()
            sums = jnp.sum(grad_pre.astype(F32), axis=0, keepdims=True)
            for at in range(0, FF_TILE, 128):
                row, column = divmod(start + at, width)
                vectors[8 + row : 9 + row, column : column + 128] = sums[:, at : at + 128]
            back = dims_dot(up_w[:, part], grad_pre, 1, 1)
            if start == 0:
                grad_mlp[...] = back
            else:
                grad_mlp[...] += back

        @pl.when(micro < micros - 1)
        def _():
            upcoming[0].start()

        for load in stash[1:6]:
            load.wait()

        def turn_back(grad):
            low, high = grad[:HALF], grad[HALF:ROTARY]
            return jnp.concatenate(
                [low * cos_rows + high * sin_rows, high * cos_rows - low * sin_rows, grad[ROTARY:]], axis=0
            )

        def over_queries(left, early, late):
            both = dims_dot(left[:, half:], late, 1, 1)
            return jnp.concatenate([both[:, :half] + dims_dot(left[:, :half], early, 1, 1), both[:, half:]], axis=1)

        def attend(head):
            at = head * HEAD_DIM
            place = slice(at, at + HEAD_DIM)
            query, key, value, grad = queries[place, :], keys[place, :], values[place, :], grad_context[place, :]
            inner = jnp.sum(grad.astype(F32) * context[place, :].astype(F32), axis=0, keepdims=True)
            early, late = probs[head, :half, :half], probs[head, :, half:]
            grad_early = dims_dot(value[:, :half], grad[:, :half], 0, 0) - inner[:, :half]
            grad_late = dims_dot(value, grad[:, half:], 0, 0) - inner[:, half:]
            grad_early = (early.astype(F32) * grad_early).astype(BF16)
            grad_late = (late.astype(F32) * grad_late).astype(BF16)
            grad_value = over_queries(grad, early, late)
            grad_key = over_queries(query, grad_early, grad_late)
            grad_query = jnp.concatenate(
                [
                    jnp.dot(key[:, :half], grad_early, preferred_element_type=F32),
                    jnp.dot(key, grad_late, preferred_element_type=F32),
                ],
                axis=1,
            )
            grad_heads[place, :] = turn_back(grad_query * SCALE).astype(BF16)
            grad_heads[slice(width + at, width + at + HEAD_DIM), :] = turn_back(grad_key * SCALE).astype(BF16)
            grad_heads[slice(2 * width + at, 2 * width + at + HEAD_DIM), :] = grad_value.astype(BF16)

        settle(1, 2)
        for head in range(HEADS):
            attend(head)
        store[1].start()

        @pl.when(micro < micros - 1)
        def _():
            for load in upcoming[1:6]:
                load.start()

        @pl.when(micro == 0)
        def _():
            loads[4].wait()

        stash[6].wait()
        column_sums[...] = jnp.zeros_like(column_sums)
        settle(2, 3)

        def norm_chunk(index, carry):
            part = pl.ds(pl.multiple_of(index * NORM_CHUNK, NORM_CHUNK), NORM_CHUNK)
            grad_attn_in = jnp.dot(qkv_w[...], grad_heads[:, part], preferred_element_type=F32)
            grad_mlp_in = grad_mlp[:, part]
            turned = x[part, :].astype(F32).T
            centred = turned - jnp.mean(turned, axis=0, keepdims=True)
            inv_spread = lax.rsqrt(jnp.mean(centred * centred, axis=0, keepdims=True) + EPSILON)
            unit = centred * inv_spread
            grad_unit = grad_attn_in * attn_column + grad_mlp_in * mlp_column
            through = inv_spread * (
                grad_unit
                - jnp.mean(grad_unit, axis=0, keepdims=True)
                - unit * jnp.mean(grad_unit * unit, axis=0, keepdims=True)
            )
            exact = through.T + grad_out[micro, part, :].astype(F32)
            low = exact.astype(BF16)
            grad_low[micro, part, :] = low
            grad_in[part, :] = jnp.where(section == 0, exact, low.astype(F32))
            terms = (grad_attn_in * unit, grad_attn_in, grad_mlp_in * unit, grad_mlp_in)
            for i, term in enumerate(terms):
                for at in range(0, NORM_CHUNK, 128):
                    column_sums[i] += term[:, at : at + 128]
            return carry

        lax.fori_loop(0, rows // NORM_CHUNK, norm_chunk, 0)

        @pl.when(section == 1)
        def _():
            hand_over(micro).start()

        @pl.when(micro < micros - 1)
        def _():
            upcoming[6].start()

        store[2].start()
        columns = [jnp.sum(column_sums[i], axis=1, keepdims=True) for i in range(4)]
        for start in range(0, 3 * width, width):
            columns.append(jnp.sum(grad_heads[start : start + width, :].astype(F32), axis=1, keepdims=True))
        lanes = lax.broadcasted_iota(jnp.int32, (width, 128), 1)
        gathered = jnp.zeros((width, 128), F32)
        for lane, column in enumerate(columns):
            gathered = jnp.where(lanes == lane, column, gathered)
        vectors[0:7, :] = gathered.T[0:7, :]
        store[3].start()
        return carry

    lax.fori_loop(0, micros, sentence, 0)
    for copy in stores(micros - 1):
        copy.wait()

    @pl.when(section == 1)
    def _():
        for micro in range(micros):
            hand_over(micro).wait_send()


def backward_call(lengths, cotangent, weights, tables, stash):
    attn_gain, _, qkv_weight, _, out_weight, _, mlp_gain, _, up_weight, _, down_weight, _ = weights
    _, inputs, _, _, queries, keys, values, probs, context, _, slope = stash
    micros, rows, width = cotangent.shape
    hidden_width = up_weight.shape[1]
    vector_rows = 16
    wide, tall = (micros, rows, width), (width, rows)
    outs = [
        jax.ShapeDtypeStruct(wide, F32),
        jax.ShapeDtypeStruct((micros, 3 * width, rows), BF16),
        jax.ShapeDtypeStruct((micros, rows, hidden_width), BF16),
        jax.ShapeDtypeStruct(wide, BF16),
        jax.ShapeDtypeStruct((micros, vector_rows, width), F32),
    ]
    return pl.pallas_call(
        functools.partial(backward_kernel, micros),
        out_shape=outs,
        in_specs=[SMEM] + [ANY] * 2 + [VMEM] * 4 + [ANY] * 10,
        out_specs=[ANY] * len(outs),
        scratch_shapes=[
            pltpu.VMEM(qkv_weight.shape, BF16),
            pltpu.VMEM(out_weight.shape, BF16),
            pltpu.VMEM(up_weight.shape, BF16),
            pltpu.VMEM(down_weight.shape, BF16),
            pltpu.VMEM(tall, BF16),
            pltpu.VMEM(tall, BF16),
            pltpu.VMEM(tall, BF16),
            pltpu.VMEM(tall, BF16),
            pltpu.VMEM((rows, hidden_width), BF16),
            pltpu.VMEM((HEADS, rows, rows), BF16),
            pltpu.VMEM(wide, BF16),
            pltpu.VMEM((rows, width), BF16),
            pltpu.VMEM(tall, BF16),
            pltpu.VMEM((rows, hidden_width), BF16),
            pltpu.VMEM((3 * width, rows), BF16),
            pltpu.VMEM(wide, BF16),
            pltpu.VMEM(tall, F32),
            pltpu.VMEM((rows, width), F32),
            pltpu.VMEM((4, width, 128), F32),
            pltpu.VMEM((vector_rows, width), F32),
            pltpu.SemaphoreType.DMA((5,)),
            pltpu.SemaphoreType.DMA((7,)),
            pltpu.SemaphoreType.DMA((4 + hidden_width // FF_TILE,)),
            pltpu.SemaphoreType.DMA((micros,)),
            pltpu.SemaphoreType.DMA((micros,)),
        ],
        compiler_params=pltpu.CompilerParams(collective_id=2, has_side_effects=True, vmem_limit_bytes=58 << 20),
        cost_estimate=pl.CostEstimate(
            flops=micros * (2 * rows * width * (4 * width + 2 * hidden_width) + 8 * rows * rows * width),
            bytes_accessed=80 << 20,
            transcendentals=0,
        ),
        name="layer_backward",
    )(
        lengths, cotangent, inputs, attn_gain, mlp_gain, *tables, qkv_weight, out_weight, up_weight, down_weight,
        queries, keys, values, probs, context, slope,
    )


def partner(axis, bit):
    index = lax.axis_index(axis)
    own_bit = (index // bit) % 2
    return {axis: index + bit - 2 * bit * own_bit}, own_bit


def piece_plan(width, hidden_width, piece):
    counts = [width // piece, hidden_width // piece, hidden_width // piece, 3 * width // piece]
    starts = [0]
    for count in counts:
        starts.append(starts[-1] + count)
    return starts


def reduce_kernel(bits, piece, *refs):
    (
        context_h, hidden_h, mlp_in_h, attn_in_h, grad_out_h, grad_up_h, grad_heads_h, vectors_h,
        qkv_o, out_o, up_o, down_o, vectors_o,
        left, right, heads, vectors, own, final, from_first, *rest,
    ) = refs
    from_dp, rest = rest[:bits], rest[bits:]
    (
        from_second, vector_sum, from_vector,
        in_sems, send_sems, recv_sems, vector_send, vector_recv, out_sems,
    ) = rest
    micros, devices, share, rows = attn_in_h.shape
    width = devices * share
    hidden_width = grad_up_h.shape[2]
    groups = hidden_width // width
    out_at, down_at, up_at, qkv_at, pieces = piece_plan(width, hidden_width, piece)
    across = width // piece

    barrier = pltpu.get_barrier_semaphore()
    dp_peers = [partner("dp", 1 << bit) for bit in range(bits)]
    replica_peers = [partner("replica", 1), partner("replica", 2)]
    for device, _ in dp_peers + replica_peers:
        pl.semaphore_signal(barrier, inc=1, device_id=device, device_id_type=pl.DeviceIdType.MESH)

    wide = hidden_width + width
    loads = [
        [(context_h, left.at[0]), (grad_out_h, right.at[:, :, 0:width]), (vectors_h, vectors)],
        [(hidden_h.at[:, :, group], left.at[3 + group]) for group in range(groups)],
        [(mlp_in_h, left.at[1]), (grad_up_h, right.at[:, :, width:wide])],
        [(attn_in_h, left.at[2]), (grad_heads_h, heads)],
    ]
    copies, count = [], 0
    for group in loads:
        copies.append([])
        for src, dst in group:
            copies[-1].append(pltpu.make_async_copy(src, dst, in_sems.at[count]))
            count += 1
    for copy in copies[0]:
        copy.start()
    for copy in copies[0]:
        copy.wait()
    for group in copies[1:]:
        for copy in group:
            copy.start()
    vector_sum[0] = jnp.sum(vectors[...], axis=0)
    pl.semaphore_wait(barrier, len(dp_peers) + len(replica_peers))

    dp_bits = [own_bit for _, own_bit in dp_peers]

    def keep(k, depth, first_bit=None, second_bit=None, flip=None):
        index = [k] + [slice(None)] * (bits - depth)
        for bit in reversed(range(depth)):
            index.append(1 - dp_bits[bit] if flip == bit else dp_bits[bit])
        if first_bit is not None:
            index.append(first_bit)
        if second_bit is not None:
            index.append(second_bit)
        return tuple(index)

    def transfers(k, turned):
        (first, first_bit), (second, second_bit) = replica_peers[::-1] if turned else replica_peers
        steps = [
            (own.at[keep(k, 0, 1 - first_bit)], from_first.at[k], first, own.at[keep(k, 0, first_bit)]),
        ]
        for bit in range(bits):
            steps.append(
                (
                    own.at[keep(k, bit + 1, first_bit, flip=bit)],
                    from_dp[bit].at[k],
                    dp_peers[bit][0],
                    own.at[keep(k, bit + 1, first_bit)],
                )
            )
        mine = final.at[k, first_bit, second_bit]
        steps.append(
            (
                own.at[keep(k, bits, first_bit, 1 - second_bit)],
                from_second.at[k],
                second,
                own.at[keep(k, bits, first_bit, second_bit)],
            )
        )
        steps.append((mine, mine, second, None))
        steps.append((final.at[k, first_bit], final.at[k, first_bit], first, None))
        return steps, mine

    def copy_of(k, stage, step):
        src, dst, device, _ = step
        return pltpu.make_async_remote_copy(
            src_ref=src,
            dst_ref=dst,
            send_sem=send_sems.at[k, stage],
            recv_sem=recv_sems.at[k, stage],
            device_id=device,
            device_id_type=pl.DeviceIdType.MESH,
        )

    n_steps = bits + 4

    def advance(k, stage, turned):
        steps, mine = transfers(k, turned)
        if stage > 0:
            step = steps[stage - 1]
            copy_of(k, stage - 1, step).wait()
            if step[3] is not None:
                total = step[3][...].astype(F32) + step[1][...].astype(F32)
                if stage == bits + 2:
                    mine[...] = total.astype(BF16)
                else:
                    step[3][...] = total.astype(BF16)
        if stage < n_steps:
            copy_of(k, stage, steps[stage]).start()

    def advance_either(k, stage):
        for turned in (False, True):

            @pl.when(k % 2 == int(turned))
            def _():
                advance(k, stage, turned)

    shape = own.shape[1:]

    def panel(index, micro):
        return left[index, micro].reshape(width, rows)

    def set_own(k, index, columns):
        value = columns(0, panel(index, 0))
        for micro in range(1, micros):
            value = value + columns(micro, panel(index, micro))
        own[k] = value.astype(BF16).reshape(shape)

    def lanes(index):
        return pl.ds(pl.multiple_of(index * piece, 128), piece)

    def compute(k):
        @pl.when(k < down_at)
        def _():
            part = lanes(k)
            set_own(k, 0, lambda micro, block: dims_dot(block, right[micro, :, part], 1, 0))

        @pl.when((k >= down_at) & (k < up_at))
        def _():
            part = lanes((k - down_at) % across)
            set_own(
                k, 3 + (k - down_at) // across, lambda micro, block: dims_dot(block, right[micro, :, part], 1, 0)
            )

        @pl.when((k >= up_at) & (k < qkv_at))
        def _():
            part = lanes(across + k - up_at)
            set_own(k, 1, lambda micro, block: dims_dot(block, right[micro, :, part], 1, 0))

        @pl.when(k >= qkv_at)
        def _():
            part = lanes(k - qkv_at)
            set_own(k, 2, lambda micro, block: dims_dot(block, heads[micro, part, :], 1, 1))

    def out_copy(k, kind):
        if kind == "down":
            target = down_o.at[(k - down_at) // across, :, :, :, lanes((k - down_at) % across)]
        else:
            ref, start = {"out": (out_o, out_at), "up": (up_o, up_at), "qkv": (qkv_o, qkv_at)}[kind]
            target = ref.at[:, :, :, lanes(k - start)]
        return pltpu.make_async_copy(final.at[k], target, out_sems.at[k])

    ranges = {"out": (out_at, down_at), "down": (down_at, up_at), "up": (up_at, qkv_at), "qkv": (qkv_at, pieces)}

    def stored(k, do):
        for kind, (first, end) in ranges.items():

            @pl.when((k >= first) & (k < end))
            def _():
                do(out_copy(k, kind))

    vector_peers = dp_peers + replica_peers

    def vector_copy(i):
        return pltpu.make_async_remote_copy(
            src_ref=vector_sum.at[i],
            dst_ref=from_vector.at[i],
            send_sem=vector_send.at[i],
            recv_sem=vector_recv.at[i],
            device_id=vector_peers[i][0],
            device_id_type=pl.DeviceIdType.MESH,
        )

    lags = [0]
    for stage in range(n_steps):
        lags.append(lags[-1] + 3)

    def turn(t, carry):
        for at, group in zip((down_at, up_at, qkv_at), copies[1:]):

            @pl.when(t == at)
            def _():
                for copy in group:
                    copy.wait()

        @pl.when(t < pieces)
        def _():
            compute(t)

        for stage in range(n_steps + 1):
            k = t - lags[stage]

            @pl.when((k >= 0) & (k < pieces))
            def _():
                advance_either(k, stage)
                if stage == n_steps:
                    stored(k, lambda copy: copy.start())

        for i in range(len(vector_peers) + 1):

            @pl.when(t == 4 * i)
            def _():
                if i > 0:
                    vector_copy(i - 1).wait()
                    vector_sum[i] = vector_sum[i - 1] + from_vector[i - 1]
                if i < len(vector_peers):
                    vector_copy(i).start()
                else:
                    pltpu.make_async_copy(vector_sum.at[i], vectors_o, out_sems.at[pieces]).start()

        return carry

    lax.fori_loop(0, pieces + lags[-1], turn, 0)

    def finish(k, carry):
        stored(k, lambda copy: copy.wait())
        return carry

    lax.fori_loop(0, pieces, finish, 0)
    pltpu.make_async_copy(vector_sum.at[len(vector_peers)], vectors_o, out_sems.at[pieces]).wait()


def reduce_call(stash, kept):
    _, _, attn_in, mlp_in, _, _, _, _, context, hidden, _ = stash
    _, grad_heads, grad_up, grad_out, vectors = kept
    micros, width, rows = attn_in.shape
    hidden_width = hidden.shape[1]
    groups = hidden_width // width
    devices = lax.axis_size("dp")
    bits = devices.bit_length() - 1
    share, quarter = width // devices, width // devices // 4
    piece = PIECE
    pieces = piece_plan(width, hidden_width, piece)[-1]
    loads = 6 + groups + 1
    tall = (micros, devices, share, rows)
    halves = [2] * bits
    steps = bits + 4
    peers = bits + 2
    shape = lambda columns: jax.ShapeDtypeStruct((2, 2, quarter, columns), BF16)
    outs = pl.pallas_call(
        functools.partial(reduce_kernel, bits, piece),
        out_shape=[
            shape(3 * width),
            shape(width),
            shape(hidden_width),
            jax.ShapeDtypeStruct((groups, 2, 2, quarter, width), BF16),
            jax.ShapeDtypeStruct(vectors.shape[1:], F32),
        ],
        in_specs=[ANY] * 8,
        out_specs=[ANY] * 5,
        scratch_shapes=[
            pltpu.VMEM((3 + groups, *tall), BF16),
            pltpu.VMEM((micros, rows, width + hidden_width), BF16),
            pltpu.VMEM(grad_heads.shape, BF16),
            pltpu.VMEM(vectors.shape, F32),
            pltpu.VMEM((pieces, *halves, 2, 2, quarter, piece), BF16),
            pltpu.VMEM((pieces, 2, 2, quarter, piece), BF16),
            pltpu.VMEM((pieces, *halves, 2, quarter, piece), BF16),
            *[pltpu.VMEM((pieces, *halves[bit + 1 :], 2, quarter, piece), BF16) for bit in range(bits)],
            pltpu.VMEM((pieces, quarter, piece), BF16),
            pltpu.VMEM((peers + 1, *vectors.shape[1:]), F32),
            pltpu.VMEM((peers, *vectors.shape[1:]), F32),
            pltpu.SemaphoreType.DMA((loads,)),
            pltpu.SemaphoreType.DMA((pieces, steps)),
            pltpu.SemaphoreType.DMA((pieces, steps)),
            pltpu.SemaphoreType.DMA((peers,)),
            pltpu.SemaphoreType.DMA((peers,)),
            pltpu.SemaphoreType.DMA((pieces + 1,)),
        ],
        compiler_params=pltpu.CompilerParams(
            collective_id=0, has_side_effects=True, vmem_limit_bytes=60 << 20
        ),
        cost_estimate=pl.CostEstimate(
            flops=2 * micros * rows * width * (4 * width + 2 * hidden_width),
            bytes_accessed=30 << 20,
            transcendentals=0,
        ),
        name="weight_gradients",
    )(
        context.reshape(tall),
        hidden.reshape(micros, devices, groups, share, rows),
        mlp_in.reshape(tall),
        attn_in.reshape(tall),
        grad_out,
        grad_up,
        grad_heads,
        vectors,
    )
    qkv, out, up, down, sums = outs
    scattered = [array.reshape(-1, array.shape[-1]) for array in (qkv, out, up, down)]
    return scattered, sums


def finish_kernel(grad_scale, *refs):
    vectors = refs[0]
    sources = refs[1:7]
    targets = refs[7:13]
    vector_outs = refs[13:21]
    held, wide = refs[21:27], refs[27:31]
    in_sems, out_sems = refs[31:]
    ready = (*held[:2], *wide)
    loads = [pltpu.make_async_copy(src, dst, in_sems.at[i]) for i, (src, dst) in enumerate(zip(sources, held))]
    stores = [pltpu.make_async_copy(src, dst, out_sems.at[i]) for i, (src, dst) in enumerate(zip(ready, targets))]
    for load in loads:
        load.start()
    devices = lax.axis_size("dp")
    mine = lax.axis_index("dp")
    width = vectors.shape[1]
    first_rows = (0, 1, 4, 7, 2, 3, 8, 7)
    for device in range(devices):

        @pl.when(mine == device)
        def _():
            for out, first in zip(vector_outs, first_rows):
                at, size, filled = device * out.shape[1], out.shape[1], 0
                while filled < size:
                    row, column = divmod(at + filled, width)
                    count = min(size - filled, width - column)
                    piece = vectors[first + row : first + row + 1, column : column + count]
                    out[:, filled : filled + count] = piece * grad_scale
                    filled += count

    for i, (load, store) in enumerate(zip(loads, stores)):
        load.wait()
        if i >= 2:
            wide[i - 2][...] = held[i][...].astype(F32) * grad_scale
        store.start()
    for store in stores:
        store.wait()


def finish_call(grad_scale, shares, vectors, outputs, grad_in, hidden_width):
    width = vectors.shape[1]
    devices = lax.axis_size("dp")
    sizes = [width, width, 3 * width, width, width, width, hidden_width, width]
    matrices = [jax.ShapeDtypeStruct(share.shape, F32) for share in shares]
    results = pl.pallas_call(
        functools.partial(finish_kernel, grad_scale),
        out_shape=[
            jax.ShapeDtypeStruct(outputs.shape, BF16),
            jax.ShapeDtypeStruct(grad_in.shape, F32),
            *matrices,
            *[jax.ShapeDtypeStruct((1, size // devices), F32) for size in sizes],
        ],
        in_specs=[VMEM] + [ANY] * 6,
        out_specs=[ANY] * 6 + [VMEM] * 8,
        scratch_shapes=[pltpu.VMEM(array.shape, array.dtype) for array in (outputs, grad_in, *shares)]
        + [pltpu.VMEM(share.shape, F32) for share in shares]
        + [pltpu.SemaphoreType.DMA((6,)), pltpu.SemaphoreType.DMA((6,))],
        compiler_params=pltpu.CompilerParams(vmem_limit_bytes=60 << 20),
        name="finish",
    )(vectors, outputs, grad_in, *shares)
    return results[:2], results[2:6], results[6:]


def rotary_tables(seq_len):
    positions = jnp.arange(seq_len, dtype=F32)
    inverse = 1.0 / ROTARY_BASE ** (jnp.arange(0, ROTARY, 2, dtype=F32) / ROTARY)
    angles = inverse[:, None] * positions[None, :]
    return jnp.cos(angles), jnp.sin(angles)


def summed(share):
    part = lax.psum_scatter(share.astype(BF16), "dp", scatter_dimension=0, tiled=True)
    return lax.psum(part, "replica").astype(F32)


def in_pieces(width):
    devices = lax.axis_size("dp")
    return devices & (devices - 1) == 0 and lax.axis_size("replica") == 4 and width % (64 * devices) == 0


def local_totals(stash, kept):
    _, _, attn_in, mlp_in, _, _, _, _, context, hidden, _ = stash
    _, grad_heads, grad_up, grad_out, vectors = kept
    vector_sums = jnp.sum(vectors, axis=0)
    groups = hidden.shape[1] // attn_in.shape[1]
    return (
        vector_sums[0],
        vector_sums[1],
        jnp.einsum("mdr,mer->de", attn_in, grad_heads, preferred_element_type=F32),
        vector_sums[4:7].reshape(-1),
        jnp.einsum("mer,mrd->ed", context, grad_out, preferred_element_type=F32),
        vector_sums[7],
        vector_sums[2],
        vector_sums[3],
        jnp.einsum("mdr,mrf->df", mlp_in, grad_up, preferred_element_type=F32),
        vector_sums[8 : 8 + groups].reshape(-1),
        jnp.einsum("mfr,mrd->fd", hidden, grad_out, preferred_element_type=F32),
        vector_sums[7],
    )


def body(tokens, cotangent, lengths, *weights):
    weights = tuple(array if array.ndim == 2 else array[0] for array in weights)
    micros = lengths.shape[0]
    width = tokens.shape[1]
    rows = tokens.shape[0] // micros
    tables = rotary_tables(rows)
    stash = forward_call(lengths, tokens.reshape(micros, rows, width), weights, tables)
    kept = backward_call(lengths, cotangent.reshape(micros, rows, width), weights, tables, stash)
    grad_scale = float(tokens.shape[0] * lax.axis_size("dp") * lax.axis_size("replica")) ** (-0.5)
    if in_pieces(width):
        shares, vectors = reduce_call(stash, kept)
        (outputs, grad_in), matrices, parts = finish_call(
            grad_scale, shares, vectors, stash[0], kept[0], weights[8].shape[1]
        )
        qkv, out, up, down = (matrix[None] for matrix in matrices)
        gain, shift, qkv_bias, out_bias, mlp_gain, mlp_shift, up_bias, down_bias = parts
        grads = (gain, shift, qkv, qkv_bias, out, out_bias, mlp_gain, mlp_shift, up, up_bias, down, down_bias)
    else:
        outputs, grad_in = stash[0], kept[0]
        grads = tuple(summed(total)[None] * grad_scale for total in local_totals(stash, kept))
    return (outputs.reshape(1, micros * rows, width), grad_in.reshape(1, micros * rows, width), *grads)


def solution(mesh):
    rows = P(("dp", "replica"), None)
    vector, matrix = P("section", None), P("section", None, None)
    out_rows = P("section", ("dp", "replica"), None)
    vector_out, matrix_out = P("section", "dp"), P("section", "dp", None)
    return jax.shard_map(
        body,
        mesh=mesh,
        in_specs=(
            rows, rows, P(("dp", "replica")), vector, vector, matrix, vector, matrix, vector, vector, vector, matrix,
            vector, matrix, vector,
        ),
        out_specs=(
            out_rows, out_rows, vector_out, vector_out, matrix_out, vector_out, matrix_out, vector_out, vector_out,
            vector_out, matrix_out, vector_out, matrix_out, vector_out,
        ),
        check_vma=False,
    )
```

```python
import functools

import jax
import jax.numpy as jnp
import numpy as np
from jax import lax
from jax.experimental import pallas as pl
from jax.experimental.pallas import tpu as pltpu
from jax.sharding import PartitionSpec as P

HEADS = 12
HEAD_DIM = 64
ROTARY = 16
HALF = ROTARY // 2
EPSILON = 1e-05
ROTARY_BASE = 10000.0
MASKED = -1e30
LOG2_E = 1.4426950408889634
LOG2_DENSITY = -1.3257480647361593
SCALE = HEAD_DIM**-0.5
F32 = jnp.float32
BF16 = jnp.bfloat16
ANY = pl.BlockSpec(memory_space=pl.ANY)
VMEM = pl.BlockSpec(memory_space=pltpu.VMEM)
SMEM = pl.BlockSpec(memory_space=pltpu.SMEM)
ROW_CHUNK = 128
NORM_CHUNK = 256
QKV_TILE = 256
FF_TILE = 768
PIECE = 384


def dims_dot(left, right, left_dim, right_dim):
    return lax.dot_general(
        left, right, (((left_dim,), (right_dim,)), ((), ())), preferred_element_type=F32
    )


def normal_parts(v):
    scaled = v * 0.7071067811865476
    bell = jnp.exp2(LOG2_DENSITY - scaled * (scaled * LOG2_E))
    return 0.5 + 0.5 * lax.erf(scaled), bell


def forward_kernel(micros, *refs):
    (
        lengths, tokens_h, attn_gain, attn_shift, qkv_bias, out_bias, mlp_gain, mlp_shift, up_bias, down_bias,
        cosine, sine, qkv_h, out_h, up_h, down_h,
        y_h, inputs_h, attn_in_h, mlp_in_h, queries_h, keys_h, values_h, probs_h, context_h, hidden_h, slope_h,
        qkv_w, out_w, up_w, down_w, x, attn_in, mlp_in, attn_in_t, mlp_in_t, heads_t, context_t, hidden_t, slope,
        bias, total, probs, y, in_sems, out_sems, send_sems, recv_sems,
    ) = refs
    section = lax.axis_index("section")
    rows, width = attn_in.shape
    hidden_width = up_w.shape[1]
    half = rows // 2
    other = {"section": 1 - section}

    barrier = pltpu.get_barrier_semaphore()
    pl.semaphore_signal(barrier, inc=1, device_id=other, device_id_type=pl.DeviceIdType.MESH)
    loads = [
        pltpu.make_async_copy(src, dst, in_sems.at[i])
        for i, (src, dst) in enumerate(
            ((tokens_h, x), (qkv_h, qkv_w), (out_h, out_w), (up_h, up_w), (down_h, down_w))
        )
    ]

    @pl.when(section == 0)
    def _():
        loads[0].start()

    loads[1].start()
    probs[:, half:, :half] = jnp.zeros((probs.shape[0], half, half), BF16)
    cos_rows, sin_rows = cosine[...], sine[...]

    def hand_over(micro):
        return pltpu.make_async_remote_copy(
            src_ref=y.at[micro],
            dst_ref=x.at[micro],
            send_sem=send_sems.at[micro],
            recv_sem=recv_sems.at[micro],
            device_id=other,
            device_id_type=pl.DeviceIdType.MESH,
        )

    def stores(micro):
        pairs = [
            (x.at[micro], inputs_h.at[micro]),
            (attn_in_t, attn_in_h.at[micro]),
            (mlp_in_t, mlp_in_h.at[micro]),
            (heads_t.at[0:width], queries_h.at[micro]),
            (heads_t.at[width : 2 * width], keys_h.at[micro]),
            (heads_t.at[2 * width :], values_h.at[micro]),
            (context_t, context_h.at[micro]),
            (y.at[micro], y_h.at[micro]),
            (probs, probs_h.at[micro]),
        ]
        for start in range(0, hidden_width, FF_TILE):
            part = slice(start, start + FF_TILE)
            pairs.append((hidden_t.at[part], hidden_h.at[micro, part]))
            pairs.append((slope.at[:, part], slope_h.at[micro, :, part]))
        return [pltpu.make_async_copy(src, dst, out_sems.at[i]) for i, (src, dst) in enumerate(pairs)]

    pl.semaphore_wait(barrier, 1)

    def sentence(micro, carry):
        store = stores(micro)

        def settle(first, end):
            @pl.when(micro > 0)
            def _():
                for copy in stores(micro - 1)[first:end]:
                    copy.wait()

        length = lengths[micro]
        key_ids = lax.broadcasted_iota(jnp.int32, (rows, rows), 0)
        query_ids = lax.broadcasted_iota(jnp.int32, (rows, rows), 1)
        bias[...] = jnp.where((key_ids <= query_ids) & (key_ids < length), 0.0, MASKED)

        settle(0, 3)

        @pl.when((section == 0) & (micro == 0))
        def _():
            loads[0].wait()

        @pl.when(section == 1)
        def _():
            hand_over(micro).wait_recv()

        store[0].start()
        for start in range(0, rows, ROW_CHUNK):
            part = slice(start, start + ROW_CHUNK)
            block = x[micro, part, :].astype(F32)
            centred = block - jnp.mean(block, axis=-1, keepdims=True)
            unit = centred * lax.rsqrt(jnp.mean(centred * centred, axis=-1, keepdims=True) + EPSILON)
            attn = (unit * attn_gain[...].astype(F32) + attn_shift[...].astype(F32)).astype(BF16)
            mlp = (unit * mlp_gain[...].astype(F32) + mlp_shift[...].astype(F32)).astype(BF16)
            attn_in[part, :] = attn
            mlp_in[part, :] = mlp
            attn_in_t[:, part] = attn.T
            mlp_in_t[:, part] = mlp.T
        store[1].start()
        store[2].start()

        @pl.when(micro == 0)
        def _():
            loads[1].wait()
            for load in loads[2:]:
                load.start()

        settle(3, 6)
        for start in range(0, 3 * width, QKV_TILE):
            part = slice(start, start + QKV_TILE)
            projected = jnp.dot(attn_in[...], qkv_w[:, part], preferred_element_type=F32)
            turned = (projected + qkv_bias[:, part].astype(F32)).T
            if start >= 2 * width:
                heads_t[part, :] = turned.astype(BF16)
                continue
            for at in range(0, QKV_TILE, HEAD_DIM):
                low, high = turned[at : at + HALF], turned[at + HALF : at + ROTARY]
                heads_t[start + at : start + at + HEAD_DIM, :] = jnp.concatenate(
                    [
                        low * cos_rows - high * sin_rows,
                        high * cos_rows + low * sin_rows,
                        turned[at + ROTARY : at + HEAD_DIM],
                    ],
                    axis=0,
                ).astype(BF16)
        for copy in store[3:6]:
            copy.start()

        def softmax(scores):
            raised = jnp.exp(scores - jnp.max(scores, axis=0, keepdims=True))
            return (raised * (1.0 / jnp.sum(raised, axis=0, keepdims=True))).astype(BF16)

        def scored(head):
            at = head * HEAD_DIM
            query = heads_t[at : at + HEAD_DIM, :] * jnp.bfloat16(SCALE)
            key = heads_t[width + at : width + at + HEAD_DIM, :]
            early = dims_dot(key[:, :half], query[:, :half], 0, 0) + bias[:half, :half]
            return early, dims_dot(key, query[:, half:], 0, 0) + bias[:, half:]

        settle(6, 7)
        settle(8, 9)
        upcoming = scored(0)
        for head in range(HEADS):
            early, late = upcoming
            if head + 1 < HEADS:
                upcoming = scored(head + 1)
            early, late = softmax(early), softmax(late)
            probs[head, :half, :half] = early
            probs[head, :, half:] = late
            place = slice(head * HEAD_DIM, (head + 1) * HEAD_DIM)
            value = heads_t[2 * width + head * HEAD_DIM : 2 * width + (head + 1) * HEAD_DIM, :]
            context_t[place, :half] = jnp.dot(value[:, :half], early, preferred_element_type=F32).astype(BF16)
            context_t[place, half:] = jnp.dot(value, late, preferred_element_type=F32).astype(BF16)
        store[8].start()
        store[6].start()

        @pl.when(micro == 0)
        def _():
            for load in loads[2:]:
                load.wait()

        total[...] = (
            dims_dot(context_t[...], out_w[...], 0, 0)
            + x[micro].astype(F32)
            + (out_bias[...].astype(F32) + down_bias[...].astype(F32))
        )
        settle(7, 8)
        settle(9, len(store))
        for start in range(0, hidden_width, FF_TILE):
            part = slice(start, start + FF_TILE)
            up = jnp.dot(mlp_in[...], up_w[:, part], preferred_element_type=F32)
            up = up + up_bias[:, part].astype(F32)
            share, density = normal_parts(up)
            hidden = (up * share).astype(BF16)
            slope[:, part] = (share + up * density).astype(BF16)
            hidden_t[part, :] = hidden.T
            tile = start // FF_TILE
            store[9 + 2 * tile].start()
            store[10 + 2 * tile].start()
            total[...] += jnp.dot(hidden, down_w[part, :], preferred_element_type=F32)
        y[micro] = total[...].astype(BF16)

        @pl.when(section == 0)
        def _():
            hand_over(micro).start()

        store[7].start()
        return carry

    lax.fori_loop(0, micros, sentence, 0)
    for copy in stores(micros - 1):
        copy.wait()

    @pl.when(section == 0)
    def _():
        for micro in range(micros):
            hand_over(micro).wait_send()


def forward_call(lengths, tokens, weights, tables):
    (
        attn_gain, attn_shift, qkv_weight, qkv_bias, out_weight, out_bias, mlp_gain, mlp_shift, up_weight, up_bias,
        down_weight, down_bias,
    ) = weights
    micros, rows, width = tokens.shape
    hidden_width = up_weight.shape[1]
    wide, tall = (micros, rows, width), (micros, width, rows)
    shapes = [
        wide, wide, tall, tall, tall, tall, tall, (micros, HEADS, rows, rows), tall, (micros, hidden_width, rows),
        (micros, rows, hidden_width),
    ]
    buffers = [
        qkv_weight.shape, out_weight.shape, up_weight.shape, down_weight.shape, wide, (rows, width), (rows, width),
        (width, rows), (width, rows), (3 * width, rows), (width, rows), (hidden_width, rows), (rows, hidden_width),
    ]
    return pl.pallas_call(
        functools.partial(forward_kernel, micros),
        out_shape=[jax.ShapeDtypeStruct(shape, BF16) for shape in shapes],
        in_specs=[SMEM, ANY] + [VMEM] * 10 + [ANY] * 4,
        out_specs=[ANY] * len(shapes),
        scratch_shapes=[pltpu.VMEM(shape, BF16) for shape in buffers]
        + [
            pltpu.VMEM((rows, rows), F32),
            pltpu.VMEM((rows, width), F32),
            pltpu.VMEM((HEADS, rows, rows), BF16),
            pltpu.VMEM(wide, BF16),
            pltpu.SemaphoreType.DMA((5,)),
            pltpu.SemaphoreType.DMA((9 + 2 * (hidden_width // FF_TILE),)),
            pltpu.SemaphoreType.DMA((micros,)),
            pltpu.SemaphoreType.DMA((micros,)),
        ],
        compiler_params=pltpu.CompilerParams(collective_id=1, has_side_effects=True, vmem_limit_bytes=58 << 20),
        cost_estimate=pl.CostEstimate(
            flops=micros * (2 * rows * width * (4 * width + 2 * hidden_width) + 4 * rows * rows * width),
            bytes_accessed=80 << 20,
            transcendentals=micros * rows * hidden_width,
        ),
        name="layer_forward",
    )(
        lengths, tokens, attn_gain, attn_shift, qkv_bias, out_bias, mlp_gain, mlp_shift, up_bias, down_bias,
        *tables, qkv_weight, out_weight, up_weight, down_weight,
    )


def backward_kernel(micros, *refs):
    (
        lengths, cotangent_h, inputs_h, attn_gain, mlp_gain, cosine, sine, qkv_h, out_h, up_h, down_h,
        queries_h, keys_h, values_h, probs_h, context_h, slope_h,
        grad_in_h, grad_heads_h, grad_up_h, grad_out_h, vectors_h,
        qkv_w, out_w, up_w, down_w, queries, keys, values, context, slope, probs, grad_out, x, grad_context,
        grad_up, grad_heads, grad_low, grad_mlp, grad_in, column_sums, vectors,
        in_sems, stash_sems, out_sems, send_sems, recv_sems,
    ) = refs
    section = lax.axis_index("section")
    rows, width = x.shape
    hidden_width = up_w.shape[1]
    half = rows // 2
    other = {"section": 1 - section}

    barrier = pltpu.get_barrier_semaphore()
    pl.semaphore_signal(barrier, inc=1, device_id=other, device_id_type=pl.DeviceIdType.MESH)
    loads = [
        pltpu.make_async_copy(src, dst, in_sems.at[i])
        for i, (src, dst) in enumerate(
            ((cotangent_h, grad_out), (out_h, out_w), (down_h, down_w), (up_h, up_w), (qkv_h, qkv_w))
        )
    ]

    def stash_loads(micro):
        pairs = (
            (slope_h, slope), (values_h, values), (context_h, context), (queries_h, queries), (keys_h, keys),
            (probs_h, probs), (inputs_h, x),
        )
        return [
            pltpu.make_async_copy(src.at[micro], dst, stash_sems.at[i]) for i, (src, dst) in enumerate(pairs)
        ]

    @pl.when(section == 1)
    def _():
        loads[0].start()

    for load in loads[1:3]:
        load.start()
    stash_loads(0)[0].start()
    loads[3].start()
    for load in stash_loads(0)[1:]:
        load.start()
    loads[4].start()
    cos_rows, sin_rows = cosine[...], sine[...]
    attn_column = jnp.broadcast_to(attn_gain[...].astype(F32), (8, width)).T[:, 0:1]
    mlp_column = jnp.broadcast_to(mlp_gain[...].astype(F32), (8, width)).T[:, 0:1]

    def hand_over(micro):
        return pltpu.make_async_remote_copy(
            src_ref=grad_low.at[micro],
            dst_ref=grad_out.at[micro],
            send_sem=send_sems.at[micro],
            recv_sem=recv_sems.at[micro],
            device_id=other,
            device_id_type=pl.DeviceIdType.MESH,
        )

    def stores(micro):
        pairs = [
            (grad_out.at[micro], grad_out_h.at[micro]),
            (grad_heads, grad_heads_h.at[micro]),
            (grad_in, grad_in_h.at[micro]),
            (vectors, vectors_h.at[micro]),
        ]
        for start in range(0, hidden_width, FF_TILE):
            part = slice(start, start + FF_TILE)
            pairs.append((grad_up.at[:, part], grad_up_h.at[micro, :, part]))
        return [pltpu.make_async_copy(src, dst, out_sems.at[i]) for i, (src, dst) in enumerate(pairs)]

    pl.semaphore_wait(barrier, 1)

    def sentence(micro, carry):
        store = stores(micro)
        stash = stash_loads(micro)
        upcoming = stash_loads(micro + 1)

        def settle(first, end):
            @pl.when(micro > 0)
            def _():
                for copy in stores(micro - 1)[first:end]:
                    copy.wait()

        @pl.when((section == 1) & (micro == 0))
        def _():
            loads[0].wait()

        @pl.when(section == 0)
        def _():
            hand_over(micro).wait_recv()

        row_ids = lax.broadcasted_iota(jnp.int32, (rows, 1), 0)
        grad_wide = jnp.where(row_ids < lengths[micro], grad_out[micro].astype(F32), 0.0)
        grad_out[micro] = grad_wide.astype(BF16)

        settle(0, 1)
        settle(3, len(store))
        vectors[...] = jnp.zeros_like(vectors)
        vectors[7:8, :] = jnp.sum(grad_wide, axis=0, keepdims=True)
        store[0].start()

        @pl.when(micro == 0)
        def _():
            loads[1].wait()

        grad_context[...] = dims_dot(out_w[...], grad_out[micro], 1, 1).astype(BF16)

        @pl.when(micro == 0)
        def _():
            loads[2].wait()
            loads[3].wait()

        stash[0].wait()
        for start in range(0, hidden_width, FF_TILE):
            part = slice(start, start + FF_TILE)
            grad_hidden = dims_dot(grad_out[micro], down_w[part, :], 1, 1)
            grad_pre = (grad_hidden * slope[:, part].astype(F32)).astype(BF16)
            grad_up[:, part] = grad_pre
            store[4 + start // FF_TILE].start()
            sums = jnp.sum(grad_pre.astype(F32), axis=0, keepdims=True)
            for at in range(0, FF_TILE, 128):
                row, column = divmod(start + at, width)
                vectors[8 + row : 9 + row, column : column + 128] = sums[:, at : at + 128]
            back = dims_dot(up_w[:, part], grad_pre, 1, 1)
            if start == 0:
                grad_mlp[...] = back
            else:
                grad_mlp[...] += back

        @pl.when(micro < micros - 1)
        def _():
            upcoming[0].start()

        for load in stash[1:6]:
            load.wait()

        def turn_back(grad):
            low, high = grad[:HALF], grad[HALF:ROTARY]
            return jnp.concatenate(
                [low * cos_rows + high * sin_rows, high * cos_rows - low * sin_rows, grad[ROTARY:]], axis=0
            )

        def over_queries(left, early, late):
            both = dims_dot(left[:, half:], late, 1, 1)
            return jnp.concatenate([both[:, :half] + dims_dot(left[:, :half], early, 1, 1), both[:, half:]], axis=1)

        def attend(head):
            at = head * HEAD_DIM
            place = slice(at, at + HEAD_DIM)
            query, key, value, grad = queries[place, :], keys[place, :], values[place, :], grad_context[place, :]
            inner = jnp.sum(grad.astype(F32) * context[place, :].astype(F32), axis=0, keepdims=True)
            early, late = probs[head, :half, :half], probs[head, :, half:]
            grad_early = dims_dot(value[:, :half], grad[:, :half], 0, 0) - inner[:, :half]
            grad_late = dims_dot(value, grad[:, half:], 0, 0) - inner[:, half:]
            grad_early = (early.astype(F32) * grad_early).astype(BF16)
            grad_late = (late.astype(F32) * grad_late).astype(BF16)
            grad_value = over_queries(grad, early, late)
            grad_key = over_queries(query, grad_early, grad_late)
            grad_query = jnp.concatenate(
                [
                    jnp.dot(key[:, :half], grad_early, preferred_element_type=F32),
                    jnp.dot(key, grad_late, preferred_element_type=F32),
                ],
                axis=1,
            )
            grad_heads[place, :] = turn_back(grad_query * SCALE).astype(BF16)
            grad_heads[slice(width + at, width + at + HEAD_DIM), :] = turn_back(grad_key * SCALE).astype(BF16)
            grad_heads[slice(2 * width + at, 2 * width + at + HEAD_DIM), :] = grad_value.astype(BF16)

        settle(1, 2)
        for head in range(HEADS):
            attend(head)
        store[1].start()

        @pl.when(micro < micros - 1)
        def _():
            for load in upcoming[1:6]:
                load.start()

        @pl.when(micro == 0)
        def _():
            loads[4].wait()

        stash[6].wait()
        column_sums[...] = jnp.zeros_like(column_sums)
        settle(2, 3)

        def norm_chunk(index, carry):
            part = pl.ds(pl.multiple_of(index * NORM_CHUNK, NORM_CHUNK), NORM_CHUNK)
            grad_attn_in = jnp.dot(qkv_w[...], grad_heads[:, part], preferred_element_type=F32)
            grad_mlp_in = grad_mlp[:, part]
            turned = x[part, :].astype(F32).T
            centred = turned - jnp.mean(turned, axis=0, keepdims=True)
            inv_spread = lax.rsqrt(jnp.mean(centred * centred, axis=0, keepdims=True) + EPSILON)
            unit = centred * inv_spread
            grad_unit = grad_attn_in * attn_column + grad_mlp_in * mlp_column
            through = inv_spread * (
                grad_unit
                - jnp.mean(grad_unit, axis=0, keepdims=True)
                - unit * jnp.mean(grad_unit * unit, axis=0, keepdims=True)
            )
            exact = through.T + grad_out[micro, part, :].astype(F32)
            low = exact.astype(BF16)
            grad_low[micro, part, :] = low
            grad_in[part, :] = jnp.where(section == 0, exact, low.astype(F32))
            terms = (grad_attn_in * unit, grad_attn_in, grad_mlp_in * unit, grad_mlp_in)
            for i, term in enumerate(terms):
                for at in range(0, NORM_CHUNK, 128):
                    column_sums[i] += term[:, at : at + 128]
            return carry

        lax.fori_loop(0, rows // NORM_CHUNK, norm_chunk, 0)

        @pl.when(section == 1)
        def _():
            hand_over(micro).start()

        @pl.when(micro < micros - 1)
        def _():
            upcoming[6].start()

        store[2].start()
        columns = [jnp.sum(column_sums[i], axis=1, keepdims=True) for i in range(4)]
        for start in range(0, 3 * width, width):
            columns.append(jnp.sum(grad_heads[start : start + width, :].astype(F32), axis=1, keepdims=True))
        lanes = lax.broadcasted_iota(jnp.int32, (width, 128), 1)
        gathered = jnp.zeros((width, 128), F32)
        for lane, column in enumerate(columns):
            gathered = jnp.where(lanes == lane, column, gathered)
        vectors[0:7, :] = gathered.T[0:7, :]
        store[3].start()
        return carry

    lax.fori_loop(0, micros, sentence, 0)
    for copy in stores(micros - 1):
        copy.wait()

    @pl.when(section == 1)
    def _():
        for micro in range(micros):
            hand_over(micro).wait_send()


def backward_call(lengths, cotangent, weights, tables, stash):
    attn_gain, _, qkv_weight, _, out_weight, _, mlp_gain, _, up_weight, _, down_weight, _ = weights
    _, inputs, _, _, queries, keys, values, probs, context, _, slope = stash
    micros, rows, width = cotangent.shape
    hidden_width = up_weight.shape[1]
    vector_rows = 16
    wide, tall = (micros, rows, width), (width, rows)
    outs = [
        jax.ShapeDtypeStruct(wide, F32),
        jax.ShapeDtypeStruct((micros, 3 * width, rows), BF16),
        jax.ShapeDtypeStruct((micros, rows, hidden_width), BF16),
        jax.ShapeDtypeStruct(wide, BF16),
        jax.ShapeDtypeStruct((micros, vector_rows, width), F32),
    ]
    return pl.pallas_call(
        functools.partial(backward_kernel, micros),
        out_shape=outs,
        in_specs=[SMEM] + [ANY] * 2 + [VMEM] * 4 + [ANY] * 10,
        out_specs=[ANY] * len(outs),
        scratch_shapes=[
            pltpu.VMEM(qkv_weight.shape, BF16),
            pltpu.VMEM(out_weight.shape, BF16),
            pltpu.VMEM(up_weight.shape, BF16),
            pltpu.VMEM(down_weight.shape, BF16),
            pltpu.VMEM(tall, BF16),
            pltpu.VMEM(tall, BF16),
            pltpu.VMEM(tall, BF16),
            pltpu.VMEM(tall, BF16),
            pltpu.VMEM((rows, hidden_width), BF16),
            pltpu.VMEM((HEADS, rows, rows), BF16),
            pltpu.VMEM(wide, BF16),
            pltpu.VMEM((rows, width), BF16),
            pltpu.VMEM(tall, BF16),
            pltpu.VMEM((rows, hidden_width), BF16),
            pltpu.VMEM((3 * width, rows), BF16),
            pltpu.VMEM(wide, BF16),
            pltpu.VMEM(tall, F32),
            pltpu.VMEM((rows, width), F32),
            pltpu.VMEM((4, width, 128), F32),
            pltpu.VMEM((vector_rows, width), F32),
            pltpu.SemaphoreType.DMA((5,)),
            pltpu.SemaphoreType.DMA((7,)),
            pltpu.SemaphoreType.DMA((4 + hidden_width // FF_TILE,)),
            pltpu.SemaphoreType.DMA((micros,)),
            pltpu.SemaphoreType.DMA((micros,)),
        ],
        compiler_params=pltpu.CompilerParams(collective_id=2, has_side_effects=True, vmem_limit_bytes=58 << 20),
        cost_estimate=pl.CostEstimate(
            flops=micros * (2 * rows * width * (4 * width + 2 * hidden_width) + 8 * rows * rows * width),
            bytes_accessed=80 << 20,
            transcendentals=0,
        ),
        name="layer_backward",
    )(
        lengths, cotangent, inputs, attn_gain, mlp_gain, *tables, qkv_weight, out_weight, up_weight, down_weight,
        queries, keys, values, probs, context, slope,
    )


def partner(axis, bit):
    index = lax.axis_index(axis)
    own_bit = (index // bit) % 2
    return {axis: index + bit - 2 * bit * own_bit}, own_bit


def piece_plan(width, hidden_width, piece):
    counts = [width // piece, hidden_width // piece, hidden_width // piece, 3 * width // piece]
    starts = [0]
    for count in counts:
        starts.append(starts[-1] + count)
    return starts


def reduce_kernel(bits, piece, *refs):
    (
        context_h, hidden_h, mlp_in_h, attn_in_h, grad_out_h, grad_up_h, grad_heads_h, vectors_h,
        qkv_o, out_o, up_o, down_o, vectors_o,
        left, right, heads, vectors, own, final, from_first, *rest,
    ) = refs
    from_dp, rest = rest[:bits], rest[bits:]
    (
        from_second, vector_sum, from_vector,
        in_sems, send_sems, recv_sems, vector_send, vector_recv, out_sems,
    ) = rest
    micros, devices, share, rows = attn_in_h.shape
    width = devices * share
    hidden_width = grad_up_h.shape[2]
    groups = hidden_width // width
    out_at, down_at, up_at, qkv_at, pieces = piece_plan(width, hidden_width, piece)
    across = width // piece

    barrier = pltpu.get_barrier_semaphore()
    dp_peers = [partner("dp", 1 << bit) for bit in range(bits)]
    replica_peers = [partner("replica", 1), partner("replica", 2)]
    for device, _ in dp_peers + replica_peers:
        pl.semaphore_signal(barrier, inc=1, device_id=device, device_id_type=pl.DeviceIdType.MESH)

    wide = hidden_width + width
    loads = [
        [(context_h, left.at[0]), (grad_out_h, right.at[:, :, 0:width]), (vectors_h, vectors)],
        [(hidden_h.at[:, :, group], left.at[3 + group]) for group in range(groups)],
        [(mlp_in_h, left.at[1]), (grad_up_h, right.at[:, :, width:wide])],
        [(attn_in_h, left.at[2]), (grad_heads_h, heads)],
    ]
    copies, count = [], 0
    for group in loads:
        copies.append([])
        for src, dst in group:
            copies[-1].append(pltpu.make_async_copy(src, dst, in_sems.at[count]))
            count += 1
    for copy in copies[0]:
        copy.start()
    for copy in copies[0]:
        copy.wait()
    for group in copies[1:]:
        for copy in group:
            copy.start()
    vector_sum[0] = jnp.sum(vectors[...], axis=0)
    pl.semaphore_wait(barrier, len(dp_peers) + len(replica_peers))

    dp_bits = [own_bit for _, own_bit in dp_peers]

    def keep(k, depth, first_bit=None, second_bit=None, flip=None):
        index = [k] + [slice(None)] * (bits - depth)
        for bit in reversed(range(depth)):
            index.append(1 - dp_bits[bit] if flip == bit else dp_bits[bit])
        if first_bit is not None:
            index.append(first_bit)
        if second_bit is not None:
            index.append(second_bit)
        return tuple(index)

    def transfers(k, turned):
        (first, first_bit), (second, second_bit) = replica_peers[::-1] if turned else replica_peers
        steps = [
            (own.at[keep(k, 0, 1 - first_bit)], from_first.at[k], first, own.at[keep(k, 0, first_bit)]),
        ]
        for bit in range(bits):
            steps.append(
                (
                    own.at[keep(k, bit + 1, first_bit, flip=bit)],
                    from_dp[bit].at[k],
                    dp_peers[bit][0],
                    own.at[keep(k, bit + 1, first_bit)],
                )
            )
        mine = final.at[k, first_bit, second_bit]
        steps.append(
            (
                own.at[keep(k, bits, first_bit, 1 - second_bit)],
                from_second.at[k],
                second,
                own.at[keep(k, bits, first_bit, second_bit)],
            )
        )
        steps.append((mine, mine, second, None))
        steps.append((final.at[k, first_bit], final.at[k, first_bit], first, None))
        return steps, mine

    def copy_of(k, stage, step):
        src, dst, device, _ = step
        return pltpu.make_async_remote_copy(
            src_ref=src,
            dst_ref=dst,
            send_sem=send_sems.at[k, stage],
            recv_sem=recv_sems.at[k, stage],
            device_id=device,
            device_id_type=pl.DeviceIdType.MESH,
        )

    n_steps = bits + 4

    def advance(k, stage, turned):
        steps, mine = transfers(k, turned)
        if stage > 0:
            step = steps[stage - 1]
            copy_of(k, stage - 1, step).wait()
            if step[3] is not None:
                total = step[3][...].astype(F32) + step[1][...].astype(F32)
                if stage == bits + 2:
                    mine[...] = total.astype(BF16)
                else:
                    step[3][...] = total.astype(BF16)
        if stage < n_steps:
            copy_of(k, stage, steps[stage]).start()

    def advance_either(k, stage):
        for turned in (False, True):

            @pl.when(k % 2 == int(turned))
            def _():
                advance(k, stage, turned)

    shape = own.shape[1:]

    def panel(index, micro):
        return left[index, micro].reshape(width, rows)

    def set_own(k, index, columns):
        value = columns(0, panel(index, 0))
        for micro in range(1, micros):
            value = value + columns(micro, panel(index, micro))
        own[k] = value.astype(BF16).reshape(shape)

    def lanes(index):
        return pl.ds(pl.multiple_of(index * piece, 128), piece)

    def compute(k):
        @pl.when(k < down_at)
        def _():
            part = lanes(k)
            set_own(k, 0, lambda micro, block: dims_dot(block, right[micro, :, part], 1, 0))

        @pl.when((k >= down_at) & (k < up_at))
        def _():
            part = lanes((k - down_at) % across)
            set_own(
                k, 3 + (k - down_at) // across, lambda micro, block: dims_dot(block, right[micro, :, part], 1, 0)
            )

        @pl.when((k >= up_at) & (k < qkv_at))
        def _():
            part = lanes(across + k - up_at)
            set_own(k, 1, lambda micro, block: dims_dot(block, right[micro, :, part], 1, 0))

        @pl.when(k >= qkv_at)
        def _():
            part = lanes(k - qkv_at)
            set_own(k, 2, lambda micro, block: dims_dot(block, heads[micro, part, :], 1, 1))

    def out_copy(k, kind):
        if kind == "down":
            target = down_o.at[(k - down_at) // across, :, :, :, lanes((k - down_at) % across)]
        else:
            ref, start = {"out": (out_o, out_at), "up": (up_o, up_at), "qkv": (qkv_o, qkv_at)}[kind]
            target = ref.at[:, :, :, lanes(k - start)]
        return pltpu.make_async_copy(final.at[k], target, out_sems.at[k])

    ranges = {"out": (out_at, down_at), "down": (down_at, up_at), "up": (up_at, qkv_at), "qkv": (qkv_at, pieces)}

    def stored(k, do):
        for kind, (first, end) in ranges.items():

            @pl.when((k >= first) & (k < end))
            def _():
                do(out_copy(k, kind))

    vector_peers = dp_peers + replica_peers

    def vector_copy(i):
        return pltpu.make_async_remote_copy(
            src_ref=vector_sum.at[i],
            dst_ref=from_vector.at[i],
            send_sem=vector_send.at[i],
            recv_sem=vector_recv.at[i],
            device_id=vector_peers[i][0],
            device_id_type=pl.DeviceIdType.MESH,
        )

    lags = [0]
    for stage in range(n_steps):
        lags.append(lags[-1] + 3)

    def turn(t, carry):
        for at, group in zip((down_at, up_at, qkv_at), copies[1:]):

            @pl.when(t == at)
            def _():
                for copy in group:
                    copy.wait()

        @pl.when(t < pieces)
        def _():
            compute(t)

        for stage in range(n_steps + 1):
            k = t - lags[stage]

            @pl.when((k >= 0) & (k < pieces))
            def _():
                advance_either(k, stage)
                if stage == n_steps:
                    stored(k, lambda copy: copy.start())

        for i in range(len(vector_peers) + 1):

            @pl.when(t == 4 * i)
            def _():
                if i > 0:
                    vector_copy(i - 1).wait()
                    vector_sum[i] = vector_sum[i - 1] + from_vector[i - 1]
                if i < len(vector_peers):
                    vector_copy(i).start()
                else:
                    pltpu.make_async_copy(vector_sum.at[i], vectors_o, out_sems.at[pieces]).start()

        return carry

    lax.fori_loop(0, pieces + lags[-1], turn, 0)

    def finish(k, carry):
        stored(k, lambda copy: copy.wait())
        return carry

    lax.fori_loop(0, pieces, finish, 0)
    pltpu.make_async_copy(vector_sum.at[len(vector_peers)], vectors_o, out_sems.at[pieces]).wait()


def reduce_call(stash, kept):
    _, _, attn_in, mlp_in, _, _, _, _, context, hidden, _ = stash
    _, grad_heads, grad_up, grad_out, vectors = kept
    micros, width, rows = attn_in.shape
    hidden_width = hidden.shape[1]
    groups = hidden_width // width
    devices = lax.axis_size("dp")
    bits = devices.bit_length() - 1
    share, quarter = width // devices, width // devices // 4
    piece = PIECE
    pieces = piece_plan(width, hidden_width, piece)[-1]
    loads = 6 + groups + 1
    tall = (micros, devices, share, rows)
    halves = [2] * bits
    steps = bits + 4
    peers = bits + 2
    shape = lambda columns: jax.ShapeDtypeStruct((2, 2, quarter, columns), BF16)
    outs = pl.pallas_call(
        functools.partial(reduce_kernel, bits, piece),
        out_shape=[
            shape(3 * width),
            shape(width),
            shape(hidden_width),
            jax.ShapeDtypeStruct((groups, 2, 2, quarter, width), BF16),
            jax.ShapeDtypeStruct(vectors.shape[1:], F32),
        ],
        in_specs=[ANY] * 8,
        out_specs=[ANY] * 5,
        scratch_shapes=[
            pltpu.VMEM((3 + groups, *tall), BF16),
            pltpu.VMEM((micros, rows, width + hidden_width), BF16),
            pltpu.VMEM(grad_heads.shape, BF16),
            pltpu.VMEM(vectors.shape, F32),
            pltpu.VMEM((pieces, *halves, 2, 2, quarter, piece), BF16),
            pltpu.VMEM((pieces, 2, 2, quarter, piece), BF16),
            pltpu.VMEM((pieces, *halves, 2, quarter, piece), BF16),
            *[pltpu.VMEM((pieces, *halves[bit + 1 :], 2, quarter, piece), BF16) for bit in range(bits)],
            pltpu.VMEM((pieces, quarter, piece), BF16),
            pltpu.VMEM((peers + 1, *vectors.shape[1:]), F32),
            pltpu.VMEM((peers, *vectors.shape[1:]), F32),
            pltpu.SemaphoreType.DMA((loads,)),
            pltpu.SemaphoreType.DMA((pieces, steps)),
            pltpu.SemaphoreType.DMA((pieces, steps)),
            pltpu.SemaphoreType.DMA((peers,)),
            pltpu.SemaphoreType.DMA((peers,)),
            pltpu.SemaphoreType.DMA((pieces + 1,)),
        ],
        compiler_params=pltpu.CompilerParams(
            collective_id=0, has_side_effects=True, vmem_limit_bytes=60 << 20
        ),
        cost_estimate=pl.CostEstimate(
            flops=2 * micros * rows * width * (4 * width + 2 * hidden_width),
            bytes_accessed=30 << 20,
            transcendentals=0,
        ),
        name="weight_gradients",
    )(
        context.reshape(tall),
        hidden.reshape(micros, devices, groups, share, rows),
        mlp_in.reshape(tall),
        attn_in.reshape(tall),
        grad_out,
        grad_up,
        grad_heads,
        vectors,
    )
    qkv, out, up, down, sums = outs
    scattered = [array.reshape(-1, array.shape[-1]) for array in (qkv, out, up, down)]
    return scattered, sums


def finish_kernel(grad_scale, *refs):
    vectors = refs[0]
    sources = refs[1:7]
    targets = refs[7:13]
    vector_outs = refs[13:21]
    held, wide = refs[21:27], refs[27:31]
    in_sems, out_sems = refs[31:]
    ready = (*held[:2], *wide)
    loads = [pltpu.make_async_copy(src, dst, in_sems.at[i]) for i, (src, dst) in enumerate(zip(sources, held))]
    stores = [pltpu.make_async_copy(src, dst, out_sems.at[i]) for i, (src, dst) in enumerate(zip(ready, targets))]
    order = (1, 0, 3, 2, 4, 5)
    for i in order:
        loads[i].start()
    devices = lax.axis_size("dp")
    mine = lax.axis_index("dp")
    width = vectors.shape[1]
    first_rows = (0, 1, 4, 7, 2, 3, 8, 7)
    for device in range(devices):

        @pl.when(mine == device)
        def _():
            for out, first in zip(vector_outs, first_rows):
                at, size, filled = device * out.shape[1], out.shape[1], 0
                while filled < size:
                    row, column = divmod(at + filled, width)
                    count = min(size - filled, width - column)
                    piece = vectors[first + row : first + row + 1, column : column + count]
                    out[:, filled : filled + count] = piece * grad_scale
                    filled += count

    for i in order:
        loads[i].wait()
        if i >= 2:
            wide[i - 2][...] = held[i][...].astype(F32) * grad_scale
        stores[i].start()
    for store in stores:
        store.wait()


def finish_call(grad_scale, shares, vectors, outputs, grad_in, hidden_width):
    width = vectors.shape[1]
    devices = lax.axis_size("dp")
    sizes = [width, width, 3 * width, width, width, width, hidden_width, width]
    matrices = [jax.ShapeDtypeStruct(share.shape, F32) for share in shares]
    results = pl.pallas_call(
        functools.partial(finish_kernel, grad_scale),
        out_shape=[
            jax.ShapeDtypeStruct(outputs.shape, BF16),
            jax.ShapeDtypeStruct(grad_in.shape, F32),
            *matrices,
            *[jax.ShapeDtypeStruct((1, size // devices), F32) for size in sizes],
        ],
        in_specs=[VMEM] + [ANY] * 6,
        out_specs=[ANY] * 6 + [VMEM] * 8,
        scratch_shapes=[pltpu.VMEM(array.shape, array.dtype) for array in (outputs, grad_in, *shares)]
        + [pltpu.VMEM(share.shape, F32) for share in shares]
        + [pltpu.SemaphoreType.DMA((6,)), pltpu.SemaphoreType.DMA((6,))],
        compiler_params=pltpu.CompilerParams(vmem_limit_bytes=60 << 20),
        name="finish",
    )(vectors, outputs, grad_in, *shares)
    return results[:2], results[2:6], results[6:]


def rotary_tables(seq_len):
    positions = np.arange(seq_len, dtype=np.float32)
    exponents = np.arange(0, ROTARY, 2, dtype=np.float32) / np.float32(ROTARY)
    inverse = np.float32(1.0) / np.float32(ROTARY_BASE) ** exponents
    angles = inverse[:, None] * positions[None, :]
    return jnp.asarray(np.cos(angles)), jnp.asarray(np.sin(angles))


def summed(share):
    part = lax.psum_scatter(share.astype(BF16), "dp", scatter_dimension=0, tiled=True)
    return lax.psum(part, "replica").astype(F32)


def in_pieces(width):
    devices = lax.axis_size("dp")
    return devices & (devices - 1) == 0 and lax.axis_size("replica") == 4 and width % (64 * devices) == 0


def local_totals(stash, kept):
    _, _, attn_in, mlp_in, _, _, _, _, context, hidden, _ = stash
    _, grad_heads, grad_up, grad_out, vectors = kept
    vector_sums = jnp.sum(vectors, axis=0)
    groups = hidden.shape[1] // attn_in.shape[1]
    return (
        vector_sums[0],
        vector_sums[1],
        jnp.einsum("mdr,mer->de", attn_in, grad_heads, preferred_element_type=F32),
        vector_sums[4:7].reshape(-1),
        jnp.einsum("mer,mrd->ed", context, grad_out, preferred_element_type=F32),
        vector_sums[7],
        vector_sums[2],
        vector_sums[3],
        jnp.einsum("mdr,mrf->df", mlp_in, grad_up, preferred_element_type=F32),
        vector_sums[8 : 8 + groups].reshape(-1),
        jnp.einsum("mfr,mrd->fd", hidden, grad_out, preferred_element_type=F32),
        vector_sums[7],
    )


def body(tokens, cotangent, lengths, *weights):
    weights = tuple(array if array.ndim == 2 else array[0] for array in weights)
    micros = lengths.shape[0]
    width = tokens.shape[1]
    rows = tokens.shape[0] // micros
    tables = rotary_tables(rows)
    stash = forward_call(lengths, tokens.reshape(micros, rows, width), weights, tables)
    kept = backward_call(lengths, cotangent.reshape(micros, rows, width), weights, tables, stash)
    grad_scale = float(tokens.shape[0] * lax.axis_size("dp") * lax.axis_size("replica")) ** (-0.5)
    if in_pieces(width):
        shares, vectors = reduce_call(stash, kept)
        (outputs, grad_in), matrices, parts = finish_call(
            grad_scale, shares, vectors, stash[0], kept[0], weights[8].shape[1]
        )
        qkv, out, up, down = (matrix[None] for matrix in matrices)
        gain, shift, qkv_bias, out_bias, mlp_gain, mlp_shift, up_bias, down_bias = parts
        grads = (gain, shift, qkv, qkv_bias, out, out_bias, mlp_gain, mlp_shift, up, up_bias, down, down_bias)
    else:
        outputs, grad_in = stash[0], kept[0]
        grads = tuple(summed(total)[None] * grad_scale for total in local_totals(stash, kept))
    return (outputs.reshape(1, micros * rows, width), grad_in.reshape(1, micros * rows, width), *grads)


def solution(mesh):
    rows = P(("dp", "replica"), None)
    vector, matrix = P("section", None), P("section", None, None)
    out_rows = P("section", ("dp", "replica"), None)
    vector_out, matrix_out = P("section", "dp"), P("section", "dp", None)
    return jax.shard_map(
        body,
        mesh=mesh,
        in_specs=(
            rows, rows, P(("dp", "replica")), vector, vector, matrix, vector, matrix, vector, vector, vector, matrix,
            vector, matrix, vector,
        ),
        out_specs=(
            out_rows, out_rows, vector_out, vector_out, matrix_out, vector_out, matrix_out, vector_out, vector_out,
            vector_out, matrix_out, vector_out, matrix_out, vector_out,
        ),
        check_vma=False,
    )
```

```python
import functools

import jax
import jax.numpy as jnp
import numpy as np
from jax import lax
from jax.experimental import pallas as pl
from jax.experimental.pallas import tpu as pltpu
from jax.sharding import PartitionSpec as P

HEADS = 12
HEAD_DIM = 64
ROTARY = 16
HALF = ROTARY // 2
EPSILON = 1e-05
ROTARY_BASE = 10000.0
MASKED = -1e30
LOG2_E = 1.4426950408889634
LOG2_DENSITY = -1.3257480647361593
SCALE = HEAD_DIM**-0.5
F32 = jnp.float32
BF16 = jnp.bfloat16
ANY = pl.BlockSpec(memory_space=pl.ANY)
VMEM = pl.BlockSpec(memory_space=pltpu.VMEM)
SMEM = pl.BlockSpec(memory_space=pltpu.SMEM)
ROW_CHUNK = 256
NORM_CHUNK = 256
QKV_TILE = 256
FF_TILE = 768
PIECE = 384


def dims_dot(left, right, left_dim, right_dim):
    return lax.dot_general(
        left, right, (((left_dim,), (right_dim,)), ((), ())), preferred_element_type=F32
    )


def normal_parts(v):
    scaled = v * 0.7071067811865476
    bell = jnp.exp2(LOG2_DENSITY - scaled * (scaled * LOG2_E))
    return 0.5 + 0.5 * lax.erf(scaled), bell


def forward_kernel(micros, *refs):
    (
        lengths, tokens_h, attn_gain, attn_shift, qkv_bias, out_bias, mlp_gain, mlp_shift, up_bias, down_bias,
        cosine, sine, qkv_h, out_h, up_h, down_h,
        y_h, inputs_h, attn_in_h, mlp_in_h, queries_h, keys_h, values_h, probs_h, context_h, hidden_h, slope_h,
        qkv_w, out_w, up_w, down_w, x, attn_in, mlp_in, attn_in_t, mlp_in_t, heads_t, context_t, hidden_t, slope,
        bias, total, probs, y, in_sems, out_sems, send_sems, recv_sems,
    ) = refs
    section = lax.axis_index("section")
    rows, width = attn_in.shape
    hidden_width = up_w.shape[1]
    half = rows // 2
    other = {"section": 1 - section}

    barrier = pltpu.get_barrier_semaphore()
    pl.semaphore_signal(barrier, inc=1, device_id=other, device_id_type=pl.DeviceIdType.MESH)
    loads = [
        pltpu.make_async_copy(src, dst, in_sems.at[i])
        for i, (src, dst) in enumerate(
            ((tokens_h, x), (qkv_h, qkv_w), (out_h, out_w), (up_h, up_w), (down_h, down_w))
        )
    ]

    @pl.when(section == 0)
    def _():
        loads[0].start()

    loads[1].start()
    probs[:, half:, :half] = jnp.zeros((probs.shape[0], half, half), BF16)
    cos_rows, sin_rows = cosine[...], sine[...]

    def hand_over(micro):
        return pltpu.make_async_remote_copy(
            src_ref=y.at[micro],
            dst_ref=x.at[micro],
            send_sem=send_sems.at[micro],
            recv_sem=recv_sems.at[micro],
            device_id=other,
            device_id_type=pl.DeviceIdType.MESH,
        )

    def stores(micro):
        pairs = [
            (x.at[micro], inputs_h.at[micro]),
            (attn_in_t, attn_in_h.at[micro]),
            (mlp_in_t, mlp_in_h.at[micro]),
            (heads_t.at[0:width], queries_h.at[micro]),
            (heads_t.at[width : 2 * width], keys_h.at[micro]),
            (heads_t.at[2 * width :], values_h.at[micro]),
            (context_t, context_h.at[micro]),
            (y.at[micro], y_h.at[micro]),
            (probs, probs_h.at[micro]),
        ]
        for start in range(0, hidden_width, FF_TILE):
            part = slice(start, start + FF_TILE)
            pairs.append((hidden_t.at[part], hidden_h.at[micro, part]))
            pairs.append((slope.at[:, part], slope_h.at[micro, :, part]))
        return [pltpu.make_async_copy(src, dst, out_sems.at[i]) for i, (src, dst) in enumerate(pairs)]

    @pl.when(section == 1)
    def _():
        for load in loads[2:]:
            load.start()

    pl.semaphore_wait(barrier, 1)

    def sentence(micro, carry):
        store = stores(micro)

        def settle(first, end):
            @pl.when(micro > 0)
            def _():
                for copy in stores(micro - 1)[first:end]:
                    copy.wait()

        length = lengths[micro]
        key_ids = lax.broadcasted_iota(jnp.int32, (rows, rows), 0)
        query_ids = lax.broadcasted_iota(jnp.int32, (rows, rows), 1)
        bias[...] = jnp.where((key_ids <= query_ids) & (key_ids < length), 0.0, MASKED)

        settle(0, 3)

        @pl.when((section == 0) & (micro == 0))
        def _():
            loads[0].wait()

        @pl.when(section == 1)
        def _():
            hand_over(micro).wait_recv()

        store[0].start()
        for start in range(0, rows, ROW_CHUNK):
            part = slice(start, start + ROW_CHUNK)
            block = x[micro, part, :].astype(F32)
            centred = block - jnp.mean(block, axis=-1, keepdims=True)
            unit = centred * lax.rsqrt(jnp.mean(centred * centred, axis=-1, keepdims=True) + EPSILON)
            attn = (unit * attn_gain[...].astype(F32) + attn_shift[...].astype(F32)).astype(BF16)
            mlp = (unit * mlp_gain[...].astype(F32) + mlp_shift[...].astype(F32)).astype(BF16)
            attn_in[part, :] = attn
            mlp_in[part, :] = mlp
            attn_in_t[:, part] = attn.T
            mlp_in_t[:, part] = mlp.T
        store[1].start()
        store[2].start()

        @pl.when(micro == 0)
        def _():
            loads[1].wait()

        @pl.when((micro == 0) & (section == 0))
        def _():
            for load in loads[2:]:
                load.start()

        settle(3, 6)
        for start in range(0, 3 * width, QKV_TILE):
            part = slice(start, start + QKV_TILE)
            projected = jnp.dot(attn_in[...], qkv_w[:, part], preferred_element_type=F32)
            turned = (projected + qkv_bias[:, part].astype(F32)).T
            if start >= 2 * width:
                heads_t[part, :] = turned.astype(BF16)
                continue
            for at in range(0, QKV_TILE, HEAD_DIM):
                low, high = turned[at : at + HALF], turned[at + HALF : at + ROTARY]
                heads_t[start + at : start + at + HEAD_DIM, :] = jnp.concatenate(
                    [
                        low * cos_rows - high * sin_rows,
                        high * cos_rows + low * sin_rows,
                        turned[at + ROTARY : at + HEAD_DIM],
                    ],
                    axis=0,
                ).astype(BF16)
        for copy in store[3:6]:
            copy.start()

        def softmax(scores):
            raised = jnp.exp(scores - jnp.max(scores, axis=0, keepdims=True))
            return (raised * (1.0 / jnp.sum(raised, axis=0, keepdims=True))).astype(BF16)

        def scored(head):
            at = head * HEAD_DIM
            query = heads_t[at : at + HEAD_DIM, :] * jnp.bfloat16(SCALE)
            key = heads_t[width + at : width + at + HEAD_DIM, :]
            early = dims_dot(key[:, :half], query[:, :half], 0, 0) + bias[:half, :half]
            return early, dims_dot(key, query[:, half:], 0, 0) + bias[:, half:]

        settle(6, 7)
        settle(8, 9)
        upcoming = scored(0)
        for head in range(HEADS):
            early, late = upcoming
            if head + 1 < HEADS:
                upcoming = scored(head + 1)
            early, late = softmax(early), softmax(late)
            probs[head, :half, :half] = early
            probs[head, :, half:] = late
            place = slice(head * HEAD_DIM, (head + 1) * HEAD_DIM)
            value = heads_t[2 * width + head * HEAD_DIM : 2 * width + (head + 1) * HEAD_DIM, :]
            context_t[place, :half] = jnp.dot(value[:, :half], early, preferred_element_type=F32).astype(BF16)
            context_t[place, half:] = jnp.dot(value, late, preferred_element_type=F32).astype(BF16)
        store[8].start()
        store[6].start()

        @pl.when(micro == 0)
        def _():
            for load in loads[2:]:
                load.wait()

        total[...] = (
            dims_dot(context_t[...], out_w[...], 0, 0)
            + x[micro].astype(F32)
            + (out_bias[...].astype(F32) + down_bias[...].astype(F32))
        )
        settle(7, 8)
        settle(9, len(store))
        for start in range(0, hidden_width, FF_TILE):
            part = slice(start, start + FF_TILE)
            up = jnp.dot(mlp_in[...], up_w[:, part], preferred_element_type=F32)
            up = up + up_bias[:, part].astype(F32)
            share, density = normal_parts(up)
            hidden = (up * share).astype(BF16)
            slope[:, part] = (share + up * density).astype(BF16)
            hidden_t[part, :] = hidden.T
            tile = start // FF_TILE
            store[9 + 2 * tile].start()
            store[10 + 2 * tile].start()
            total[...] += jnp.dot(hidden, down_w[part, :], preferred_element_type=F32)
        y[micro] = total[...].astype(BF16)

        @pl.when(section == 0)
        def _():
            hand_over(micro).start()

        store[7].start()
        return carry

    lax.fori_loop(0, micros, sentence, 0)
    for copy in stores(micros - 1):
        copy.wait()

    @pl.when(section == 0)
    def _():
        for micro in range(micros):
            hand_over(micro).wait_send()


def forward_call(lengths, tokens, weights, tables):
    (
        attn_gain, attn_shift, qkv_weight, qkv_bias, out_weight, out_bias, mlp_gain, mlp_shift, up_weight, up_bias,
        down_weight, down_bias,
    ) = weights
    micros, rows, width = tokens.shape
    hidden_width = up_weight.shape[1]
    wide, tall = (micros, rows, width), (micros, width, rows)
    shapes = [
        wide, wide, tall, tall, tall, tall, tall, (micros, HEADS, rows, rows), tall, (micros, hidden_width, rows),
        (micros, rows, hidden_width),
    ]
    buffers = [
        qkv_weight.shape, out_weight.shape, up_weight.shape, down_weight.shape, wide, (rows, width), (rows, width),
        (width, rows), (width, rows), (3 * width, rows), (width, rows), (hidden_width, rows), (rows, hidden_width),
    ]
    return pl.pallas_call(
        functools.partial(forward_kernel, micros),
        out_shape=[jax.ShapeDtypeStruct(shape, BF16) for shape in shapes],
        in_specs=[SMEM, ANY] + [VMEM] * 10 + [ANY] * 4,
        out_specs=[ANY] * len(shapes),
        scratch_shapes=[pltpu.VMEM(shape, BF16) for shape in buffers]
        + [
            pltpu.VMEM((rows, rows), F32),
            pltpu.VMEM((rows, width), F32),
            pltpu.VMEM((HEADS, rows, rows), BF16),
            pltpu.VMEM(wide, BF16),
            pltpu.SemaphoreType.DMA((5,)),
            pltpu.SemaphoreType.DMA((9 + 2 * (hidden_width // FF_TILE),)),
            pltpu.SemaphoreType.DMA((micros,)),
            pltpu.SemaphoreType.DMA((micros,)),
        ],
        compiler_params=pltpu.CompilerParams(collective_id=1, has_side_effects=True, vmem_limit_bytes=58 << 20),
        cost_estimate=pl.CostEstimate(
            flops=micros * (2 * rows * width * (4 * width + 2 * hidden_width) + 4 * rows * rows * width),
            bytes_accessed=80 << 20,
            transcendentals=micros * rows * hidden_width,
        ),
        name="layer_forward",
    )(
        lengths, tokens, attn_gain, attn_shift, qkv_bias, out_bias, mlp_gain, mlp_shift, up_bias, down_bias,
        *tables, qkv_weight, out_weight, up_weight, down_weight,
    )


def backward_kernel(micros, *refs):
    (
        lengths, cotangent_h, inputs_h, attn_gain, mlp_gain, cosine, sine, qkv_h, out_h, up_h, down_h,
        queries_h, keys_h, values_h, probs_h, context_h, slope_h,
        grad_in_h, grad_heads_h, grad_up_h, grad_out_h, vectors_h,
        qkv_w, out_w, up_w, down_w, queries, keys, values, context, slope, probs, grad_out, x, grad_context,
        grad_up, grad_heads, grad_low, grad_mlp, grad_in, column_sums, vectors,
        in_sems, stash_sems, out_sems, send_sems, recv_sems,
    ) = refs
    section = lax.axis_index("section")
    rows, width = x.shape
    hidden_width = up_w.shape[1]
    half = rows // 2
    other = {"section": 1 - section}

    barrier = pltpu.get_barrier_semaphore()
    pl.semaphore_signal(barrier, inc=1, device_id=other, device_id_type=pl.DeviceIdType.MESH)
    loads = [
        pltpu.make_async_copy(src, dst, in_sems.at[i])
        for i, (src, dst) in enumerate(
            ((cotangent_h, grad_out), (out_h, out_w), (down_h, down_w), (up_h, up_w), (qkv_h, qkv_w))
        )
    ]

    def stash_loads(micro):
        pairs = (
            (slope_h, slope), (values_h, values), (context_h, context), (queries_h, queries), (keys_h, keys),
            (probs_h, probs), (inputs_h, x),
        )
        return [
            pltpu.make_async_copy(src.at[micro], dst, stash_sems.at[i]) for i, (src, dst) in enumerate(pairs)
        ]

    @pl.when(section == 1)
    def _():
        loads[0].start()

    for load in loads[1:3]:
        load.start()
    stash_loads(0)[0].start()
    loads[3].start()
    for load in stash_loads(0)[1:]:
        load.start()
    loads[4].start()
    cos_rows, sin_rows = cosine[...], sine[...]
    attn_column = jnp.broadcast_to(attn_gain[...].astype(F32), (8, width)).T[:, 0:1]
    mlp_column = jnp.broadcast_to(mlp_gain[...].astype(F32), (8, width)).T[:, 0:1]

    def hand_over(micro):
        return pltpu.make_async_remote_copy(
            src_ref=grad_low.at[micro],
            dst_ref=grad_out.at[micro],
            send_sem=send_sems.at[micro],
            recv_sem=recv_sems.at[micro],
            device_id=other,
            device_id_type=pl.DeviceIdType.MESH,
        )

    def stores(micro):
        pairs = [
            (grad_out.at[micro], grad_out_h.at[micro]),
            (grad_heads, grad_heads_h.at[micro]),
            (grad_in, grad_in_h.at[micro]),
            (vectors, vectors_h.at[micro]),
        ]
        for start in range(0, hidden_width, FF_TILE):
            part = slice(start, start + FF_TILE)
            pairs.append((grad_up.at[:, part], grad_up_h.at[micro, :, part]))
        return [pltpu.make_async_copy(src, dst, out_sems.at[i]) for i, (src, dst) in enumerate(pairs)]

    pl.semaphore_wait(barrier, 1)

    def sentence(micro, carry):
        store = stores(micro)
        stash = stash_loads(micro)
        upcoming = stash_loads(micro + 1)

        def settle(first, end):
            @pl.when(micro > 0)
            def _():
                for copy in stores(micro - 1)[first:end]:
                    copy.wait()

        @pl.when((section == 1) & (micro == 0))
        def _():
            loads[0].wait()

        @pl.when(section == 0)
        def _():
            hand_over(micro).wait_recv()

        row_ids = lax.broadcasted_iota(jnp.int32, (rows, 1), 0)
        grad_wide = jnp.where(row_ids < lengths[micro], grad_out[micro].astype(F32), 0.0)
        grad_out[micro] = grad_wide.astype(BF16)

        settle(0, 1)
        settle(3, len(store))
        vectors[...] = jnp.zeros_like(vectors)
        vectors[7:8, :] = jnp.sum(grad_wide, axis=0, keepdims=True)
        store[0].start()

        @pl.when(micro == 0)
        def _():
            loads[1].wait()

        grad_context[...] = dims_dot(out_w[...], grad_out[micro], 1, 1).astype(BF16)

        @pl.when(micro == 0)
        def _():
            loads[2].wait()
            loads[3].wait()

        stash[0].wait()
        for start in range(0, hidden_width, FF_TILE):
            part = slice(start, start + FF_TILE)
            grad_hidden = dims_dot(grad_out[micro], down_w[part, :], 1, 1)
            grad_pre = (grad_hidden * slope[:, part].astype(F32)).astype(BF16)
            grad_up[:, part] = grad_pre
            store[4 + start // FF_TILE].start()
            sums = jnp.sum(grad_pre.astype(F32), axis=0, keepdims=True)
            for at in range(0, FF_TILE, 128):
                row, column = divmod(start + at, width)
                vectors[8 + row : 9 + row, column : column + 128] = sums[:, at : at + 128]
            back = dims_dot(up_w[:, part], grad_pre, 1, 1)
            if start == 0:
                grad_mlp[...] = back
            else:
                grad_mlp[...] += back

        @pl.when(micro < micros - 1)
        def _():
            upcoming[0].start()

        for load in stash[1:6]:
            load.wait()

        def turn_back(grad):
            low, high = grad[:HALF], grad[HALF:ROTARY]
            return jnp.concatenate(
                [low * cos_rows + high * sin_rows, high * cos_rows - low * sin_rows, grad[ROTARY:]], axis=0
            )

        def over_queries(left, early, late):
            both = dims_dot(left[:, half:], late, 1, 1)
            return jnp.concatenate([both[:, :half] + dims_dot(left[:, :half], early, 1, 1), both[:, half:]], axis=1)

        def attend(head):
            at = head * HEAD_DIM
            place = slice(at, at + HEAD_DIM)
            query, key, value, grad = queries[place, :], keys[place, :], values[place, :], grad_context[place, :]
            inner = jnp.sum(grad.astype(F32) * context[place, :].astype(F32), axis=0, keepdims=True)
            early, late = probs[head, :half, :half], probs[head, :, half:]
            grad_early = dims_dot(value[:, :half], grad[:, :half], 0, 0) - inner[:, :half]
            grad_late = dims_dot(value, grad[:, half:], 0, 0) - inner[:, half:]
            grad_early = (early.astype(F32) * grad_early).astype(BF16)
            grad_late = (late.astype(F32) * grad_late).astype(BF16)
            grad_value = over_queries(grad, early, late)
            grad_key = over_queries(query, grad_early, grad_late)
            grad_query = jnp.concatenate(
                [
                    jnp.dot(key[:, :half], grad_early, preferred_element_type=F32),
                    jnp.dot(key, grad_late, preferred_element_type=F32),
                ],
                axis=1,
            )
            grad_heads[place, :] = turn_back(grad_query * SCALE).astype(BF16)
            grad_heads[slice(width + at, width + at + HEAD_DIM), :] = turn_back(grad_key * SCALE).astype(BF16)
            grad_heads[slice(2 * width + at, 2 * width + at + HEAD_DIM), :] = grad_value.astype(BF16)

        settle(1, 2)
        for head in range(HEADS):
            attend(head)
        store[1].start()

        @pl.when(micro < micros - 1)
        def _():
            for load in upcoming[1:6]:
                load.start()

        @pl.when(micro == 0)
        def _():
            loads[4].wait()

        stash[6].wait()
        column_sums[...] = jnp.zeros_like(column_sums)
        settle(2, 3)

        def norm_chunk(index, carry):
            part = pl.ds(pl.multiple_of(index * NORM_CHUNK, NORM_CHUNK), NORM_CHUNK)
            grad_attn_in = jnp.dot(qkv_w[...], grad_heads[:, part], preferred_element_type=F32)
            grad_mlp_in = grad_mlp[:, part]
            turned = x[part, :].astype(F32).T
            centred = turned - jnp.mean(turned, axis=0, keepdims=True)
            inv_spread = lax.rsqrt(jnp.mean(centred * centred, axis=0, keepdims=True) + EPSILON)
            unit = centred * inv_spread
            grad_unit = grad_attn_in * attn_column + grad_mlp_in * mlp_column
            through = inv_spread * (
                grad_unit
                - jnp.mean(grad_unit, axis=0, keepdims=True)
                - unit * jnp.mean(grad_unit * unit, axis=0, keepdims=True)
            )
            exact = through.T + grad_out[micro, part, :].astype(F32)
            low = exact.astype(BF16)
            grad_low[micro, part, :] = low
            grad_in[part, :] = jnp.where(section == 0, exact, low.astype(F32))
            terms = (grad_attn_in * unit, grad_attn_in, grad_mlp_in * unit, grad_mlp_in)
            for i, term in enumerate(terms):
                for at in range(0, NORM_CHUNK, 128):
                    column_sums[i] += term[:, at : at + 128]
            return carry

        lax.fori_loop(0, rows // NORM_CHUNK, norm_chunk, 0)

        @pl.when(section == 1)
        def _():
            hand_over(micro).start()

        @pl.when(micro < micros - 1)
        def _():
            upcoming[6].start()

        store[2].start()
        columns = [jnp.sum(column_sums[i], axis=1, keepdims=True) for i in range(4)]
        for start in range(0, 3 * width, width):
            columns.append(jnp.sum(grad_heads[start : start + width, :].astype(F32), axis=1, keepdims=True))
        lanes = lax.broadcasted_iota(jnp.int32, (width, 128), 1)
        gathered = jnp.zeros((width, 128), F32)
        for lane, column in enumerate(columns):
            gathered = jnp.where(lanes == lane, column, gathered)
        vectors[0:7, :] = gathered.T[0:7, :]
        store[3].start()
        return carry

    lax.fori_loop(0, micros, sentence, 0)
    for copy in stores(micros - 1):
        copy.wait()

    @pl.when(section == 1)
    def _():
        for micro in range(micros):
            hand_over(micro).wait_send()


def backward_call(lengths, cotangent, weights, tables, stash):
    attn_gain, _, qkv_weight, _, out_weight, _, mlp_gain, _, up_weight, _, down_weight, _ = weights
    _, inputs, _, _, queries, keys, values, probs, context, _, slope = stash
    micros, rows, width = cotangent.shape
    hidden_width = up_weight.shape[1]
    vector_rows = 16
    wide, tall = (micros, rows, width), (width, rows)
    outs = [
        jax.ShapeDtypeStruct(wide, F32),
        jax.ShapeDtypeStruct((micros, 3 * width, rows), BF16),
        jax.ShapeDtypeStruct((micros, rows, hidden_width), BF16),
        jax.ShapeDtypeStruct(wide, BF16),
        jax.ShapeDtypeStruct((micros, vector_rows, width), F32),
    ]
    return pl.pallas_call(
        functools.partial(backward_kernel, micros),
        out_shape=outs,
        in_specs=[SMEM] + [ANY] * 2 + [VMEM] * 4 + [ANY] * 10,
        out_specs=[ANY] * len(outs),
        scratch_shapes=[
            pltpu.VMEM(qkv_weight.shape, BF16),
            pltpu.VMEM(out_weight.shape, BF16),
            pltpu.VMEM(up_weight.shape, BF16),
            pltpu.VMEM(down_weight.shape, BF16),
            pltpu.VMEM(tall, BF16),
            pltpu.VMEM(tall, BF16),
            pltpu.VMEM(tall, BF16),
            pltpu.VMEM(tall, BF16),
            pltpu.VMEM((rows, hidden_width), BF16),
            pltpu.VMEM((HEADS, rows, rows), BF16),
            pltpu.VMEM(wide, BF16),
            pltpu.VMEM((rows, width), BF16),
            pltpu.VMEM(tall, BF16),
            pltpu.VMEM((rows, hidden_width), BF16),
            pltpu.VMEM((3 * width, rows), BF16),
            pltpu.VMEM(wide, BF16),
            pltpu.VMEM(tall, F32),
            pltpu.VMEM((rows, width), F32),
            pltpu.VMEM((4, width, 128), F32),
            pltpu.VMEM((vector_rows, width), F32),
            pltpu.SemaphoreType.DMA((5,)),
            pltpu.SemaphoreType.DMA((7,)),
            pltpu.SemaphoreType.DMA((4 + hidden_width // FF_TILE,)),
            pltpu.SemaphoreType.DMA((micros,)),
            pltpu.SemaphoreType.DMA((micros,)),
        ],
        compiler_params=pltpu.CompilerParams(collective_id=2, has_side_effects=True, vmem_limit_bytes=58 << 20),
        cost_estimate=pl.CostEstimate(
            flops=micros * (2 * rows * width * (4 * width + 2 * hidden_width) + 8 * rows * rows * width),
            bytes_accessed=80 << 20,
            transcendentals=0,
        ),
        name="layer_backward",
    )(
        lengths, cotangent, inputs, attn_gain, mlp_gain, *tables, qkv_weight, out_weight, up_weight, down_weight,
        queries, keys, values, probs, context, slope,
    )


def partner(axis, bit):
    index = lax.axis_index(axis)
    own_bit = (index // bit) % 2
    return {axis: index + bit - 2 * bit * own_bit}, own_bit


def piece_plan(width, hidden_width, piece):
    counts = [width // piece, hidden_width // piece, hidden_width // piece, 3 * width // piece]
    starts = [0]
    for count in counts:
        starts.append(starts[-1] + count)
    return starts


def reduce_kernel(bits, piece, *refs):
    (
        context_h, hidden_h, mlp_in_h, attn_in_h, grad_out_h, grad_up_h, grad_heads_h, vectors_h,
        qkv_o, out_o, up_o, down_o, vectors_o,
        left, right, heads, vectors, own, final, from_first, *rest,
    ) = refs
    from_dp, rest = rest[:bits], rest[bits:]
    (
        from_second, vector_sum, from_vector,
        in_sems, send_sems, recv_sems, vector_send, vector_recv, out_sems,
    ) = rest
    micros, devices, share, rows = attn_in_h.shape
    width = devices * share
    hidden_width = grad_up_h.shape[2]
    groups = hidden_width // width
    out_at, down_at, up_at, qkv_at, pieces = piece_plan(width, hidden_width, piece)
    across = width // piece

    barrier = pltpu.get_barrier_semaphore()
    dp_peers = [partner("dp", 1 << bit) for bit in range(bits)]
    replica_peers = [partner("replica", 1), partner("replica", 2)]
    for device, _ in dp_peers + replica_peers:
        pl.semaphore_signal(barrier, inc=1, device_id=device, device_id_type=pl.DeviceIdType.MESH)

    wide = hidden_width + width
    loads = [
        [(context_h, left.at[0]), (grad_out_h, right.at[:, :, 0:width]), (vectors_h, vectors)],
        [(hidden_h.at[:, :, group], left.at[3 + group]) for group in range(groups)],
        [(mlp_in_h, left.at[1]), (grad_up_h, right.at[:, :, width:wide])],
        [(attn_in_h, left.at[2]), (grad_heads_h, heads)],
    ]
    copies, count = [], 0
    for group in loads:
        copies.append([])
        for src, dst in group:
            copies[-1].append(pltpu.make_async_copy(src, dst, in_sems.at[count]))
            count += 1
    for copy in copies[0]:
        copy.start()
    for copy in copies[0]:
        copy.wait()
    for group in copies[1:]:
        for copy in group:
            copy.start()
    vector_sum[0] = jnp.sum(vectors[...], axis=0)
    pl.semaphore_wait(barrier, len(dp_peers) + len(replica_peers))

    dp_bits = [own_bit for _, own_bit in dp_peers]

    def keep(k, depth, first_bit=None, second_bit=None, flip=None):
        index = [k] + [slice(None)] * (bits - depth)
        for bit in reversed(range(depth)):
            index.append(1 - dp_bits[bit] if flip == bit else dp_bits[bit])
        if first_bit is not None:
            index.append(first_bit)
        if second_bit is not None:
            index.append(second_bit)
        return tuple(index)

    def transfers(k, turned):
        (first, first_bit), (second, second_bit) = replica_peers[::-1] if turned else replica_peers
        steps = [
            (own.at[keep(k, 0, 1 - first_bit)], from_first.at[k], first, own.at[keep(k, 0, first_bit)]),
        ]
        for bit in range(bits):
            steps.append(
                (
                    own.at[keep(k, bit + 1, first_bit, flip=bit)],
                    from_dp[bit].at[k],
                    dp_peers[bit][0],
                    own.at[keep(k, bit + 1, first_bit)],
                )
            )
        mine = final.at[k, first_bit, second_bit]
        steps.append(
            (
                own.at[keep(k, bits, first_bit, 1 - second_bit)],
                from_second.at[k],
                second,
                own.at[keep(k, bits, first_bit, second_bit)],
            )
        )
        steps.append((mine, mine, second, None))
        steps.append((final.at[k, first_bit], final.at[k, first_bit], first, None))
        return steps, mine

    def copy_of(k, stage, step):
        src, dst, device, _ = step
        return pltpu.make_async_remote_copy(
            src_ref=src,
            dst_ref=dst,
            send_sem=send_sems.at[k, stage],
            recv_sem=recv_sems.at[k, stage],
            device_id=device,
            device_id_type=pl.DeviceIdType.MESH,
        )

    n_steps = bits + 4

    def advance(k, stage, turned):
        steps, mine = transfers(k, turned)
        if stage > 0:
            step = steps[stage - 1]
            copy_of(k, stage - 1, step).wait()
            if step[3] is not None:
                total = step[3][...].astype(F32) + step[1][...].astype(F32)
                if stage == bits + 2:
                    mine[...] = total.astype(BF16)
                else:
                    step[3][...] = total.astype(BF16)
        if stage < n_steps:
            copy_of(k, stage, steps[stage]).start()

    def advance_either(k, stage):
        for turned in (False, True):

            @pl.when(k % 2 == int(turned))
            def _():
                advance(k, stage, turned)

    shape = own.shape[1:]

    def panel(index, micro):
        return left[index, micro].reshape(width, rows)

    def set_own(k, index, columns):
        value = columns(0, panel(index, 0))
        for micro in range(1, micros):
            value = value + columns(micro, panel(index, micro))
        own[k] = value.astype(BF16).reshape(shape)

    def lanes(index):
        return pl.ds(pl.multiple_of(index * piece, 128), piece)

    def compute(k):
        @pl.when(k < down_at)
        def _():
            part = lanes(k)
            set_own(k, 0, lambda micro, block: dims_dot(block, right[micro, :, part], 1, 0))

        @pl.when((k >= down_at) & (k < up_at))
        def _():
            part = lanes((k - down_at) % across)
            set_own(
                k, 3 + (k - down_at) // across, lambda micro, block: dims_dot(block, right[micro, :, part], 1, 0)
            )

        @pl.when((k >= up_at) & (k < qkv_at))
        def _():
            part = lanes(across + k - up_at)
            set_own(k, 1, lambda micro, block: dims_dot(block, right[micro, :, part], 1, 0))

        @pl.when(k >= qkv_at)
        def _():
            part = lanes(k - qkv_at)
            set_own(k, 2, lambda micro, block: dims_dot(block, heads[micro, part, :], 1, 1))

    def out_copy(k, kind):
        if kind == "down":
            target = down_o.at[(k - down_at) // across, :, :, :, lanes((k - down_at) % across)]
        else:
            ref, start = {"out": (out_o, out_at), "up": (up_o, up_at), "qkv": (qkv_o, qkv_at)}[kind]
            target = ref.at[:, :, :, lanes(k - start)]
        return pltpu.make_async_copy(final.at[k], target, out_sems.at[k])

    ranges = {"out": (out_at, down_at), "down": (down_at, up_at), "up": (up_at, qkv_at), "qkv": (qkv_at, pieces)}

    def stored(k, do):
        for kind, (first, end) in ranges.items():

            @pl.when((k >= first) & (k < end))
            def _():
                do(out_copy(k, kind))

    vector_peers = dp_peers + replica_peers

    def vector_copy(i):
        return pltpu.make_async_remote_copy(
            src_ref=vector_sum.at[i],
            dst_ref=from_vector.at[i],
            send_sem=vector_send.at[i],
            recv_sem=vector_recv.at[i],
            device_id=vector_peers[i][0],
            device_id_type=pl.DeviceIdType.MESH,
        )

    lags = [0]
    for stage in range(n_steps):
        lags.append(lags[-1] + 3)

    def turn(t, carry):
        for at, group in zip((down_at, up_at, qkv_at), copies[1:]):

            @pl.when(t == at)
            def _():
                for copy in group:
                    copy.wait()

        @pl.when(t < pieces)
        def _():
            compute(t)

        for stage in range(n_steps + 1):
            k = t - lags[stage]

            @pl.when((k >= 0) & (k < pieces))
            def _():
                advance_either(k, stage)
                if stage == n_steps:
                    stored(k, lambda copy: copy.start())

        for i in range(len(vector_peers) + 1):

            @pl.when(t == 4 * i)
            def _():
                if i > 0:
                    vector_copy(i - 1).wait()
                    vector_sum[i] = vector_sum[i - 1] + from_vector[i - 1]
                if i < len(vector_peers):
                    vector_copy(i).start()
                else:
                    pltpu.make_async_copy(vector_sum.at[i], vectors_o, out_sems.at[pieces]).start()

        return carry

    lax.fori_loop(0, pieces + lags[-1], turn, 0)

    def finish(k, carry):
        stored(k, lambda copy: copy.wait())
        return carry

    lax.fori_loop(0, pieces, finish, 0)
    pltpu.make_async_copy(vector_sum.at[len(vector_peers)], vectors_o, out_sems.at[pieces]).wait()


def reduce_call(stash, kept):
    _, _, attn_in, mlp_in, _, _, _, _, context, hidden, _ = stash
    _, grad_heads, grad_up, grad_out, vectors = kept
    micros, width, rows = attn_in.shape
    hidden_width = hidden.shape[1]
    groups = hidden_width // width
    devices = lax.axis_size("dp")
    bits = devices.bit_length() - 1
    share, quarter = width // devices, width // devices // 4
    piece = PIECE
    pieces = piece_plan(width, hidden_width, piece)[-1]
    loads = 6 + groups + 1
    tall = (micros, devices, share, rows)
    halves = [2] * bits
    steps = bits + 4
    peers = bits + 2
    shape = lambda columns: jax.ShapeDtypeStruct((2, 2, quarter, columns), BF16)
    outs = pl.pallas_call(
        functools.partial(reduce_kernel, bits, piece),
        out_shape=[
            shape(3 * width),
            shape(width),
            shape(hidden_width),
            jax.ShapeDtypeStruct((groups, 2, 2, quarter, width), BF16),
            jax.ShapeDtypeStruct(vectors.shape[1:], F32),
        ],
        in_specs=[ANY] * 8,
        out_specs=[ANY] * 5,
        scratch_shapes=[
            pltpu.VMEM((3 + groups, *tall), BF16),
            pltpu.VMEM((micros, rows, width + hidden_width), BF16),
            pltpu.VMEM(grad_heads.shape, BF16),
            pltpu.VMEM(vectors.shape, F32),
            pltpu.VMEM((pieces, *halves, 2, 2, quarter, piece), BF16),
            pltpu.VMEM((pieces, 2, 2, quarter, piece), BF16),
            pltpu.VMEM((pieces, *halves, 2, quarter, piece), BF16),
            *[pltpu.VMEM((pieces, *halves[bit + 1 :], 2, quarter, piece), BF16) for bit in range(bits)],
            pltpu.VMEM((pieces, quarter, piece), BF16),
            pltpu.VMEM((peers + 1, *vectors.shape[1:]), F32),
            pltpu.VMEM((peers, *vectors.shape[1:]), F32),
            pltpu.SemaphoreType.DMA((loads,)),
            pltpu.SemaphoreType.DMA((pieces, steps)),
            pltpu.SemaphoreType.DMA((pieces, steps)),
            pltpu.SemaphoreType.DMA((peers,)),
            pltpu.SemaphoreType.DMA((peers,)),
            pltpu.SemaphoreType.DMA((pieces + 1,)),
        ],
        compiler_params=pltpu.CompilerParams(
            collective_id=0, has_side_effects=True, vmem_limit_bytes=60 << 20
        ),
        cost_estimate=pl.CostEstimate(
            flops=2 * micros * rows * width * (4 * width + 2 * hidden_width),
            bytes_accessed=30 << 20,
            transcendentals=0,
        ),
        name="weight_gradients",
    )(
        context.reshape(tall),
        hidden.reshape(micros, devices, groups, share, rows),
        mlp_in.reshape(tall),
        attn_in.reshape(tall),
        grad_out,
        grad_up,
        grad_heads,
        vectors,
    )
    qkv, out, up, down, sums = outs
    scattered = [array.reshape(-1, array.shape[-1]) for array in (qkv, out, up, down)]
    return scattered, sums


def finish_kernel(grad_scale, *refs):
    vectors = refs[0]
    sources = refs[1:7]
    targets = refs[7:13]
    vector_outs = refs[13:21]
    held, wide = refs[21:27], refs[27:31]
    in_sems, out_sems = refs[31:]
    ready = (*held[:2], *wide)
    loads = [pltpu.make_async_copy(src, dst, in_sems.at[i]) for i, (src, dst) in enumerate(zip(sources, held))]
    stores = [pltpu.make_async_copy(src, dst, out_sems.at[i]) for i, (src, dst) in enumerate(zip(ready, targets))]
    order = (1, 0, 3, 2, 4, 5)
    for i in order:
        loads[i].start()
    devices = lax.axis_size("dp")
    mine = lax.axis_index("dp")
    width = vectors.shape[1]
    first_rows = (0, 1, 4, 7, 2, 3, 8, 7)
    for device in range(devices):

        @pl.when(mine == device)
        def _():
            for out, first in zip(vector_outs, first_rows):
                at, size, filled = device * out.shape[1], out.shape[1], 0
                while filled < size:
                    row, column = divmod(at + filled, width)
                    count = min(size - filled, width - column)
                    piece = vectors[first + row : first + row + 1, column : column + count]
                    out[:, filled : filled + count] = piece * grad_scale
                    filled += count

    for i in order:
        loads[i].wait()
        if i >= 2:
            wide[i - 2][...] = held[i][...].astype(F32) * grad_scale
        stores[i].start()
    for store in stores:
        store.wait()


def finish_call(grad_scale, shares, vectors, outputs, grad_in, hidden_width):
    width = vectors.shape[1]
    devices = lax.axis_size("dp")
    sizes = [width, width, 3 * width, width, width, width, hidden_width, width]
    matrices = [jax.ShapeDtypeStruct(share.shape, F32) for share in shares]
    results = pl.pallas_call(
        functools.partial(finish_kernel, grad_scale),
        out_shape=[
            jax.ShapeDtypeStruct(outputs.shape, BF16),
            jax.ShapeDtypeStruct(grad_in.shape, F32),
            *matrices,
            *[jax.ShapeDtypeStruct((1, size // devices), F32) for size in sizes],
        ],
        in_specs=[VMEM] + [ANY] * 6,
        out_specs=[ANY] * 6 + [VMEM] * 8,
        scratch_shapes=[pltpu.VMEM(array.shape, array.dtype) for array in (outputs, grad_in, *shares)]
        + [pltpu.VMEM(share.shape, F32) for share in shares]
        + [pltpu.SemaphoreType.DMA((6,)), pltpu.SemaphoreType.DMA((6,))],
        compiler_params=pltpu.CompilerParams(vmem_limit_bytes=60 << 20),
        name="finish",
    )(vectors, outputs, grad_in, *shares)
    return results[:2], results[2:6], results[6:]


def rotary_tables(seq_len):
    positions = np.arange(seq_len, dtype=np.float32)
    exponents = np.arange(0, ROTARY, 2, dtype=np.float32) / np.float32(ROTARY)
    inverse = np.float32(1.0) / np.float32(ROTARY_BASE) ** exponents
    angles = inverse[:, None] * positions[None, :]
    return jnp.asarray(np.cos(angles)), jnp.asarray(np.sin(angles))


def summed(share):
    part = lax.psum_scatter(share.astype(BF16), "dp", scatter_dimension=0, tiled=True)
    return lax.psum(part, "replica").astype(F32)


def in_pieces(width):
    devices = lax.axis_size("dp")
    return devices & (devices - 1) == 0 and lax.axis_size("replica") == 4 and width % (64 * devices) == 0


def local_totals(stash, kept):
    _, _, attn_in, mlp_in, _, _, _, _, context, hidden, _ = stash
    _, grad_heads, grad_up, grad_out, vectors = kept
    vector_sums = jnp.sum(vectors, axis=0)
    groups = hidden.shape[1] // attn_in.shape[1]
    return (
        vector_sums[0],
        vector_sums[1],
        jnp.einsum("mdr,mer->de", attn_in, grad_heads, preferred_element_type=F32),
        vector_sums[4:7].reshape(-1),
        jnp.einsum("mer,mrd->ed", context, grad_out, preferred_element_type=F32),
        vector_sums[7],
        vector_sums[2],
        vector_sums[3],
        jnp.einsum("mdr,mrf->df", mlp_in, grad_up, preferred_element_type=F32),
        vector_sums[8 : 8 + groups].reshape(-1),
        jnp.einsum("mfr,mrd->fd", hidden, grad_out, preferred_element_type=F32),
        vector_sums[7],
    )


def body(tokens, cotangent, lengths, *weights):
    weights = tuple(array if array.ndim == 2 else array[0] for array in weights)
    micros = lengths.shape[0]
    width = tokens.shape[1]
    rows = tokens.shape[0] // micros
    tables = rotary_tables(rows)
    stash = forward_call(lengths, tokens.reshape(micros, rows, width), weights, tables)
    kept = backward_call(lengths, cotangent.reshape(micros, rows, width), weights, tables, stash)
    grad_scale = float(tokens.shape[0] * lax.axis_size("dp") * lax.axis_size("replica")) ** (-0.5)
    if in_pieces(width):
        shares, vectors = reduce_call(stash, kept)
        (outputs, grad_in), matrices, parts = finish_call(
            grad_scale, shares, vectors, stash[0], kept[0], weights[8].shape[1]
        )
        qkv, out, up, down = (matrix[None] for matrix in matrices)
        gain, shift, qkv_bias, out_bias, mlp_gain, mlp_shift, up_bias, down_bias = parts
        grads = (gain, shift, qkv, qkv_bias, out, out_bias, mlp_gain, mlp_shift, up, up_bias, down, down_bias)
    else:
        outputs, grad_in = stash[0], kept[0]
        grads = tuple(summed(total)[None] * grad_scale for total in local_totals(stash, kept))
    return (outputs.reshape(1, micros * rows, width), grad_in.reshape(1, micros * rows, width), *grads)


def solution(mesh):
    rows = P(("dp", "replica"), None)
    vector, matrix = P("section", None), P("section", None, None)
    out_rows = P("section", ("dp", "replica"), None)
    vector_out, matrix_out = P("section", "dp"), P("section", "dp", None)
    return jax.shard_map(
        body,
        mesh=mesh,
        in_specs=(
            rows, rows, P(("dp", "replica")), vector, vector, matrix, vector, matrix, vector, vector, vector, matrix,
            vector, matrix, vector,
        ),
        out_specs=(
            out_rows, out_rows, vector_out, vector_out, matrix_out, vector_out, matrix_out, vector_out, vector_out,
            vector_out, matrix_out, vector_out, matrix_out, vector_out,
        ),
        check_vma=False,
    )
```
